256 devices in a mesh: exp: 64 (over y, z, core), pair: 4 (over x).
Axes of the slice: x: 4, y: 4, z: 8, core: 2. Of those that a mesh axis runs over, the one named last changes fastest.
Arguments:
- teacher_in: bfloat16 [16384, 7168], P('exp', 'pair'), may hold values from -6 to 6
- expert_ids: int32 [16384, 8], P('exp'), may hold values from 0 to 255, all different within a row; in each aligned block of 256 rows (0 to 255, 256 to 511, ...) at most 8 rows name the same one
- gate_codes: int32 [16384, 8], P('exp'), may hold values from 1 to 256
- w_gate: bfloat16 [7168, 32768], P('pair', 'exp'), may hold values from -0.0625 to 0.0625
- w_up: bfloat16 [7168, 32768], P('pair', 'exp'), may hold values from -0.0625 to 0.0625
- w_down: bfloat16 [32768, 7168], P('exp', 'pair'), may hold values from -0.125 to 0.125
- student_in: bfloat16 [16384, 2048], P('exp'), may hold values from -16 to 16
- projection: bfloat16 [2048, 7168], P('exp', 'pair'), may hold values from -0.125 to 0.125
Outputs:
- target: bfloat16 [16384, 7168], P('exp', 'pair')
- grad_projection: float32 [2048, 7168], P('exp', 'pair')
The draws below stay inside these ranges and needn't reach their ends.
Inputs may be any that keep to these rules, and one draw needn't show every extreme that they name: `expert_ids`: each row names 8 different experts. Within each aligned block of 256 rows no expert is named by more than 8 rows, and in every draw some expert is named by exactly 8 rows of some block.
All inputs are finite; a program needn't handle non-finite values.
Results may differ from the reference program's by a relative error of at most 0.0057.
Values may be sent and summed in bfloat16 or wider, within the bound.
A program may use at most 128 MiB of HBM per device.

```python
import math
import jax
import jax.numpy as jnp
import numpy as np
from jax import lax

DT = 7168
MOE_FF = 2048
EXPERTS = 256
TOP = 8
DS = 2048
TOK_DEV = 256
TOKENS = 16384
IN_FLIGHT = 16
CAP = 8
N_EXP = 64


def with_ends(result, own_key, least, high):
    spot = [jax.random.randint(jax.random.fold_in(own_key, axis), (), 0, length) for axis, length in enumerate(result.shape)]
    longest = result.shape.index(max(result.shape))
    neighbour = spot[:longest] + [(spot[longest] + 1) % result.shape[longest]] + spot[longest + 1:]
    return result.at[tuple(spot)].set(least).at[tuple(neighbour)].set(high)


def with_spikes(drawn, key, source, target, blocks, factor):
    owner, partner = [(jnp.arange(drawn.shape[position]) // (drawn.shape[position] // blocks)).reshape([-1 if axis == position else 1 for axis in range(drawn.ndim)]) for position in (source, target)]
    chosen = jax.random.permutation(key, blocks)[partner]
    strong = (owner == chosen) | (owner == (partner + blocks // 2) % blocks)
    return jnp.where(strong, factor * drawn, drawn)


def level_of(stream_key, extent, shards, least, top_value):
    loudness = 1.0
    for position, blocks in shards:
        heights = jax.random.uniform(jax.random.fold_in(jax.random.fold_in(stream_key, 6), position), (blocks,), jnp.float32, least / len(shards), top_value / len(shards))
        loudness = loudness * jnp.repeat(jnp.exp(heights), extent[position] // blocks).reshape((-1,) + (1,) * (len(extent) - 1 - position))
    return loudness


def deal_out(stream_key, own, number, rows, amount, top, most, slope):
    ranking = jax.random.permutation(stream_key, amount)
    crowded, ordinary = shares(amount, rows * top, most, slope, True), shares(amount, rows * top, most, slope, False)
    places = jnp.arange(amount)

    def named(tallies, turn):
        used = int((tallies > 0).sum())
        fixed = max(1, used // 4)
        passed = fixed + (places - fixed + turn * (used - fixed)) % max(1, amount - fixed)
        return jnp.zeros((amount,), jnp.int32).at[ranking[jnp.where(places < fixed, places, passed)]].set(jnp.asarray(tallies, jnp.int32))

    tallies = jnp.where(number % 4 == 0, named(crowded, number // 4), named(ordinary, number - number // 4 - 1))
    mixed = jax.random.permutation(jax.random.fold_in(own, 3), amount)
    donor, taker = mixed[0:amount // 2 * 2:2], mixed[1:amount // 2 * 2:2]
    slack = jnp.minimum(tallies[donor] - 1, most - tallies[taker]) // 2
    slack = jnp.where((donor == ranking[0]) | (taker == ranking[0]) | (tallies[taker] == 0), 0, jnp.maximum(slack, 0))
    passed = jax.random.randint(jax.random.fold_in(own, 4), (amount // 2,), 0, 1 << 20) % (slack + 1)
    tallies = tallies.at[donor].add(-passed).at[taker].add(passed)
    items = jnp.searchsorted(jnp.cumsum(tallies), jnp.arange(rows * top), side="right").astype(jnp.int32)
    table = items.reshape(top, rows).T
    table = table[jax.random.permutation(jax.random.fold_in(own, 1), rows)]
    turn = jax.random.randint(jax.random.fold_in(own, 2), (rows, 1), 0, top)
    return jnp.take_along_axis(table, (jnp.arange(top)[None, :] + turn) % top, axis=1)


def shares(number_of, total, bound, skew, full):
    weights = [(1 << 20) // math.isqrt(standing ** skew) + 1 for standing in range(1, number_of + 1)]
    largest = bound if full else min(bound, max(-(-total // number_of), total * weights[0] // sum(weights)))
    least = 1 if total - largest >= number_of - 1 else 0
    given, surplus = [largest] + [least] * (number_of - 1), total - largest - least * (number_of - 1)
    while surplus > 0:
        candidates = [i for i in range(1, number_of) if given[i] < largest] or [i for i in range(1, number_of) if given[i] < bound]
        pool, budget = sum([weights[i] for i in candidates]), surplus
        for i in candidates:
            extra = min(bound - given[i], max(1, budget * weights[i] // pool), surplus)
            given[i] = given[i] + extra
            surplus = surplus - extra
    return np.array(given)


def scatter_about(own_key, shape, scale, bound, pieces=(), kind=jnp.bfloat16):
    entries = jax.random.normal(own_key, shape, jnp.float32) * scale
    if len(pieces) > 0:
        entries = level_of(own_key, shape, pieces, -0.22, 0.18) * entries
    return jnp.clip(entries, min=-bound, max=bound).astype(kind)


def gaussian_with(stream_key, extent, width, bound, split, heavy, kind=jnp.bfloat16):
    values = width * jax.random.normal(stream_key, extent, jnp.float32)
    if split:
        values = values * level_of(stream_key, extent, split, -0.22, 0.18)
    return jnp.clip(with_spikes(values, jax.random.fold_in(stream_key, 3), *heavy), -bound, bound).astype(kind)


def setup_inputs(seed: int = 0) -> dict:
    arg_keys = jax.random.split(jax.random.key(seed), 9)
    teacher_in = scatter_about(arg_keys[0], (TOKENS, DT), 1.0, 6.0, ((0, 64), (1, 4)))
    expert_ids_keys = jax.random.split(jax.random.fold_in(arg_keys[1], 1), TOKENS // TOK_DEV)
    expert_ids_turns = jax.random.permutation(jax.random.fold_in(arg_keys[1], 3), TOKENS // TOK_DEV)
    expert_ids = jax.vmap(lambda own, number: deal_out(jax.random.fold_in(arg_keys[1], 2), own, number, TOK_DEV, EXPERTS, TOP, CAP, 2))(expert_ids_keys, expert_ids_turns).reshape((TOKENS, TOP))
    gate_codes = with_ends(jax.random.randint(arg_keys[2], (TOKENS, TOP), 1, 257), jax.random.fold_in(arg_keys[2], 1), 1, 256).astype(jnp.int32)
    w_gate = scatter_about(arg_keys[3], (DT, IN_FLIGHT * MOE_FF), DT ** -0.5, 0.0625, ((0, 4), (1, 64)))
    w_up = scatter_about(arg_keys[4], (DT, IN_FLIGHT * MOE_FF), DT ** -0.5, 0.0625, ((0, 4), (1, 64)))
    w_down = scatter_about(arg_keys[5], (IN_FLIGHT * MOE_FF, DT), MOE_FF ** -0.5, 0.125, ((0, 64), (1, 4)))
    student_in = gaussian_with(arg_keys[6], (TOKENS, DS), 1.0, 16.0, ((0, 64),), (0, 1, 64, 4.0))
    projection = scatter_about(arg_keys[7], (DS, DT), DS ** -0.5, 0.125, ((0, 64), (1, 4)))
    return dict(teacher_in=teacher_in, expert_ids=expert_ids, gate_codes=gate_codes, w_gate=w_gate, w_up=w_up, w_down=w_down, student_in=student_in, projection=projection)


loss_scale = 128.0
norm_epsilon = 1e-06

def reference(teacher_in, expert_ids, gate_codes, w_gate, w_up, w_down, student_in, projection):
    in_flight = N_EXP // 4
    quarter = MOE_FF // 4
    limit = N_EXP * CAP
    codes = gate_codes.astype(jnp.float32) / 256.0
    summed = jnp.zeros((TOKENS, DT), jnp.float32)
    for expert in range(in_flight):
        hits = expert_ids == expert
        weight_tok = lax.optimization_barrier(jnp.sum(jnp.where(hits, codes, 0.0), axis=1))
        chosen = jnp.any(hits, axis=1)
        count = jnp.sum(chosen.astype(jnp.int32))
        index = jnp.nonzero(chosen, size=limit, fill_value=0)[0].astype(jnp.int32)
        valid = jnp.arange(limit, dtype=jnp.int32) < count
        weight_row = jnp.where(valid, weight_tok[index], 0.0)
        rows = teacher_in[index]
        lo = expert * MOE_FF
        gate_pre = jnp.dot(rows, w_gate[:, lo:lo + MOE_FF], preferred_element_type=jnp.float32)
        up_pre = jnp.dot(rows, w_up[:, lo:lo + MOE_FF], preferred_element_type=jnp.float32)
        active = (jax.nn.silu(gate_pre) * up_pre).astype(jnp.bfloat16)
        output = jnp.zeros((limit, DT), jnp.float32)
        for part in range(4):
            block = jnp.dot(active[:, part * quarter:(part + 1) * quarter], w_down[lo + part * quarter:lo + (part + 1) * quarter, :], preferred_element_type=jnp.float32)
            output = output + block.astype(jnp.bfloat16).astype(jnp.float32)
        summed = summed.at[index].add(weight_row[:, None] * output)
    target = summed.astype(jnp.bfloat16)
    wide = student_in.astype(jnp.float32)
    scale = lax_rsqrt(lax.optimization_barrier(jnp.mean(wide * wide, axis=1, keepdims=True)) + norm_epsilon)
    normed = (wide * scale).astype(jnp.bfloat16)
    student_out = jnp.dot(normed, projection, preferred_element_type=jnp.float32)
    resid = ((student_out - target.astype(jnp.float32)) * (loss_scale / TOKENS)).astype(jnp.bfloat16)
    grad_projection = jnp.dot(normed.T, resid, preferred_element_type=jnp.float32)
    return (target, grad_projection)

def lax_rsqrt(value):
    return 1.0 / jnp.sqrt(value)
```

```python
import jax
import jax.numpy as jnp
from jax import lax
from jax.experimental import pallas as pl
from jax.experimental.pallas import tpu as pltpu
from jax.sharding import PartitionSpec as P

CAP = 8
MESH = pl.DeviceIdType.MESH
BF = jnp.bfloat16
F32 = jnp.float32

loss_scale = 128.0
norm_epsilon = 1e-06

W = 1792
H = 512


def dot_t(a, b):
    return lax.dot_general(a, b, (((0,), (0,)), ((), ())), preferred_element_type=F32)


def dot(a, b):
    return jnp.dot(a, b, preferred_element_type=F32)


def tiles(count, size, f, first=0):
    def step(i, carry):
        f(pl.ds(pl.multiple_of(first + i * size, 128), size))
        return carry

    lax.fori_loop(0, count, step, 0)


def kernel(
    teacher, ids, codes, student_in, proj, wg_hbm, wu_hbm, wd_hbm,
    target, grad,
    wgu, wd, weigh, packed, normed, left_x, wn, gx, rows, xk, gu, xr, act, prodf, ps, pr, vs, vr, ob, ret, tb, tg,
    wnb, pb, gxr, gs1, gr1, gs2, gr2, gt, gtt, wk, m, ms, mr, zs, zr,
    send_sem, recv_sem, local_sem,
):
    e = lax.axis_index("exp")
    x = lax.axis_index("pair")
    y, z, c = e // 16, (e // 2) % 8, e % 2
    sg = 1 - 2 * (z % 2)

    def at(dy=0, dz=0, other=False):
        yy, zz = (y + dy + 4) % 4, (z + dz + 8) % 8
        return (yy * 16 + zz * 2 + (1 - c if other else c), x)

    def at_x(dx):
        return (e, (x + dx) % 4)

    number = [0, 0]
    started = []

    def new_recv():
        number[1] += 1
        return number[1] - 1

    def copy_to(src, dst, device, recv=None):
        i = number[0]
        number[0] += 1
        copy = pltpu.make_async_remote_copy(
            src_ref=src, dst_ref=dst, send_sem=send_sem.at[i],
            recv_sem=recv_sem.at[new_recv() if recv is None else recv],
            device_id=device, device_id_type=MESH,
        )
        copy.start()
        started.append(copy)
        return copy

    def arrival(dst, recv):
        return pltpu.make_async_remote_copy(
            src_ref=dst, dst_ref=dst, send_sem=send_sem.at[0], recv_sem=recv_sem.at[recv],
            device_id=at(other=True), device_id_type=MESH,
        )

    weights = [
        pltpu.make_async_copy(wg_hbm, wgu.at[0], local_sem.at[0]),
        pltpu.make_async_copy(wu_hbm, wgu.at[1], local_sem.at[1]),
        pltpu.make_async_copy(wd_hbm, wd, local_sem.at[2]),
    ]

    barrier = pltpu.get_barrier_semaphore()
    peers = [at(dy=dy, dz=dz) for dy in range(4) for dz in (0, 1, -1, 2, -2, 3, -3) if dy or dz]
    peers += [at(dz=4), at(other=True)] + [at_x(d) for d in (1, 2, 3)]
    for peer in peers:
        pl.semaphore_signal(barrier, inc=1, device_id=peer, device_id_type=MESH)

    place = lax.broadcasted_iota(jnp.int32, (128, 256), 0)
    hop = (place >> 3) & 3
    shift = jnp.where(hop == 0, 0, jnp.where(hop == 1, -sg, jnp.where(hop == 2, sg, 2)))
    expert = ((y + 4 - (place >> 5)) & 3) * 4 + ((z // 2 + 4 + shift) & 3)
    hit = jnp.zeros((128, 256), F32)
    code = jnp.zeros((128, 256), jnp.int32)
    for k in range(8):
        same = ids[k:k + 1, :] == expert
        hit = jnp.where(same, 1.0, hit)
        code = jnp.where(same, codes[k:k + 1, :], code)
    ahead = lax.broadcasted_iota(jnp.int32, (256, 256), 0) < lax.broadcasted_iota(jnp.int32, (256, 256), 1)
    rank = dot(hit.astype(BF), jnp.where(ahead, 1.0, 0.0).astype(BF))
    chosen = jnp.where(rank == (place & 7).astype(F32), hit, 0.0)
    weigh[...] = (chosen * code.astype(F32) * (1.0 / 256.0)).astype(BF)
    chosen = chosen.astype(BF)

    def pack(cols):
        low = dot(chosen, teacher[:, cols]).reshape(16, 8, 128)
        high = dot(chosen, teacher[:, pl.ds(pl.multiple_of(896 + cols.start, 128), 128)]).reshape(16, 8, 128)
        packed[:, :, cols] = jnp.concatenate([low, high], axis=1).astype(BF)

    tiles(7, 128, pack)
    pl.semaphore_wait(barrier, len(peers))

    out_hop = (0, -1, 2, -3)
    direct, via, over, over_via = {}, {}, {}, {}
    direct[0], via[0] = new_recv(), new_recv()
    for d in (1, 3, 2):
        copy_to(packed.at[d * 4], rows.at[0, 0, 0, d], at(dy=-d), direct[0])
    for d in (0, 1, 3, 2):
        copy_to(packed.at[d * 4], rows.at[1, 0, 0, d], at(dy=-d, dz=sg), via[0])
    for j in (1, 2, 3):
        direct[j] = new_recv()
        for d in (0, 1, 3, 2):
            copy_to(packed.at[d * 4 + j], rows.at[0, j, 0, d], at(dy=-d, dz=out_hop[j] * sg), direct[j])
    rows[0, 0, 0, 0] = packed[0]
    for copy in weights:
        copy.start()

    wide = student_in[...].astype(F32)
    scale = 1.0 / jnp.sqrt(jnp.mean(wide * wide, axis=1, keepdims=True) + norm_epsilon)
    normed[...] = (wide * scale).astype(BF)
    left_x[...] = normed[:, pl.ds(pl.multiple_of(x * 512, 512), 512)].astype(F32).T.astype(BF)

    def early(cols):
        gx[:, :, :, cols] = dot(left_x[...], normed[:, cols]).reshape(8, 2, 32, 256).astype(BF)

    def early_rows(cols):
        out = dot(weigh[...], normed[:, cols]).reshape(4, 4, 8, 256)
        for j in range(4):
            wn[j, :, cols] = jnp.concatenate([out[d, j] for d in range(4)], axis=0).astype(BF)

    gram = {}

    def gram_start():
        tiles(8, 256, early)
        gram["core"] = copy_to(gx.at[:, 1 - c], gxr, at(other=True))

    def gram_0():
        gram["core"].wait_recv()
        for q in range(4):
            cols = slice(q * 512, q * 512 + 512)
            gs1[q] = (gx[:, c, :, cols].astype(F32) + gxr[:, :, cols].astype(F32)).astype(BF)
        gram["y"] = [copy_to(gs1.at[(y + d) % 4], gr1.at[d], at(dy=d)) for d in (1, 3, 2)]

    def gram_1():
        for copy in gram["y"]:
            copy.wait_recv()
        total = gs1[y].astype(F32) + sum(gr1[d].astype(F32) for d in (1, 2, 3))
        gs2[...] = total.astype(BF)
        gram["z"] = [copy_to(gs2.at[(z + d) % 8], gr2.at[d], at(dz=d)) for d in (1, 7, 2, 6, 3, 5, 4)]

    def gram_2():
        for copy in gram["z"]:
            copy.wait_recv()
        total = gs2[z].astype(F32) + sum(gr2[d].astype(F32) for d in range(1, 8))
        gt[x] = total.astype(BF)
        gram["x"] = [copy_to(gt.at[x], gt.at[x], at_x(d)) for d in (1, 3, 2)]

    early_y, early_wn = [], []

    def send_early():
        tiles(8, 256, early_rows)
        early_y.extend([copy_to(proj, pb.at[y], at(dy=d)) for d in (1, 3, 2)])
        pb[y] = proj[...]
        for j in range(4):
            early_wn.append(new_recv())
            for d in (0, 1, 3, 2):
                cols = pl.ds(pl.multiple_of(((y + 4 - d) % 4) * 512, 512), 512)
                if j == 0 and d == 0:
                    wnb[0, 0] = wn[0, :, cols]
                else:
                    copy_to(wn.at[j, :, cols], wnb.at[j, d], at(dy=-d, dz=out_hop[j] * sg), early_wn[j])

    def student():
        for copy in early_y + gram["x"]:
            copy.wait_recv()
        gtt[...] = gt[...].reshape(128, 512).astype(F32).T.astype(BF)

        def step(cols):
            m[:, :, :, cols] = dot(gtt[...], pb[:, :, cols].reshape(128, 256)).reshape(8, 2, 32, 256)

        tiles(7, 256, step)
        for j in range(4):
            into = wnb.at[j, pl.ds(1, 3)] if j == 0 else wnb.at[j]
            arrival(into, early_wn[j]).wait_recv()
            blocks = [wnb[j, d].astype(F32) for d in range(4)]
            order = [blocks[(d + 4 - g) % 4][d * 8:d * 8 + 8] for g in range(4) for d in range(4)]
            wk[j] = jnp.concatenate(order, axis=0).T.astype(BF)

    to_x, act_x, back_core, back_pair, back_z, round_y, far_y = {}, {}, {}, {}, {}, {}, {}

    def arrive(j):
        into = rows.at[0, 0, 0, pl.ds(1, 3)] if j == 0 else rows.at[0, j, 0]
        arrival(into, direct[j]).wait_recv()
        over[j] = copy_to(rows.at[0, j, 0], rows.at[0, j, 1], at(other=True))
        if j:
            via[j] = new_recv()
            copy_to(rows.at[0, j, 0], rows.at[1, j, 0], at(dz=sg), via[j])

    def arrive_via(j):
        arrival(rows.at[1, j, 0], via[j]).wait_recv()
        over_via[j] = copy_to(rows.at[1, j, 0], rows.at[1, j, 1], at(other=True))

    def gate_up(j):
        over[j].wait_recv()
        over_via[j].wait_recv()

        def unfold(cols):
            block = rows[:, j, :, :, :, cols].astype(F32).reshape(16, 2, 8, 128)
            xk[:, cols] = block[:, 0].reshape(128, 128).astype(BF)
            xk[:, pl.ds(pl.multiple_of(896 + cols.start, 128), 128)] = block[:, 1].reshape(128, 128).astype(BF)

        tiles(7, 128, unfold)
        if j == 0:
            weights[0].wait()
            weights[1].wait()
        for part in range(2):
            def step(cols):
                out = dot(xk[...], wgu[part, :, cols])
                gu[j, part, :, :, cols] = out.reshape(4, 32, 256).astype(BF)

            tiles(2, 256, step)
        to_x[j] = [copy_to(gu.at[j, :, (x + d) % 4], xr.at[j, d], at_x(d)) for d in (1, 3, 2)]

    def activate(j):
        for copy in to_x[j]:
            copy.wait_recv()
        gate, up = [
            gu[j, part, x].astype(F32) + sum(xr[j, d, part].astype(F32) for d in (1, 2, 3)) for part in range(2)
        ]
        act[j, x] = (gate / (1.0 + jnp.exp(-gate)) * up).astype(BF)
        act_x[j] = [copy_to(act.at[j, x], act.at[j, x], at_x(d)) for d in (1, 3, 2)]

    def down(j):
        for copy in act_x[j]:
            copy.wait_recv()
        if j == 0:
            weights[2].wait()

        def step(cols):
            out = dot(act[j].reshape(128, H), wd[:, cols]).reshape(4, 32, 256)
            for i in range(2):
                prodf[j, i, :, cols] = out[2 * i]
                ps[j, i, :, cols] = out[2 * i + 1].astype(BF)

        tiles(7, 256, step)
        back_core[j] = copy_to(ps.at[j], pr.at[j], at(other=True))

    def core_sum(j):
        back_core[j].wait_recv()

        def step(cols):
            vs[j, :, cols] = (prodf[j, 1, :, cols] + pr[j, 1, :, cols].astype(F32)).astype(BF)

        tiles(7, 256, step)
        back_pair[j] = copy_to(vs.at[j], vr.at[j], at(dz=sg))

    def pair_sum(j):
        back_pair[j].wait_recv()

        def step(cols):
            ob[j, 0, :, cols] = (
                prodf[j, 0, :, cols] + pr[j, 0, :, cols].astype(F32) + vr[j, :, cols].astype(F32)
            ).astype(BF)

        tiles(7, 256, step)
        round_y[j] = [copy_to(ob.at[j, 0], ob.at[j, g], at(dy=g)) for g in (1, 3)]
        if j:
            back_z[j] = copy_to(ob.at[j, 0], ret.at[j], at(dz=-j * sg))

    def relay(j):
        low, high = pl.ds(0, 16), pl.ds(16, 16)
        round_y[j][0].wait_recv()
        far_y[j] = [copy_to(ob.at[j, 1, low], ob.at[j, 2, low], at(dy=1))]
        round_y[j][1].wait_recv()
        far_y[j].append(copy_to(ob.at[j, 3, high], ob.at[j, 2, high], at(dy=-1)))

    def teacher_part(j):
        for copy in far_y[j]:
            copy.wait_recv()

        def step(cols):
            part = dot(wk[j], ob[j, :, :, cols].reshape(128, 256))
            m[:, :, :, cols] -= part.reshape(8, 2, 32, 256)

        tiles(7, 256, step)

    stages = (arrive, arrive_via, gate_up, activate, down, core_sum, pair_sum, relay)
    after = {0: gram_start, 1: send_early, 2: gram_0, 4: gram_1, 5: gram_2, 7: student}
    for t in range(len(stages) + 3):
        for j in range(4):
            if 0 <= t - j < len(stages):
                stages[t - j](j)
        if t in after:
            after[t]()
        if t >= 8:
            teacher_part(t - 8)

    parts = ((0, 4), (1024, 3))
    over_m = []
    for copy in far_y[3]:
        copy.wait_recv()

    def finish(cols):
        part = dot(wk[3], ob[3, :, :, cols].reshape(128, 256))
        m[:, :, :, cols] -= part.reshape(8, 2, 32, 256)
        ms[:, :, cols] = m[:, 1 - c, :, cols].astype(BF)

    for first, count in parts:
        tiles(count, 256, finish, first)
        span = pl.ds(first, count * 256)
        over_m.append(copy_to(ms.at[:, :, span], mr.at[:, :, span], at(other=True)))

    for j in (1, 2, 3):
        back_z[j].wait_recv()

    def sort_rows(cols):
        blocks = [ob[0, 0, :, cols].astype(F32)] + [ret[j, :, cols].astype(F32) for j in (1, 2, 3)]
        for d in range(4):
            tb[d, :, cols] = jnp.concatenate([b[d * 8:d * 8 + 8] for b in blocks], axis=0).astype(BF)

    tiles(7, 256, sort_rows)
    to_owner = [copy_to(tb.at[d], tg.at[d], at(dy=d)) for d in (1, 3, 2)]
    tg[0] = tb[0]

    def mine(d, first, count, cols):
        zz = (z + 8 + d) % 8
        span = slice(first, first + count)
        return m[zz, c, span, cols] + mr[zz, span, cols].astype(F32)

    hops = {}
    for step in range(4):
        for half, (start, count) in enumerate(parts):
            cols = pl.ds(start, count * 256)
            if step == 0:
                over_m[half].wait_recv()
            for way, sign in ((0, -1), (1, 1)):
                slot = step * 2 + way
                far = sign * (4 - step)
                if step == 0:
                    zs[slot, 0:16, cols] = mine(far, 16 * way, 16, cols).astype(BF)
                    src, dst = zs.at[slot, pl.ds(0, 16), cols], zr.at[slot, pl.ds(0, 16), cols]
                else:
                    hops[step - 1, half, way].wait_recv()
                    if step == 1:
                        first = 16 * way
                        total = mine(far, first, 16, cols) + zr[slot - 2, 0:16, cols].astype(F32)
                        zs[slot, first:first + 16, cols] = total.astype(BF)
                        zs[slot, 16 - first:32 - first, cols] = mine(far, 16 - first, 16, cols).astype(BF)
                    else:
                        zs[slot, :, cols] = (mine(far, 0, 32, cols) + zr[slot - 2, :, cols].astype(F32)).astype(BF)
                    src, dst = zs.at[slot, :, cols], zr.at[slot, :, cols]
                hops[step, half, way] = copy_to(src, dst, at(dz=sign))
        if step == 1:
            for copy in to_owner:
                copy.wait_recv()

            def write_target(cols):
                target[:, cols] = dot_t(weigh[...], tg[:, :, cols].reshape(128, 256)).astype(BF)

            tiles(7, 256, write_target)
    for half, (start, count) in enumerate(parts):
        cols = pl.ds(start, count * 256)
        total = mine(0, 0, 32, cols)
        for way in range(2):
            hops[3, half, way].wait_recv()
            total += zr[6 + way, :, cols].astype(F32)
        grad[:, cols] = total * (loss_scale / 16384)
    for copy in started:
        copy.wait_send()


N_COPIES = 19 + 3 + 8 + 12 + 12 + 4 + 4 + 3 + 16 + 3 + 15 + 14 + 3 + 2 + 16


def body(teacher_in, expert_ids, gate_codes, w_gate, w_up, w_down, student_in, projection):
    vmem = pl.BlockSpec(memory_space=pltpu.VMEM)
    hbm = pl.BlockSpec(memory_space=pl.ANY)
    return pl.pallas_call(
        kernel,
        out_shape=(
            jax.ShapeDtypeStruct((256, W), BF),
            jax.ShapeDtypeStruct((32, W), F32),
        ),
        in_specs=[vmem] * 5 + [hbm] * 3,
        out_specs=(vmem, vmem),
        scratch_shapes=[
            pltpu.VMEM((2, W, H), BF),
            pltpu.VMEM((H, W), BF),
            pltpu.VMEM((128, 256), BF),
            pltpu.VMEM((16, 16, W // 2), BF),
            pltpu.VMEM((256, 2048), BF),
            pltpu.VMEM((512, 256), BF),
            pltpu.VMEM((4, 32, 2048), BF),
            pltpu.VMEM((8, 2, 32, 2048), BF),
            pltpu.VMEM((2, 4, 2, 4, 16, W // 2), BF),
            pltpu.VMEM((128, W), BF),
            pltpu.VMEM((4, 2, 4, 32, H), BF),
            pltpu.VMEM((4, 4, 2, 32, H), BF),
            pltpu.VMEM((4, 4, 32, H), BF),
            pltpu.VMEM((4, 2, 32, W), F32),
            pltpu.VMEM((4, 2, 32, W), BF),
            pltpu.VMEM((4, 2, 32, W), BF),
            pltpu.VMEM((4, 32, W), BF),
            pltpu.VMEM((4, 32, W), BF),
            pltpu.VMEM((4, 4, 32, W), BF),
            pltpu.VMEM((4, 32, W), BF),
            pltpu.VMEM((4, 32, W), BF),
            pltpu.VMEM((4, 32, W), BF),
            pltpu.VMEM((4, 4, 32, 512), BF),
            pltpu.VMEM((4, 32, W), BF),
            pltpu.VMEM((8, 32, 2048), BF),
            pltpu.VMEM((4, 8, 32, 512), BF),
            pltpu.VMEM((4, 8, 32, 512), BF),
            pltpu.VMEM((8, 32, 512), BF),
            pltpu.VMEM((8, 32, 512), BF),
            pltpu.VMEM((4, 32, 512), BF),
            pltpu.VMEM((512, 128), BF),
            pltpu.VMEM((4, 512, 128), BF),
            pltpu.VMEM((8, 2, 32, W), F32),
            pltpu.VMEM((8, 32, W), BF),
            pltpu.VMEM((8, 32, W), BF),
            pltpu.VMEM((8, 32, W), BF),
            pltpu.VMEM((8, 32, W), BF),
            pltpu.SemaphoreType.DMA((N_COPIES,)),
            pltpu.SemaphoreType.DMA((N_COPIES,)),
            pltpu.SemaphoreType.DMA((3,)),
        ],
        compiler_params=pltpu.CompilerParams(
            collective_id=0, has_side_effects=True, vmem_limit_bytes=52 * 1024 * 1024
        ),
        cost_estimate=pl.CostEstimate(flops=8_000_000_000, bytes_accessed=12_000_000, transcendentals=0),
    )(teacher_in, expert_ids.T, gate_codes.T, student_in, projection, w_gate, w_up, w_down)


def solution(mesh):
    in_specs = (
        P("exp", "pair"),
        P("exp", None),
        P("exp", None),
        P("pair", "exp"),
        P("pair", "exp"),
        P("exp", "pair"),
        P("exp", None),
        P("exp", "pair"),
    )
    out_specs = (P("exp", "pair"), P("exp", "pair"))
    return jax.shard_map(body, mesh=mesh, in_specs=in_specs, out_specs=out_specs, check_vma=False)
```

```python
import jax
import jax.numpy as jnp
from jax import lax
from jax.experimental import pallas as pl
from jax.experimental.pallas import tpu as pltpu
from jax.sharding import PartitionSpec as P

CAP = 8
MESH = pl.DeviceIdType.MESH
BF = jnp.bfloat16
F32 = jnp.float32

loss_scale = 128.0
norm_epsilon = 1e-06

W = 1792
H = 512


def dot_t(a, b):
    return lax.dot_general(a, b, (((0,), (0,)), ((), ())), preferred_element_type=F32)


def dot(a, b):
    return jnp.dot(a, b, preferred_element_type=F32)


def tiles(count, size, f, first=0):
    def step(i, carry):
        f(pl.ds(pl.multiple_of(first + i * size, 128), size))
        return carry

    lax.fori_loop(0, count, step, 0)


def kernel(
    ids_hbm, codes_hbm, proj_hbm, teacher_hbm, student_hbm, wg_hbm, wu_hbm, wd_hbm,
    target_hbm, grad_hbm, target, grad, tg, ids, codes, proj, teacher, student_in,
    wgu, wd, weigh, packed, normed, left_x, wn, gx, rows, xk, gu, xr, act, prodf, ps, pr, vs, vr, ob, ret, tb,
    wnb, pb, gxr, gs1, gr1, gs2, gr2, gt, gtt, gtf, wkt, wk, m, zs, zr,
    send_sem, recv_sem, local_sem,
):
    e = lax.axis_index("exp")
    x = lax.axis_index("pair")
    y, z, c = e // 16, (e // 2) % 8, e % 2
    sg = 1 - 2 * (z % 2)

    def at(dy=0, dz=0, other=False):
        yy, zz = (y + dy + 4) % 4, (z + dz + 8) % 8
        return (yy * 16 + zz * 2 + (1 - c if other else c), x)

    def at_x(dx):
        return (e, (x + dx) % 4)

    number = [0, 0]
    started = []

    def new_recv():
        number[1] += 1
        return number[1] - 1

    def copy_to(src, dst, device, recv=None):
        i = number[0]
        number[0] += 1
        copy = pltpu.make_async_remote_copy(
            src_ref=src, dst_ref=dst, send_sem=send_sem.at[i],
            recv_sem=recv_sem.at[new_recv() if recv is None else recv],
            device_id=device, device_id_type=MESH,
        )
        copy.start()
        started.append(copy)
        return copy

    def arrival(dst, recv):
        return pltpu.make_async_remote_copy(
            src_ref=dst, dst_ref=dst, send_sem=send_sem.at[0], recv_sem=recv_sem.at[recv],
            device_id=at(other=True), device_id_type=MESH,
        )

    weights = [
        pltpu.make_async_copy(wg_hbm, wgu.at[0], local_sem.at[0]),
        pltpu.make_async_copy(wu_hbm, wgu.at[1], local_sem.at[1]),
        pltpu.make_async_copy(wd_hbm, wd, local_sem.at[2]),
    ]
    operands = [
        pltpu.make_async_copy(src, dst, local_sem.at[3 + i])
        for i, (src, dst) in enumerate((
            (ids_hbm, ids), (codes_hbm, codes), (teacher_hbm, teacher), (student_hbm, student_in), (proj_hbm, proj),
        ))
    ]
    for copy in operands:
        copy.start()

    barrier = pltpu.get_barrier_semaphore()
    peers = [at(dy=dy, dz=dz) for dy in range(4) for dz in (0, 1, -1, 2, -2, 3, -3) if dy or dz]
    peers += [at(dz=4), at(other=True)] + [at_x(d) for d in (1, 2, 3)]
    for peer in peers:
        pl.semaphore_signal(barrier, inc=1, device_id=peer, device_id_type=MESH)

    operands[0].wait()
    operands[1].wait()
    place = lax.broadcasted_iota(jnp.int32, (128, 256), 0)
    hop = (place >> 3) & 3
    shift = jnp.where(hop == 0, 0, jnp.where(hop == 1, -sg, jnp.where(hop == 2, sg, 2)))
    expert = ((y + 4 - (place >> 5)) & 3) * 4 + ((z // 2 + 4 + shift) & 3)
    hit = jnp.zeros((128, 256), F32)
    code = jnp.zeros((128, 256), jnp.int32)
    for k in range(8):
        same = ids[k:k + 1, :] == expert
        hit = jnp.where(same, 1.0, hit)
        code = jnp.where(same, codes[k:k + 1, :], code)
    ahead = lax.broadcasted_iota(jnp.int32, (256, 256), 0) < lax.broadcasted_iota(jnp.int32, (256, 256), 1)
    rank = dot(hit.astype(BF), jnp.where(ahead, 1.0, 0.0).astype(BF))
    chosen = jnp.where(rank == (place & 7).astype(F32), hit, 0.0)
    weigh[...] = (chosen * code.astype(F32) * (1.0 / 256.0)).astype(BF)
    chosen = chosen.astype(BF)

    def pack(cols):
        low = dot(chosen, teacher[:, cols]).reshape(16, 8, 128)
        high = dot(chosen, teacher[:, pl.ds(pl.multiple_of(896 + cols.start, 128), 128)]).reshape(16, 8, 128)
        packed[:, :, cols] = jnp.concatenate([low, high], axis=1).astype(BF)

    operands[2].wait()
    tiles(7, 128, pack)
    pl.semaphore_wait(barrier, len(peers))

    out_hop = (0, -1, 2, -3)
    direct, via, over, over_via = {}, {}, {}, {}
    for j in range(4):
        direct[j] = new_recv()
        for d in (1, 3, 2, 0):
            if j or d:
                copy_to(packed.at[d * 4 + j], rows.at[0, j, 0, d], at(dy=-d, dz=out_hop[j] * sg), direct[j])
        if j == 0:
            via[0] = new_recv()
            for d in (0, 1, 3, 2):
                copy_to(packed.at[d * 4], rows.at[1, 0, 0, d], at(dy=-d, dz=sg), via[0])
    rows[0, 0, 0, 0] = packed[0]
    for copy in weights:
        copy.start()

    operands[3].wait()
    wide = student_in[...].astype(F32)
    scale = 1.0 / jnp.sqrt(jnp.mean(wide * wide, axis=1, keepdims=True) + norm_epsilon)
    normed[...] = (wide * scale).astype(BF)
    left_x[...] = normed[:, pl.ds(pl.multiple_of(x * 512, 512), 512)].astype(F32).T.astype(BF)

    def early(cols):
        gx[:, :, :, cols] = dot(left_x[...], normed[:, cols]).reshape(8, 2, 32, 256).astype(BF)

    def early_rows(cols):
        out = dot(weigh[...], normed[:, cols]).reshape(4, 4, 8, 256)
        for j in range(4):
            wn[j, :, cols] = jnp.concatenate([out[d, j] for d in range(4)], axis=0).astype(BF)

    gram = {}

    def gram_start():
        tiles(8, 256, early)
        gram["core"] = copy_to(gx.at[:, 1 - c], gxr, at(other=True))

    def gram_0():
        gram["core"].wait_recv()
        for q in range(4):
            cols = slice(q * 512, q * 512 + 512)
            gs1[q] = (gx[:, c, :, cols].astype(F32) + gxr[:, :, cols].astype(F32)).astype(BF)
        gram["y"] = [copy_to(gs1.at[(y + d) % 4], gr1.at[d], at(dy=d)) for d in (1, 3, 2)]

    def gram_1():
        for copy in gram["y"]:
            copy.wait_recv()
        total = gs1[y].astype(F32) + sum(gr1[d].astype(F32) for d in (1, 2, 3))
        gs2[...] = total.astype(BF)
        gram["z"] = [copy_to(gs2.at[(z + d) % 8], gr2.at[d], at(dz=d)) for d in (1, 7, 2, 6, 3, 5, 4)]

    def gram_2():
        for copy in gram["z"]:
            copy.wait_recv()
        total = gs2[z].astype(F32) + sum(gr2[d].astype(F32) for d in range(1, 8))
        gt[x] = total.astype(BF)
        gram["x"] = [copy_to(gt.at[x], gt.at[x], at_x(d)) for d in (1, 3, 2)]

    early_y, swap = [], []

    def send_proj():
        operands[4].wait()
        early_y.extend([copy_to(proj, pb.at[0, y], at(dy=d)) for d in (1, 3, 2)])
        pb[0, y] = proj[...]

    def wn_rows():
        tiles(8, 256, early_rows)

    early_wn = {}

    def wn_send(j):
        early_wn[j] = new_recv()
        for d in (0, 1, 3, 2):
            cols = pl.ds(pl.multiple_of(((y + 4 - d) % 4) * 512, 512), 512)
            if j == 0 and d == 0:
                wnb[0, 0] = wn[0, :, cols]
            else:
                copy_to(wn.at[j, :, cols], wnb.at[j, d], at(dy=-d, dz=out_hop[j] * sg), early_wn[j])

    def swap_proj():
        for copy in early_y:
            copy.wait_recv()
        swap.append(copy_to(pb.at[0], pb.at[1], at(other=True)))

    other_k = pl.ds(128, 128)

    def student_rows():
        for j in range(4):
            into = wnb.at[j, pl.ds(1, 3)] if j == 0 else wnb.at[j]
            arrival(into, early_wn[j]).wait_recv()
            blocks = [wnb[j, d].astype(F32) for d in range(4)]
            order = [blocks[(d + 4 - g) % 4][d * 8:d * 8 + 8] for g in range(4) for d in range(4)]
            wkt[j] = jnp.concatenate(order, axis=0).T.reshape(8, 2, 32, 128).astype(BF)
            wk[j, :, :, 0:128] = wkt[j, :, c]
        swap.append(copy_to(wkt.at[:, :, 1 - c], wk.at[:, :, :, other_k], at(other=True)))

    def gram_3():
        for copy in gram["x"]:
            copy.wait_recv()
        gtt[...] = gt[...].reshape(128, 512).astype(F32).T.reshape(8, 2, 32, 128).astype(BF)
        gtf[:, :, 0:128] = gtt[:, c]
        swap.append(copy_to(gtt.at[:, 1 - c], gtf.at[:, :, other_k], at(other=True)))

    to_x, act_x, back_core, back_pair, back_z, round_y, far_y, whole = {}, {}, {}, {}, {}, {}, {}, {}
    parts = ((0, 4), (1024, 3))

    def spans(j):
        return parts if j == 3 else ((0, 7),)

    def arrive(j):
        into = rows.at[0, 0, 0, pl.ds(1, 3)] if j == 0 else rows.at[0, j, 0]
        arrival(into, direct[j]).wait_recv()
        if j:
            via[j] = new_recv()
            copy_to(rows.at[0, j, 0], rows.at[1, j, 0], at(dz=sg), via[j])
        over[j] = copy_to(rows.at[0, j, 0], rows.at[0, j, 1], at(other=True))

    def arrive_via(j):
        arrival(rows.at[1, j, 0], via[j]).wait_recv()
        over_via[j] = copy_to(rows.at[1, j, 0], rows.at[1, j, 1], at(other=True))

    def gate_up(j):
        over[j].wait_recv()
        over_via[j].wait_recv()

        def unfold(cols):
            block = rows[:, j, :, :, :, cols].astype(F32).reshape(16, 2, 8, 128)
            xk[:, cols] = block[:, 0].reshape(128, 128).astype(BF)
            xk[:, pl.ds(pl.multiple_of(896 + cols.start, 128), 128)] = block[:, 1].reshape(128, 128).astype(BF)

        tiles(7, 128, unfold)
        if j == 0:
            weights[0].wait()
            weights[1].wait()
        for part in range(2):
            def step(cols):
                out = dot(xk[...], wgu[part, :, cols])
                gu[j, part, :, :, cols] = out.reshape(4, 32, 256).astype(BF)

            tiles(2, 256, step)
        to_x[j] = [copy_to(gu.at[j, :, (x + d) % 4], xr.at[j, d], at_x(d)) for d in (1, 3, 2)]

    def activate(j):
        for copy in to_x[j]:
            copy.wait_recv()
        gate, up = [
            gu[j, part, x].astype(F32) + sum(xr[j, d, part].astype(F32) for d in (1, 2, 3)) for part in range(2)
        ]
        act[j, x] = (gate / (1.0 + jnp.exp(-gate)) * up).astype(BF)
        act_x[j] = [copy_to(act.at[j, x], act.at[j, x], at_x(d)) for d in (1, 3, 2)]

    def down(j):
        for copy in act_x[j]:
            copy.wait_recv()
        if j == 0:
            weights[2].wait()

        def step(cols):
            out = dot(act[j].reshape(128, H), wd[:, cols]).reshape(4, 32, 256)
            for i in range(2):
                prodf[j, i, :, cols] = out[2 * i]
                ps[j, i, :, cols] = out[2 * i + 1].astype(BF)

        for first, count in spans(j):
            tiles(count, 256, step, first)
            cols = pl.ds(first, count * 256)
            back_core[j, first] = copy_to(ps.at[j, :, :, cols], pr.at[j, :, :, cols], at(other=True))

    def core_sum(j):
        def step(cols):
            vs[j, :, cols] = (prodf[j, 1, :, cols] + pr[j, 1, :, cols].astype(F32)).astype(BF)

        for first, count in spans(j):
            back_core[j, first].wait_recv()
            tiles(count, 256, step, first)
            cols = pl.ds(first, count * 256)
            back_pair[j, first] = copy_to(vs.at[j, :, cols], vr.at[j, :, cols], at(dz=sg))

    def pair_sum(j):
        def step(cols):
            ob[j, 0, 0, :, cols] = (
                prodf[j, 0, :, cols] + pr[j, 0, :, cols].astype(F32) + vr[j, :, cols].astype(F32)
            ).astype(BF)

        for first, count in spans(j):
            back_pair[j, first].wait_recv()
            tiles(count, 256, step, first)
            cols = pl.ds(first, count * 256)
            round_y[j, first] = [
                copy_to(ob.at[j, 0, 0, :, cols], ob.at[j, 0, g, :, cols], at(dy=g)) for g in (1, 3)
            ]
        if j:
            back_z[j] = copy_to(ob.at[j, 0, 0], ret.at[j], at(dz=-j * sg))

    def relay(j):
        low, high = pl.ds(0, 16), pl.ds(16, 16)
        for first, count in spans(j):
            cols = pl.ds(first, count * 256)
            far_y[j, first] = []
            for side, (g, rows_g, dy) in enumerate(((1, low, 1), (3, high, -1))):
                round_y[j, first][side].wait_recv()
                far_y[j, first].append(
                    copy_to(ob.at[j, 0, g, rows_g, cols], ob.at[j, 0, 2, rows_g, cols], at(dy=dy))
                )

    def far(j):
        for first, count in spans(j):
            for copy in far_y[j, first]:
                copy.wait_recv()
            cols = pl.ds(first, count * 256)
            whole[j, first] = copy_to(ob.at[j, 0, :, :, cols], ob.at[j, 1, :, :, cols], at(other=True))

    def product(j, cols):
        return dot(wk[j].reshape(256, 256), ob[j, :, :, :, cols].reshape(256, 256))

    def student():
        for copy in swap:
            copy.wait_recv()
        for j in range(3):
            whole[j, 0].wait_recv()

        def step(cols):
            part = dot(gtf[...].reshape(256, 256), pb[:, :, :, cols].reshape(256, 256))
            part -= product(0, cols) + product(1, cols) + product(2, cols)
            m[:, :, cols] = part.reshape(8, 32, 256)

        tiles(7, 256, step)

    def finish(part):
        first, count = parts[part]
        whole[3, first].wait_recv()

        def step(cols):
            m[:, :, cols] -= product(3, cols).reshape(8, 32, 256)

        tiles(count, 256, step, first)

    def run(steps):
        for name, j in steps:
            name(j)

    def when(f):
        return (lambda _: f(), 0)

    run([
        when(wn_rows), (arrive, 0), (arrive_via, 0), when(gram_start), (arrive, 1), (arrive, 2), when(send_proj),
        (wn_send, 3), (gate_up, 0), (arrive_via, 1), (wn_send, 1), (arrive, 3), (wn_send, 2), (gate_up, 1),
        (arrive_via, 2), (activate, 0), when(gram_0), (gate_up, 2), (arrive_via, 3), (activate, 1), (down, 0),
        (gate_up, 3), (core_sum, 0), (activate, 2), (down, 1), (wn_send, 0), (core_sum, 1), (activate, 3),
        (pair_sum, 0), (down, 2), (core_sum, 2), (pair_sum, 1), (down, 3), (relay, 0), (core_sum, 3), when(gram_1),
        (pair_sum, 2), when(student_rows), (far, 0), when(swap_proj), (pair_sum, 3), (relay, 2), (relay, 1),
        (relay, 3), when(gram_2), (far, 2), (far, 1), when(gram_3), (far, 3), when(student),
    ])

    to_owner = []

    def send_target():
        for j in (1, 2, 3):
            back_z[j].wait_recv()

        def sort_rows(cols):
            blocks = [ob[0, 0, 0, :, cols].astype(F32)] + [ret[j, :, cols].astype(F32) for j in (1, 2, 3)]
            for d in range(4):
                tb[d, :, cols] = jnp.concatenate([b[d * 8:d * 8 + 8] for b in blocks], axis=0).astype(BF)

        tiles(7, 256, sort_rows)
        to_owner.extend([copy_to(tb.at[d], tg.at[d], at(dy=d)) for d in (1, 3, 2)])
        tg[0] = tb[0]

    def mine(d, first, count, cols):
        return m[(z + 8 + d) % 8, first:first + count, cols]

    hops = {}
    for step in range(4):
        for half, (start, count) in enumerate(parts):
            cols = pl.ds(start, count * 256)
            if step == 0:
                finish(half)
            for way, sign in ((0, -1), (1, 1)):
                slot = step * 2 + way
                far = sign * (4 - step)
                if step == 0:
                    zs[slot, 0:16, cols] = mine(far, 16 * way, 16, cols).astype(BF)
                    src, dst = zs.at[slot, pl.ds(0, 16), cols], zr.at[slot, pl.ds(0, 16), cols]
                else:
                    hops[step - 1, half, way].wait_recv()
                    if step == 1:
                        first = 16 * way
                        total = mine(far, first, 16, cols) + zr[slot - 2, 0:16, cols].astype(F32)
                        zs[slot, first:first + 16, cols] = total.astype(BF)
                        zs[slot, 16 - first:32 - first, cols] = mine(far, 16 - first, 16, cols).astype(BF)
                    else:
                        zs[slot, :, cols] = (mine(far, 0, 32, cols) + zr[slot - 2, :, cols].astype(F32)).astype(BF)
                    src, dst = zs.at[slot, :, cols], zr.at[slot, :, cols]
                hops[step, half, way] = copy_to(src, dst, at(dz=sign))
        if step == 0:
            send_target()
        if step == 1:
            for copy in started[:-8]:
                copy.wait_send()
            del started[:-8]
        if step == 2:
            for copy in to_owner:
                copy.wait_recv()

            def write_target(cols):
                target[:, cols] = dot_t(weigh[...], tg[:, :, cols].reshape(128, 256)).astype(BF)

            tiles(7, 256, write_target)
            target_out = pltpu.make_async_copy(target, target_hbm, local_sem.at[8])
            target_out.start()
    for half, (start, count) in enumerate(parts):
        cols = pl.ds(start, count * 256)
        total = mine(0, 0, 32, cols)
        for way in range(2):
            hops[3, half, way].wait_recv()
            total += zr[6 + way, :, cols].astype(F32)
        grad[:, cols] = total * (loss_scale / 16384)
    grad_out = pltpu.make_async_copy(grad, grad_hbm, local_sem.at[9])
    grad_out.start()
    for copy in started:
        copy.wait_send()
    target_out.wait()
    grad_out.wait()


N_COPIES = 19 + 3 + 8 + 12 + 12 + 5 + 5 + 3 + 40 + 3 + 15 + 14 + 3 + 3 + 16


def body(teacher_in, expert_ids, gate_codes, w_gate, w_up, w_down, student_in, projection):
    hbm = pl.BlockSpec(memory_space=pl.ANY)
    return pl.pallas_call(
        kernel,
        out_shape=(
            jax.ShapeDtypeStruct((256, W), BF),
            jax.ShapeDtypeStruct((32, W), F32),
        ),
        in_specs=[hbm] * 8,
        out_specs=(hbm, hbm),
        scratch_shapes=[
            pltpu.VMEM((256, W), BF),
            pltpu.VMEM((32, W), F32),
            pltpu.VMEM((4, 32, W), BF),
            pltpu.VMEM((8, 256), jnp.int32),
            pltpu.VMEM((8, 256), jnp.int32),
            pltpu.VMEM((32, W), BF),
            pltpu.VMEM((256, W), BF),
            pltpu.VMEM((256, 2048), BF),
            pltpu.VMEM((2, W, H), BF),
            pltpu.VMEM((H, W), BF),
            pltpu.VMEM((128, 256), BF),
            pltpu.VMEM((16, 16, W // 2), BF),
            pltpu.VMEM((256, 2048), BF),
            pltpu.VMEM((512, 256), BF),
            pltpu.VMEM((4, 32, 2048), BF),
            pltpu.VMEM((8, 2, 32, 2048), BF),
            pltpu.VMEM((2, 4, 2, 4, 16, W // 2), BF),
            pltpu.VMEM((128, W), BF),
            pltpu.VMEM((4, 2, 4, 32, H), BF),
            pltpu.VMEM((4, 4, 2, 32, H), BF),
            pltpu.VMEM((4, 4, 32, H), BF),
            pltpu.VMEM((4, 2, 32, W), F32),
            pltpu.VMEM((4, 2, 32, W), BF),
            pltpu.VMEM((4, 2, 32, W), BF),
            pltpu.VMEM((4, 32, W), BF),
            pltpu.VMEM((4, 32, W), BF),
            pltpu.VMEM((4, 2, 4, 32, W), BF),
            pltpu.VMEM((4, 32, W), BF),
            pltpu.VMEM((4, 32, W), BF),
            pltpu.VMEM((4, 4, 32, 512), BF),
            pltpu.VMEM((2, 4, 32, W), BF),
            pltpu.VMEM((8, 32, 2048), BF),
            pltpu.VMEM((4, 8, 32, 512), BF),
            pltpu.VMEM((4, 8, 32, 512), BF),
            pltpu.VMEM((8, 32, 512), BF),
            pltpu.VMEM((8, 32, 512), BF),
            pltpu.VMEM((4, 32, 512), BF),
            pltpu.VMEM((8, 2, 32, 128), BF),
            pltpu.VMEM((8, 32, 256), BF),
            pltpu.VMEM((4, 8, 2, 32, 128), BF),
            pltpu.VMEM((4, 8, 32, 256), BF),
            pltpu.VMEM((8, 32, W), F32),
            pltpu.VMEM((8, 32, W), BF),
            pltpu.VMEM((8, 32, W), BF),
            pltpu.SemaphoreType.DMA((N_COPIES,)),
            pltpu.SemaphoreType.DMA((N_COPIES,)),
            pltpu.SemaphoreType.DMA((10,)),
        ],
        compiler_params=pltpu.CompilerParams(
            collective_id=0, has_side_effects=True, vmem_limit_bytes=60 * 1024 * 1024
        ),
        cost_estimate=pl.CostEstimate(flops=8_000_000_000, bytes_accessed=12_000_000, transcendentals=0),
    )(expert_ids.T, gate_codes.T, projection, teacher_in, student_in, w_gate, w_up, w_down)


def solution(mesh):
    in_specs = (
        P("exp", "pair"),
        P("exp", None),
        P("exp", None),
        P("pair", "exp"),
        P("pair", "exp"),
        P("exp", "pair"),
        P("exp", None),
        P("exp", "pair"),
    )
    out_specs = (P("exp", "pair"), P("exp", "pair"))
    return jax.shard_map(body, mesh=mesh, in_specs=in_specs, out_specs=out_specs, check_vma=False)
```

```python
import jax
import jax.numpy as jnp
from jax import lax
from jax.experimental import pallas as pl
from jax.experimental.pallas import tpu as pltpu
from jax.sharding import PartitionSpec as P

CAP = 8
MESH = pl.DeviceIdType.MESH
BF = jnp.bfloat16
F32 = jnp.float32

loss_scale = 128.0
norm_epsilon = 1e-06

W = 1792
H = 512


def dot_t(a, b):
    return lax.dot_general(a, b, (((0,), (0,)), ((), ())), preferred_element_type=F32)


def dot(a, b):
    return jnp.dot(a, b, preferred_element_type=F32)


def tiles(count, size, f, first=0):
    for i in range(count):
        f(pl.ds(first + i * size, size))


def kernel(
    ids_hbm, codes_hbm, proj_hbm, teacher_hbm, student_hbm, wg_hbm, wu_hbm, wd_hbm,
    target_hbm, grad_hbm, target, grad, tg, ids, codes, proj, teacher, student_in,
    wgu, wd, weigh, packed, normed, left_x, wn, gx, rows, xk, gu, xr, act, prodf, ps, pr, vs, vr, ob, ret, tb,
    wnb, pb, gxr, gs1, gr1, gs2, gr2, gt, gtt, gtf, wkt, wk, m, zs, zr,
    send_sem, recv_sem, local_sem,
):
    e = lax.axis_index("exp")
    x = lax.axis_index("pair")
    y, z, c = e // 16, (e // 2) % 8, e % 2
    sg = 1 - 2 * (z % 2)

    def at(dy=0, dz=0, other=False):
        yy, zz = (y + dy + 4) % 4, (z + dz + 8) % 8
        return (yy * 16 + zz * 2 + (1 - c if other else c), x)

    def at_x(dx):
        return (e, (x + dx) % 4)

    number = [0, 0]
    started = []

    def new_recv():
        number[1] += 1
        return number[1] - 1

    def copy_to(src, dst, device, recv=None):
        i = number[0]
        number[0] += 1
        copy = pltpu.make_async_remote_copy(
            src_ref=src, dst_ref=dst, send_sem=send_sem.at[i],
            recv_sem=recv_sem.at[new_recv() if recv is None else recv],
            device_id=device, device_id_type=MESH,
        )
        copy.start()
        started.append(copy)
        return copy

    def arrival(dst, recv):
        return pltpu.make_async_remote_copy(
            src_ref=dst, dst_ref=dst, send_sem=send_sem.at[0], recv_sem=recv_sem.at[recv],
            device_id=at(other=True), device_id_type=MESH,
        )

    weights = [
        pltpu.make_async_copy(wg_hbm, wgu.at[0], local_sem.at[0]),
        pltpu.make_async_copy(wu_hbm, wgu.at[1], local_sem.at[1]),
        pltpu.make_async_copy(wd_hbm, wd, local_sem.at[2]),
    ]
    operands = [
        pltpu.make_async_copy(src, dst, local_sem.at[3 + i])
        for i, (src, dst) in enumerate((
            (ids_hbm, ids), (codes_hbm, codes), (teacher_hbm, teacher), (student_hbm, student_in), (proj_hbm, proj),
        ))
    ]
    for copy in operands:
        copy.start()

    barrier = pltpu.get_barrier_semaphore()
    peers = [at(dy=dy, dz=dz) for dy in range(4) for dz in (0, 1, -1, 2, -2, 3, -3) if dy or dz]
    peers += [at(dz=4), at(other=True)] + [at_x(d) for d in (1, 2, 3)]
    for peer in peers:
        pl.semaphore_signal(barrier, inc=1, device_id=peer, device_id_type=MESH)

    operands[0].wait()
    operands[1].wait()
    place = lax.broadcasted_iota(jnp.int32, (128, 256), 0)
    hop = (place >> 3) & 3
    shift = jnp.where(hop == 0, 0, jnp.where(hop == 1, -sg, jnp.where(hop == 2, sg, 2)))
    expert = ((y + 4 - (place >> 5)) & 3) * 4 + ((z // 2 + 4 + shift) & 3)
    hit = jnp.zeros((128, 256), F32)
    code = jnp.zeros((128, 256), jnp.int32)
    for k in range(8):
        same = ids[k:k + 1, :] == expert
        hit = jnp.where(same, 1.0, hit)
        code = jnp.where(same, codes[k:k + 1, :], code)
    ahead = lax.broadcasted_iota(jnp.int32, (256, 256), 0) < lax.broadcasted_iota(jnp.int32, (256, 256), 1)
    rank = dot(hit.astype(BF), jnp.where(ahead, 1.0, 0.0).astype(BF))
    chosen = jnp.where(rank == (place & 7).astype(F32), hit, 0.0)
    weigh[...] = (chosen * code.astype(F32) * (1.0 / 256.0)).astype(BF)
    chosen = chosen.astype(BF)

    def pack(cols):
        size = cols.size
        low = dot(chosen, teacher[:, cols]).reshape(16, 8, size)
        high = dot(chosen, teacher[:, pl.ds(896 + cols.start, size)]).reshape(16, 8, size)
        packed[:, :, cols] = jnp.concatenate([low, high], axis=1).astype(BF)

    operands[2].wait()
    tiles(3, 256, pack)
    tiles(1, 128, pack, 768)
    pl.semaphore_wait(barrier, len(peers))

    out_hop = (0, -1, 2, -3)
    direct, via, over, over_via = {}, {}, {}, {}
    for j in range(4):
        direct[j] = new_recv()
        for d in (1, 3, 2, 0):
            if j or d:
                copy_to(packed.at[d * 4 + j], rows.at[0, j, 0, d], at(dy=-d, dz=out_hop[j] * sg), direct[j])
        if j == 0:
            via[0] = new_recv()
            for d in (0, 1, 3, 2):
                copy_to(packed.at[d * 4], rows.at[1, 0, 0, d], at(dy=-d, dz=sg), via[0])
    rows[0, 0, 0, 0] = packed[0]
    for copy in weights:
        copy.start()

    operands[3].wait()
    wide = student_in[...].astype(F32)
    scale = 1.0 / jnp.sqrt(jnp.mean(wide * wide, axis=1, keepdims=True) + norm_epsilon)
    normed[...] = (wide * scale).astype(BF)
    left_x[...] = normed[:, pl.ds(pl.multiple_of(x * 512, 512), 512)].astype(F32).T.astype(BF)

    def early(cols):
        gx[:, :, :, cols] = dot(left_x[...], normed[:, cols]).reshape(8, 2, 32, 256).astype(BF)

    def early_rows(cols):
        out = dot(weigh[...], normed[:, cols]).reshape(4, 4, 8, 256)
        for j in range(4):
            wn[j, :, cols] = jnp.concatenate([out[d, j] for d in range(4)], axis=0).astype(BF)

    gram = {}

    def gram_part(q):
        tiles(2, 256, early, q * 512)
        cols = pl.ds(q * 512, 512)
        gram["core", q] = copy_to(gx.at[:, 1 - c, :, cols], gxr.at[:, :, cols], at(other=True))

    def gram_0():
        for q in range(4):
            gram["core", q].wait_recv()
            cols = slice(q * 512, q * 512 + 512)
            gs1[q] = (gx[:, c, :, cols].astype(F32) + gxr[:, :, cols].astype(F32)).astype(BF)
        gram["y"] = [copy_to(gs1.at[(y + d) % 4], gr1.at[d], at(dy=d)) for d in (1, 3, 2)]

    def gram_1():
        for copy in gram["y"]:
            copy.wait_recv()
        total = gs1[y].astype(F32) + sum(gr1[d].astype(F32) for d in (1, 2, 3))
        gs2[...] = total.astype(BF)
        gram["z"] = [copy_to(gs2.at[(z + d) % 8], gr2.at[d], at(dz=d)) for d in (1, 7, 2, 6, 3, 5, 4)]

    def gram_2():
        for copy in gram["z"]:
            copy.wait_recv()
        total = gs2[z].astype(F32) + sum(gr2[d].astype(F32) for d in range(1, 8))
        gt[x] = total.astype(BF)
        gram["x"] = [copy_to(gt.at[x], gt.at[x], at_x(d)) for d in (1, 3, 2)]

    early_y, swap = [], []

    def send_proj():
        operands[4].wait()
        early_y.extend([copy_to(proj, pb.at[0, y], at(dy=d)) for d in (1, 3, 2)])
        pb[0, y] = proj[...]

    def wn_rows():
        tiles(8, 256, early_rows)

    early_wn = {}

    def wn_send(j):
        early_wn[j] = new_recv()
        for d in (0, 1, 3, 2):
            cols = pl.ds(pl.multiple_of(((y + 4 - d) % 4) * 512, 512), 512)
            if j == 0 and d == 0:
                wnb[0, 0] = wn[0, :, cols]
            else:
                copy_to(wn.at[j, :, cols], wnb.at[j, d], at(dy=-d, dz=out_hop[j] * sg), early_wn[j])

    def swap_proj():
        for copy in early_y:
            copy.wait_recv()
        swap.append(copy_to(pb.at[0], pb.at[1], at(other=True)))

    other_k = pl.ds(128, 128)

    def student_rows():
        for j in range(4):
            into = wnb.at[j, pl.ds(1, 3)] if j == 0 else wnb.at[j]
            arrival(into, early_wn[j]).wait_recv()
            blocks = [wnb[j, d].astype(F32) for d in range(4)]
            order = [blocks[(d + 4 - g) % 4][d * 8:d * 8 + 8] for g in range(4) for d in range(4)]
            wkt[j] = jnp.concatenate(order, axis=0).T.reshape(8, 2, 32, 128).astype(BF)
            wk[j, :, :, 0:128] = wkt[j, :, c]
        swap.append(copy_to(wkt.at[:, :, 1 - c], wk.at[:, :, :, other_k], at(other=True)))

    def gram_3():
        for copy in gram["x"]:
            copy.wait_recv()
        gtt[...] = gt[...].reshape(128, 512).astype(F32).T.reshape(8, 2, 32, 128).astype(BF)
        gtf[:, :, 0:128] = gtt[:, c]
        swap.append(copy_to(gtt.at[:, 1 - c], gtf.at[:, :, other_k], at(other=True)))

    to_x, act_x, back_core, back_pair, back_z, round_y, far_y, whole = {}, {}, {}, {}, {}, {}, {}, {}
    parts = ((0, 3), (768, 2), (1280, 2))

    def spans(j):
        return parts if j == 3 else ((0, 7),)

    def arrive(j):
        into = rows.at[0, 0, 0, pl.ds(1, 3)] if j == 0 else rows.at[0, j, 0]
        arrival(into, direct[j]).wait_recv()
        if j:
            via[j] = new_recv()
            copy_to(rows.at[0, j, 0], rows.at[1, j, 0], at(dz=sg), via[j])
        over[j] = copy_to(rows.at[0, j, 0], rows.at[0, j, 1], at(other=True))

    def arrive_via(j):
        arrival(rows.at[1, j, 0], via[j]).wait_recv()
        over_via[j] = copy_to(rows.at[1, j, 0], rows.at[1, j, 1], at(other=True))

    def gate_up(j):
        over[j].wait_recv()
        over_via[j].wait_recv()

        def unfold(cols):
            block = rows[:, j, :, :, :, cols].astype(F32).reshape(16, 2, 8, 128)
            xk[:, cols] = block[:, 0].reshape(128, 128).astype(BF)
            xk[:, pl.ds(896 + cols.start, 128)] = block[:, 1].reshape(128, 128).astype(BF)

        tiles(7, 128, unfold)
        if j == 0:
            weights[0].wait()
            weights[1].wait()
        for part in range(2):
            gu[j, part] = dot(xk[...], wgu[part]).reshape(4, 32, H).astype(BF)
        to_x[j] = [copy_to(gu.at[j, :, (x + d) % 4], xr.at[j, d], at_x(d)) for d in (1, 3, 2)]

    def activate(j):
        for copy in to_x[j]:
            copy.wait_recv()
        gate, up = [
            gu[j, part, x].astype(F32) + sum(xr[j, d, part].astype(F32) for d in (1, 2, 3)) for part in range(2)
        ]
        act[j, x] = (gate / (1.0 + jnp.exp(-gate)) * up).astype(BF)
        act_x[j] = [copy_to(act.at[j, x], act.at[j, x], at_x(d)) for d in (1, 3, 2)]

    def down(j):
        for copy in act_x[j]:
            copy.wait_recv()
        if j == 0:
            weights[2].wait()

        def step(cols):
            out = dot(act[j].reshape(128, H), wd[:, cols]).reshape(4, 32, 256)
            for i in range(2):
                prodf[j, i, :, cols] = out[2 * i]
                ps[j, i, :, cols] = out[2 * i + 1].astype(BF)

        for first, count in spans(j):
            tiles(count, 256, step, first)
            cols = pl.ds(first, count * 256)
            back_core[j, first] = copy_to(ps.at[j, :, :, cols], pr.at[j, :, :, cols], at(other=True))

    def core_sum(j):
        def step(cols):
            vs[j, :, cols] = (prodf[j, 1, :, cols] + pr[j, 1, :, cols].astype(F32)).astype(BF)

        for first, count in spans(j):
            back_core[j, first].wait_recv()
            tiles(count, 256, step, first)
            cols = pl.ds(first, count * 256)
            back_pair[j, first] = copy_to(vs.at[j, :, cols], vr.at[j, :, cols], at(dz=sg))

    def pair_sum(j):
        def step(cols):
            ob[j, 0, 0, :, cols] = (
                prodf[j, 0, :, cols] + pr[j, 0, :, cols].astype(F32) + vr[j, :, cols].astype(F32)
            ).astype(BF)

        for first, count in spans(j):
            back_pair[j, first].wait_recv()
            tiles(count, 256, step, first)
            cols = pl.ds(first, count * 256)
            round_y[j, first] = [
                copy_to(ob.at[j, 0, 0, :, cols], ob.at[j, 0, g, :, cols], at(dy=g)) for g in (1, 3)
            ]
        if j:
            back_z[j] = copy_to(ob.at[j, 0, 0], ret.at[j], at(dz=-j * sg))

    def relay(j):
        low, high = pl.ds(0, 16), pl.ds(16, 16)
        for first, count in spans(j):
            cols = pl.ds(first, count * 256)
            far_y[j, first] = []
            for side, (g, rows_g, dy) in enumerate(((1, low, 1), (3, high, -1))):
                round_y[j, first][side].wait_recv()
                far_y[j, first].append(
                    copy_to(ob.at[j, 0, g, rows_g, cols], ob.at[j, 0, 2, rows_g, cols], at(dy=dy))
                )

    def far(j):
        for first, count in spans(j):
            for copy in far_y[j, first]:
                copy.wait_recv()
            cols = pl.ds(first, count * 256)
            whole[j, first] = copy_to(ob.at[j, 0, :, :, cols], ob.at[j, 1, :, :, cols], at(other=True))

    def product(j, cols):
        return dot(wk[j].reshape(256, 256), ob[j, :, :, :, cols].reshape(256, 256))

    def student():
        for copy in swap:
            copy.wait_recv()
        for j in range(3):
            whole[j, 0].wait_recv()

        def step(cols):
            part = dot(gtf[...].reshape(256, 256), pb[:, :, :, cols].reshape(256, 256))
            part -= product(0, cols) + product(1, cols) + product(2, cols)
            m[:, :, cols] = part.reshape(8, 32, 256)

        tiles(7, 256, step)

    def finish(part):
        first, count = parts[part]
        whole[3, first].wait_recv()

        def step(cols):
            m[:, :, cols] -= product(3, cols).reshape(8, 32, 256)

        tiles(count, 256, step, first)

    def run(steps):
        for name, j in steps:
            name(j)

    def when(f):
        return (lambda _: f(), 0)

    run([
        when(send_proj), (arrive, 0), (arrive_via, 0), (arrive, 1), when(wn_rows), (gram_part, 3), (gram_part, 2),
        (arrive, 2), (wn_send, 0), (gate_up, 0), (arrive_via, 1), (gram_part, 1), (arrive_via, 2), (gram_part, 0),
        (gate_up, 1), (gate_up, 2), (arrive, 3), (activate, 0), (wn_send, 1), when(gram_0), (wn_send, 2),
        (activate, 2), (arrive_via, 3), (down, 0), (activate, 1), (down, 2), (wn_send, 3), (core_sum, 0), (down, 1),
        (core_sum, 2), (gate_up, 3), when(swap_proj), (pair_sum, 0), (core_sum, 1), when(gram_1), (pair_sum, 2),
        (activate, 3), (relay, 0), when(student_rows), (pair_sum, 1), (down, 3), (relay, 2), (far, 0), (relay, 1),
        (core_sum, 3), (far, 2), when(gram_2), (far, 1), (pair_sum, 3), when(gram_3), (relay, 3), (far, 3),
        when(student),
    ])

    to_owner = []

    def send_target():
        for j in (1, 2, 3):
            back_z[j].wait_recv()

        def sort_rows(cols):
            blocks = [ob[0, 0, 0, :, cols].astype(F32)] + [ret[j, :, cols].astype(F32) for j in (1, 2, 3)]
            for d in range(4):
                tb[d, :, cols] = jnp.concatenate([b[d * 8:d * 8 + 8] for b in blocks], axis=0).astype(BF)

        tiles(7, 256, sort_rows)
        to_owner.extend([copy_to(tb.at[d], tg.at[d], at(dy=d)) for d in (1, 3, 2)])
        tg[0] = tb[0]

    def mine(d, first, count, cols):
        return m[(z + 8 + d) % 8, first:first + count, cols]

    hops = {}
    for step in range(4):
        for half, (start, count) in enumerate(parts):
            cols = pl.ds(start, count * 256)
            if step == 0:
                finish(half)
            for way, sign in ((0, -1), (1, 1)):
                slot = step * 2 + way
                far = sign * (4 - step)
                if step == 0:
                    zs[slot, 0:16, cols] = mine(far, 16 * way, 16, cols).astype(BF)
                    src, dst = zs.at[slot, pl.ds(0, 16), cols], zr.at[slot, pl.ds(0, 16), cols]
                else:
                    hops[step - 1, half, way].wait_recv()
                    if step == 1:
                        first = 16 * way
                        total = mine(far, first, 16, cols) + zr[slot - 2, 0:16, cols].astype(F32)
                        zs[slot, first:first + 16, cols] = total.astype(BF)
                        zs[slot, 16 - first:32 - first, cols] = mine(far, 16 - first, 16, cols).astype(BF)
                    else:
                        zs[slot, :, cols] = (mine(far, 0, 32, cols) + zr[slot - 2, :, cols].astype(F32)).astype(BF)
                    src, dst = zs.at[slot, :, cols], zr.at[slot, :, cols]
                hops[step, half, way] = copy_to(src, dst, at(dz=sign))
        if step == 0:
            send_target()
        if step == 1:
            for copy in started[:-10]:
                copy.wait_send()
            del started[:-10]
        if step == 2:
            for copy in to_owner:
                copy.wait_recv()

            def write_target(cols):
                target[:, cols] = dot_t(weigh[...], tg[:, :, cols].reshape(128, 256)).astype(BF)

            tiles(7, 256, write_target)
            target_out = pltpu.make_async_copy(target, target_hbm, local_sem.at[8])
            target_out.start()
    for half, (start, count) in enumerate(parts):
        cols = pl.ds(start, count * 256)
        total = mine(0, 0, 32, cols)
        for way in range(2):
            hops[3, half, way].wait_recv()
            total += zr[6 + way, :, cols].astype(F32)
        grad[:, cols] = total * (loss_scale / 16384)
    grad_out = pltpu.make_async_copy(grad, grad_hbm, local_sem.at[9])
    grad_out.start()
    for copy in started:
        copy.wait_send()
    target_out.wait()
    grad_out.wait()


N_COPIES = 40 + 19 + 3 + 8 + 12 + 12 + 5 + 5 + 3 + 40 + 3 + 15 + 14 + 3 + 3 + 16


def body(teacher_in, expert_ids, gate_codes, w_gate, w_up, w_down, student_in, projection):
    hbm = pl.BlockSpec(memory_space=pl.ANY)
    return pl.pallas_call(
        kernel,
        out_shape=(
            jax.ShapeDtypeStruct((256, W), BF),
            jax.ShapeDtypeStruct((32, W), F32),
        ),
        in_specs=[hbm] * 8,
        out_specs=(hbm, hbm),
        scratch_shapes=[
            pltpu.VMEM((256, W), BF),
            pltpu.VMEM((32, W), F32),
            pltpu.VMEM((4, 32, W), BF),
            pltpu.VMEM((8, 256), jnp.int32),
            pltpu.VMEM((8, 256), jnp.int32),
            pltpu.VMEM((32, W), BF),
            pltpu.VMEM((256, W), BF),
            pltpu.VMEM((256, 2048), BF),
            pltpu.VMEM((2, W, H), BF),
            pltpu.VMEM((H, W), BF),
            pltpu.VMEM((128, 256), BF),
            pltpu.VMEM((16, 16, W // 2), BF),
            pltpu.VMEM((256, 2048), BF),
            pltpu.VMEM((512, 256), BF),
            pltpu.VMEM((4, 32, 2048), BF),
            pltpu.VMEM((8, 2, 32, 2048), BF),
            pltpu.VMEM((2, 4, 2, 4, 16, W // 2), BF),
            pltpu.VMEM((128, W), BF),
            pltpu.VMEM((4, 2, 4, 32, H), BF),
            pltpu.VMEM((4, 4, 2, 32, H), BF),
            pltpu.VMEM((4, 4, 32, H), BF),
            pltpu.VMEM((4, 2, 32, W), F32),
            pltpu.VMEM((4, 2, 32, W), BF),
            pltpu.VMEM((4, 2, 32, W), BF),
            pltpu.VMEM((4, 32, W), BF),
            pltpu.VMEM((4, 32, W), BF),
            pltpu.VMEM((4, 2, 4, 32, W), BF),
            pltpu.VMEM((4, 32, W), BF),
            pltpu.VMEM((4, 32, W), BF),
            pltpu.VMEM((4, 4, 32, 512), BF),
            pltpu.VMEM((2, 4, 32, W), BF),
            pltpu.VMEM((8, 32, 2048), BF),
            pltpu.VMEM((4, 8, 32, 512), BF),
            pltpu.VMEM((4, 8, 32, 512), BF),
            pltpu.VMEM((8, 32, 512), BF),
            pltpu.VMEM((8, 32, 512), BF),
            pltpu.VMEM((4, 32, 512), BF),
            pltpu.VMEM((8, 2, 32, 128), BF),
            pltpu.VMEM((8, 32, 256), BF),
            pltpu.VMEM((4, 8, 2, 32, 128), BF),
            pltpu.VMEM((4, 8, 32, 256), BF),
            pltpu.VMEM((8, 32, W), F32),
            pltpu.VMEM((8, 32, W), BF),
            pltpu.VMEM((8, 32, W), BF),
            pltpu.SemaphoreType.DMA((N_COPIES,)),
            pltpu.SemaphoreType.DMA((N_COPIES,)),
            pltpu.SemaphoreType.DMA((10,)),
        ],
        compiler_params=pltpu.CompilerParams(
            collective_id=0, has_side_effects=True, vmem_limit_bytes=60 * 1024 * 1024
        ),
        cost_estimate=pl.CostEstimate(flops=8_000_000_000, bytes_accessed=12_000_000, transcendentals=0),
    )(expert_ids.T, gate_codes.T, projection, teacher_in, student_in, w_gate, w_up, w_down)


def solution(mesh):
    in_specs = (
        P("exp", "pair"),
        P("exp", None),
        P("exp", None),
        P("pair", "exp"),
        P("pair", "exp"),
        P("exp", "pair"),
        P("exp", None),
        P("exp", "pair"),
    )
    out_specs = (P("exp", "pair"), P("exp", "pair"))
    return jax.shard_map(body, mesh=mesh, in_specs=in_specs, out_specs=out_specs, check_vma=False)
```

```python
import jax
import jax.numpy as jnp
from jax import lax
from jax.experimental import pallas as pl
from jax.experimental.pallas import tpu as pltpu
from jax.sharding import PartitionSpec as P

CAP = 8
MESH = pl.DeviceIdType.MESH
BF = jnp.bfloat16
F32 = jnp.float32

loss_scale = 128.0
norm_epsilon = 1e-06

W = 1792
H = 512


def dot_t(a, b):
    return lax.dot_general(a, b, (((0,), (0,)), ((), ())), preferred_element_type=F32)


def dot(a, b):
    return jnp.dot(a, b, preferred_element_type=F32)


def tiles(count, size, f, first=0):
    for i in range(count):
        f(pl.ds(first + i * size, size))


def kernel(
    ids_hbm, codes_hbm, proj_hbm, teacher_hbm, student_hbm, wg_hbm, wu_hbm, wd_hbm,
    target_hbm, grad_hbm, target, grad, tg, ids, codes, proj, teacher, student_in,
    wgu, wd, weigh, packed, normed, left_x, wn, gx, rows, xk, gu, xr, act, prodf, ps, pr, vs, vr, ob, ret, tb,
    wny, wnb, pb, gxr, gs1, gr1, gs2, gr2, gs3, gr3, gt, gtt, gtf, wkt, wk, m, zs, zr,
    send_sem, recv_sem, local_sem,
):
    e = lax.axis_index("exp")
    x = lax.axis_index("pair")
    y, z, c = e // 16, (e // 2) % 8, e % 2
    sg = 1 - 2 * (z % 2)

    by_y = [lax.rem(y + d, 4) for d in range(4)]
    by_x = [lax.rem(x + d, 4) for d in range(4)]
    by_z = [lax.rem(z + d, 8) for d in range(8)]
    by_hop = {d: lax.rem(z + d * sg + 8, 8) for d in (1, -1, 2, -2, 3, -3)}
    known = {}

    def at(dy=0, dz=0, hop=0, other=False):
        key = dy % 4, dz % 8, hop, other
        if key not in known:
            zz = by_hop[hop] if hop else by_z[dz % 8]
            known[key] = (by_y[dy % 4] * 16 + zz * 2 + (1 - c if other else c), x)
        return known[key]

    def at_x(dx):
        return (e, by_x[dx % 4])

    number = [0, 0]
    started = []

    def new_recv():
        number[1] += 1
        return number[1] - 1

    def copy_to(src, dst, device, recv=None):
        i = number[0]
        number[0] += 1
        copy = pltpu.make_async_remote_copy(
            src_ref=src, dst_ref=dst, send_sem=send_sem.at[i],
            recv_sem=recv_sem.at[new_recv() if recv is None else recv],
            device_id=device, device_id_type=MESH,
        )
        copy.start()
        started.append(copy)
        return copy

    def arrival(dst, recv):
        return pltpu.make_async_remote_copy(
            src_ref=dst, dst_ref=dst, send_sem=send_sem.at[0], recv_sem=recv_sem.at[recv],
            device_id=at(other=True), device_id_type=MESH,
        )

    weights = [
        pltpu.make_async_copy(wg_hbm, wgu.at[0], local_sem.at[0]),
        pltpu.make_async_copy(wu_hbm, wgu.at[1], local_sem.at[1]),
        pltpu.make_async_copy(wd_hbm, wd, local_sem.at[2]),
    ]
    operands = [
        pltpu.make_async_copy(src, dst, local_sem.at[3 + i])
        for i, (src, dst) in enumerate((
            (ids_hbm, ids), (codes_hbm, codes), (teacher_hbm, teacher), (student_hbm, student_in), (proj_hbm, proj),
        ))
    ]
    for copy in operands:
        copy.start()

    barrier = pltpu.get_barrier_semaphore()
    peers = [at(dy=dy, dz=dz) for dy in range(4) for dz in (0, 1, -1, 2, -2, 3, -3) if dy or dz]
    peers += [at(dz=4), at(other=True)] + [at_x(d) for d in (1, 2, 3)]
    for peer in peers:
        pl.semaphore_signal(barrier, inc=1, device_id=peer, device_id_type=MESH)

    operands[0].wait()
    operands[1].wait()
    place = lax.broadcasted_iota(jnp.int32, (128, 256), 0)
    hop = (place >> 3) & 3
    shift = jnp.where(hop == 0, 0, jnp.where(hop == 1, -sg, jnp.where(hop == 2, sg, 2)))
    expert = ((y + 4 - (place >> 5)) & 3) * 4 + ((z // 2 + 4 + shift) & 3)
    hit = jnp.zeros((128, 256), F32)
    code = jnp.zeros((128, 256), jnp.int32)
    for k in range(8):
        same = ids[k:k + 1, :] == expert
        hit = jnp.where(same, 1.0, hit)
        code = jnp.where(same, codes[k:k + 1, :], code)
    ahead = lax.broadcasted_iota(jnp.int32, (256, 256), 0) < lax.broadcasted_iota(jnp.int32, (256, 256), 1)
    rank = dot(hit.astype(BF), jnp.where(ahead, 1.0, 0.0).astype(BF))
    chosen = jnp.where(rank == (place & 7).astype(F32), hit, 0.0)
    weigh[...] = (chosen * code.astype(F32) * (1.0 / 256.0)).astype(BF)
    chosen = chosen.astype(BF)

    def pack(cols):
        size = cols.size
        low = dot(chosen, teacher[:, cols]).reshape(16, 8, size)
        high = dot(chosen, teacher[:, pl.ds(896 + cols.start, size)]).reshape(16, 8, size)
        packed[:, :, cols] = jnp.concatenate([low, high], axis=1).astype(BF)

    operands[2].wait()
    tiles(3, 256, pack)
    tiles(1, 128, pack, 768)
    pl.semaphore_wait(barrier, len(peers))

    out_hop = (0, -1, 2, -3)
    direct, via, over = {}, {}, {}
    for j in range(4):
        direct[j] = new_recv()
        for d in (1, 3, 2, 0):
            if j or d:
                copy_to(packed.at[d * 4 + j], rows.at[0, j, 0, d], at(dy=-d, hop=out_hop[j]), direct[j])
        if j == 0:
            via[0] = new_recv()
            for d in (0, 1, 3, 2):
                copy_to(packed.at[d * 4], rows.at[1, 0, 0, d], at(dy=-d, hop=1), via[0])
    rows[0, 0, 0, 0] = packed[0]
    for copy in weights:
        copy.start()

    operands[3].wait()
    wide = student_in[...].astype(F32)
    scale = 1.0 / jnp.sqrt(jnp.mean(wide * wide, axis=1, keepdims=True) + norm_epsilon)
    normed[...] = (wide * scale).astype(BF)
    left_x[...] = normed[:, pl.ds(pl.multiple_of(x * 512, 512), 512)].astype(F32).T.astype(BF)

    def early(cols):
        gx[:, :, :, cols] = dot(left_x[...], normed[:, cols]).reshape(8, 2, 32, 256).astype(BF)

    def early_rows(cols):
        out = dot(weigh[...], normed[:, cols]).reshape(4, 4, 8, 256)
        for j in range(4):
            wn[j, :, cols] = jnp.concatenate([out[d, j] for d in range(4)], axis=0).astype(BF)

    gram = {}

    def gram_start():
        tiles(8, 256, early)
        gram["core"] = copy_to(gx.at[:, 1 - c], gxr, at(other=True))

    def gram_0():
        gram["core"].wait_recv()
        for q in range(4):
            cols = slice(q * 512, q * 512 + 512)
            gs1[q] = (gx[:, c, :, cols].astype(F32) + gxr[:, :, cols].astype(F32)).astype(BF)
        gram["y"] = [copy_to(gs1.at[by_y[d]], gr1.at[d], at(dy=d)) for d in (1, 3, 2)]

    def gram_1():
        for copy in gram["y"]:
            copy.wait_recv()
        total = gs1[y].astype(F32) + sum(gr1[d].astype(F32) for d in (1, 2, 3))
        gs2[...] = total.astype(BF).reshape(4, 2, 32, 512)
        gram["pair"] = copy_to(gs2.at[:, 1 - z % 2], gr2, at(hop=1))

    def gram_1b():
        gram["pair"].wait_recv()
        gs3[...] = (gs2[:, z % 2].astype(F32) + gr2[...].astype(F32)).astype(BF)
        gram["z"] = [copy_to(gs3.at[by_z[d] // 2], gr3.at[d // 2], at(dz=d)) for d in (2, 6, 4)]

    def gram_2():
        for copy in gram["z"]:
            copy.wait_recv()
        total = gs3[z // 2].astype(F32) + sum(gr3[d].astype(F32) for d in range(1, 4))
        gt[x] = total.astype(BF)
        gram["x"] = [copy_to(gt.at[x], gt.at[x], at_x(d)) for d in (1, 3, 2)]

    early_y, swap = [], []

    def send_proj():
        operands[4].wait()
        early_y.extend([copy_to(proj, pb.at[0, y], at(dy=d)) for d in (1, 3, 2)])
        pb[0, y] = proj[...]

    wn_y, wn_z = [], {}

    def wn_rows():
        tiles(8, 256, early_rows)

        def features(yy):
            return pl.ds(pl.multiple_of(yy * 512, 512), 512)

        wn_y.extend([copy_to(wn.at[:, :, features(by_y[4 - d])], wny.at[d], at(dy=-d)) for d in (1, 3, 2)])
        wny[0] = wn[:, :, features(y)]

    def wn_send(j):
        while wn_y:
            wn_y.pop().wait_recv()
        if j:
            wn_z[j] = copy_to(wny.at[:, j], wnb.at[j], at(hop=out_hop[j]))

    def swap_proj():
        for copy in early_y:
            copy.wait_recv()
        swap.append(copy_to(pb.at[0], pb.at[1], at(other=True)))

    other_k = pl.ds(128, 128)

    def student_rows():
        for j in range(4):
            if j:
                wn_z[j].wait_recv()
            blocks = [(wnb[j, d] if j else wny[d, 0]).astype(F32) for d in range(4)]
            order = [blocks[(d + 4 - g) % 4][d * 8:d * 8 + 8] for g in range(4) for d in range(4)]
            wkt[j] = jnp.concatenate(order, axis=0).T.reshape(8, 2, 32, 128).astype(BF)
            wk[j, :, :, 0:128] = wkt[j, :, c]
        swap.append(copy_to(wkt.at[:, :, 1 - c], wk.at[:, :, :, other_k], at(other=True)))

    def gram_3():
        for copy in gram["x"]:
            copy.wait_recv()
        gtt[...] = gt[...].reshape(128, 512).astype(F32).T.reshape(8, 2, 32, 128).astype(BF)
        gtf[:, :, 0:128] = gtt[:, c]
        swap.append(copy_to(gtt.at[:, 1 - c], gtf.at[:, :, other_k], at(other=True)))

    to_x, act_x, back_core, back_pair, back_z, round_y, far_y, whole = {}, {}, {}, {}, {}, {}, {}, {}
    parts = ((0, 4), (1024, 3))

    def spans(j):
        return parts if j == 3 else ((0, 7),)

    def arrive(j):
        into = rows.at[0, 0, 0, pl.ds(1, 3)] if j == 0 else rows.at[0, j, 0]
        arrival(into, direct[j]).wait_recv()
        if j:
            via[j] = new_recv()
            copy_to(rows.at[0, j, 0], rows.at[1, j, 0], at(hop=1), via[j])

    def arrive_via(j):
        arrival(rows.at[1, j, 0], via[j]).wait_recv()
        over[j] = copy_to(rows.at[:, j, 0], rows.at[:, j, 1], at(other=True))

    def gate_up(j):
        over[j].wait_recv()

        def unfold(cols):
            block = rows[:, j, :, :, :, cols].astype(F32).reshape(16, 2, 8, 128)
            xk[:, cols] = block[:, 0].reshape(128, 128).astype(BF)
            xk[:, pl.ds(896 + cols.start, 128)] = block[:, 1].reshape(128, 128).astype(BF)

        tiles(7, 128, unfold)
        if j == 0:
            weights[0].wait()
            weights[1].wait()
        for part in range(2):
            gu[j, part] = dot(xk[...], wgu[part]).reshape(4, 32, H).astype(BF)
        to_x[j] = [copy_to(gu.at[j, :, by_x[d]], xr.at[j, d], at_x(d)) for d in (1, 3, 2)]

    def activate(j):
        for copy in to_x[j]:
            copy.wait_recv()
        gate, up = [
            gu[j, part, x].astype(F32) + sum(xr[j, d, part].astype(F32) for d in (1, 2, 3)) for part in range(2)
        ]
        act[j, x] = (gate / (1.0 + jnp.exp(-gate)) * up).astype(BF)
        act_x[j] = [copy_to(act.at[j, x], act.at[j, x], at_x(d)) for d in (1, 3, 2)]

    def down(j):
        for copy in act_x[j]:
            copy.wait_recv()
        if j == 0:
            weights[2].wait()

        def step(cols):
            out = dot(act[j].reshape(128, H), wd[:, cols]).reshape(4, 32, 256)
            for i in range(2):
                prodf[j, i, :, cols] = out[2 * i]
                ps[j, i, :, cols] = out[2 * i + 1].astype(BF)

        for first, count in spans(j):
            tiles(count, 256, step, first)
            cols = pl.ds(first, count * 256)
            back_core[j, first] = copy_to(ps.at[j, :, :, cols], pr.at[j, :, :, cols], at(other=True))

    def core_sum(j):
        def step(cols):
            vs[j, :, cols] = (prodf[j, 1, :, cols] + pr[j, 1, :, cols].astype(F32)).astype(BF)

        for first, count in spans(j):
            back_core[j, first].wait_recv()
            tiles(count, 256, step, first)
            cols = pl.ds(first, count * 256)
            back_pair[j, first] = copy_to(vs.at[j, :, cols], vr.at[j, :, cols], at(hop=1))

    def pair_sum(j):
        def step(cols):
            ob[j, 0, 0, :, cols] = (
                prodf[j, 0, :, cols] + pr[j, 0, :, cols].astype(F32) + vr[j, :, cols].astype(F32)
            ).astype(BF)

        for first, count in spans(j):
            back_pair[j, first].wait_recv()
            tiles(count, 256, step, first)
            cols = pl.ds(first, count * 256)
            round_y[j, first] = [
                copy_to(ob.at[j, 0, 0, :, cols], ob.at[j, 0, g, :, cols], at(dy=g)) for g in (1, 3)
            ]
        if j:
            back_z[j] = copy_to(ob.at[j, 0, 0], ret.at[j], at(hop=-j))

    def relay(j):
        low, high = pl.ds(0, 16), pl.ds(16, 16)
        for first, count in spans(j):
            cols = pl.ds(first, count * 256)
            far_y[j, first] = []
            for side, (g, rows_g, dy) in enumerate(((1, low, 1), (3, high, -1))):
                round_y[j, first][side].wait_recv()
                far_y[j, first].append(
                    copy_to(ob.at[j, 0, g, rows_g, cols], ob.at[j, 0, 2, rows_g, cols], at(dy=dy))
                )

    def far(j):
        for first, count in spans(j):
            for copy in far_y[j, first]:
                copy.wait_recv()
            cols = pl.ds(first, count * 256)
            whole[j, first] = copy_to(ob.at[j, 0, :, :, cols], ob.at[j, 1, :, :, cols], at(other=True))

    def product(j, cols):
        return dot(wk[j].reshape(256, 256), ob[j, :, :, :, cols].reshape(256, 256))

    def student():
        for copy in swap:
            copy.wait_recv()
        for j in range(3):
            whole[j, 0].wait_recv()

        def step(cols):
            part = dot(gtf[...].reshape(256, 256), pb[:, :, :, cols].reshape(256, 256))
            part -= product(0, cols) + product(1, cols) + product(2, cols)
            m[:, :, cols] = part.reshape(8, 32, 256)

        tiles(7, 256, step)

    def finish(part):
        first, count = parts[part]
        whole[3, first].wait_recv()

        def step(cols):
            m[:, :, cols] -= product(3, cols).reshape(8, 32, 256)

        tiles(count, 256, step, first)

    def run(steps):
        for name, j in steps:
            name(j)

    def when(f):
        return (lambda _: f(), 0)

    run([
        (arrive, 0), (arrive_via, 0), (arrive, 1), when(gram_start), (arrive, 2), (gate_up, 0), (arrive_via, 1),
        when(wn_rows), (arrive, 3), (arrive_via, 2), when(gram_0), (activate, 0), (gate_up, 1), (gate_up, 2),
        (wn_send, 2), (down, 0), when(send_proj), (arrive_via, 3), (activate, 1), (core_sum, 0), (wn_send, 3),
        (gate_up, 3), (down, 1), (activate, 2), (core_sum, 1), when(gram_1), (pair_sum, 0), (wn_send, 0),
        (activate, 3), (down, 2), (wn_send, 1), when(swap_proj), (pair_sum, 1), (core_sum, 2), (down, 3), (relay, 0),
        (core_sum, 3), (relay, 1), when(gram_1b), (pair_sum, 2), (far, 0), (pair_sum, 3), when(student_rows),
        (far, 1), (relay, 2), when(gram_2), (relay, 3), (far, 2), when(gram_3), (far, 3), when(student),
    ])

    to_owner = []

    def send_target():
        for j in (1, 2, 3):
            back_z[j].wait_recv()

        def sort_rows(cols):
            blocks = [ob[0, 0, 0, :, cols].astype(F32)] + [ret[j, :, cols].astype(F32) for j in (1, 2, 3)]
            for d in range(4):
                tb[d, :, cols] = jnp.concatenate([b[d * 8:d * 8 + 8] for b in blocks], axis=0).astype(BF)

        tiles(7, 256, sort_rows)
        to_owner.extend([copy_to(tb.at[d], tg.at[d], at(dy=d)) for d in (1, 3, 2)])
        tg[0] = tb[0]

    def mine(d, first, count, cols):
        return m[by_z[d % 8], first:first + count, cols]

    hops = {}
    for step in range(4):
        for half, (start, count) in enumerate(parts):
            cols = pl.ds(start, count * 256)
            if step == 0:
                finish(half)
            for way, sign in ((0, -1), (1, 1)):
                slot = step * 2 + way
                far = sign * (4 - step)
                if step == 0:
                    zs[slot, 0:16, cols] = mine(far, 16 * way, 16, cols).astype(BF)
                    src, dst = zs.at[slot, pl.ds(0, 16), cols], zr.at[slot, pl.ds(0, 16), cols]
                else:
                    hops[step - 1, half, way].wait_recv()
                    if step == 1:
                        first = 16 * way
                        total = mine(far, first, 16, cols) + zr[slot - 2, 0:16, cols].astype(F32)
                        zs[slot, first:first + 16, cols] = total.astype(BF)
                        zs[slot, 16 - first:32 - first, cols] = mine(far, 16 - first, 16, cols).astype(BF)
                    else:
                        zs[slot, :, cols] = (mine(far, 0, 32, cols) + zr[slot - 2, :, cols].astype(F32)).astype(BF)
                    src, dst = zs.at[slot, :, cols], zr.at[slot, :, cols]
                hops[step, half, way] = copy_to(src, dst, at(dz=sign))
        if step == 0:
            send_target()
        if step == 1:
            for copy in started[:-8]:
                copy.wait_send()
            del started[:-8]
        if step == 2:
            for copy in to_owner:
                copy.wait_recv()

            def write_target(cols):
                target[:, cols] = dot_t(weigh[...], tg[:, :, cols].reshape(128, 256)).astype(BF)

            tiles(7, 256, write_target)
            target_out = pltpu.make_async_copy(target, target_hbm, local_sem.at[8])
            target_out.start()
    for half, (start, count) in enumerate(parts):
        cols = pl.ds(start, count * 256)
        total = mine(0, 0, 32, cols)
        for way in range(2):
            hops[3, half, way].wait_recv()
            total += zr[6 + way, :, cols].astype(F32)
        grad[:, cols] = total * (loss_scale / 16384)
    grad_out = pltpu.make_async_copy(grad, grad_hbm, local_sem.at[9])
    grad_out.start()
    for copy in started:
        copy.wait_send()
    target_out.wait()
    grad_out.wait()


N_COPIES = 140


def body(teacher_in, expert_ids, gate_codes, w_gate, w_up, w_down, student_in, projection):
    hbm = pl.BlockSpec(memory_space=pl.ANY)
    return pl.pallas_call(
        kernel,
        out_shape=(
            jax.ShapeDtypeStruct((256, W), BF),
            jax.ShapeDtypeStruct((32, W), F32),
        ),
        in_specs=[hbm] * 8,
        out_specs=(hbm, hbm),
        scratch_shapes=[
            pltpu.VMEM((256, W), BF),
            pltpu.VMEM((32, W), F32),
            pltpu.VMEM((4, 32, W), BF),
            pltpu.VMEM((8, 256), jnp.int32),
            pltpu.VMEM((8, 256), jnp.int32),
            pltpu.VMEM((32, W), BF),
            pltpu.VMEM((256, W), BF),
            pltpu.VMEM((256, 2048), BF),
            pltpu.VMEM((2, W, H), BF),
            pltpu.VMEM((H, W), BF),
            pltpu.VMEM((128, 256), BF),
            pltpu.VMEM((16, 16, W // 2), BF),
            pltpu.VMEM((256, 2048), BF),
            pltpu.VMEM((512, 256), BF),
            pltpu.VMEM((4, 32, 2048), BF),
            pltpu.VMEM((8, 2, 32, 2048), BF),
            pltpu.VMEM((2, 4, 2, 4, 16, W // 2), BF),
            pltpu.VMEM((128, W), BF),
            pltpu.VMEM((4, 2, 4, 32, H), BF),
            pltpu.VMEM((4, 4, 2, 32, H), BF),
            pltpu.VMEM((4, 4, 32, H), BF),
            pltpu.VMEM((4, 2, 32, W), F32),
            pltpu.VMEM((4, 2, 32, W), BF),
            pltpu.VMEM((4, 2, 32, W), BF),
            pltpu.VMEM((4, 32, W), BF),
            pltpu.VMEM((4, 32, W), BF),
            pltpu.VMEM((4, 2, 4, 32, W), BF),
            pltpu.VMEM((4, 32, W), BF),
            pltpu.VMEM((4, 32, W), BF),
            pltpu.VMEM((4, 4, 32, 512), BF),
            pltpu.VMEM((4, 4, 32, 512), BF),
            pltpu.VMEM((2, 4, 32, W), BF),
            pltpu.VMEM((8, 32, 2048), BF),
            pltpu.VMEM((4, 8, 32, 512), BF),
            pltpu.VMEM((4, 8, 32, 512), BF),
            pltpu.VMEM((4, 2, 32, 512), BF),
            pltpu.VMEM((4, 32, 512), BF),
            pltpu.VMEM((4, 32, 512), BF),
            pltpu.VMEM((4, 32, 512), BF),
            pltpu.VMEM((4, 32, 512), BF),
            pltpu.VMEM((8, 2, 32, 128), BF),
            pltpu.VMEM((8, 32, 256), BF),
            pltpu.VMEM((4, 8, 2, 32, 128), BF),
            pltpu.VMEM((4, 8, 32, 256), BF),
            pltpu.VMEM((8, 32, W), F32),
            pltpu.VMEM((8, 32, W), BF),
            pltpu.VMEM((8, 32, W), BF),
            pltpu.SemaphoreType.DMA((N_COPIES,)),
            pltpu.SemaphoreType.DMA((N_COPIES,)),
            pltpu.SemaphoreType.DMA((10,)),
        ],
        compiler_params=pltpu.CompilerParams(
            collective_id=0, has_side_effects=True, vmem_limit_bytes=60 * 1024 * 1024
        ),
        cost_estimate=pl.CostEstimate(flops=8_000_000_000, bytes_accessed=12_000_000, transcendentals=0),
    )(expert_ids.T, gate_codes.T, projection, teacher_in, student_in, w_gate, w_up, w_down)


def solution(mesh):
    in_specs = (
        P("exp", "pair"),
        P("exp", None),
        P("exp", None),
        P("pair", "exp"),
        P("pair", "exp"),
        P("exp", "pair"),
        P("exp", None),
        P("exp", "pair"),
    )
    out_specs = (P("exp", "pair"), P("exp", "pair"))
    return jax.shard_map(body, mesh=mesh, in_specs=in_specs, out_specs=out_specs, check_vma=False)
```

```python
import jax
import jax.numpy as jnp
from jax import lax
from jax.experimental import pallas as pl
from jax.experimental.pallas import tpu as pltpu
from jax.sharding import PartitionSpec as P

CAP = 8
MESH = pl.DeviceIdType.MESH
BF = jnp.bfloat16
F32 = jnp.float32

loss_scale = 128.0
norm_epsilon = 1e-06

W = 1792
H = 512


def dot_t(a, b):
    return lax.dot_general(a, b, (((0,), (0,)), ((), ())), preferred_element_type=F32)


def dot(a, b):
    return jnp.dot(a, b, preferred_element_type=F32)


def tiles(count, size, f, first=0):
    def step(i, carry):
        f(pl.ds(pl.multiple_of(first + i * size, 128), size))
        return carry

    lax.fori_loop(0, count, step, 0)


def kernel(
    ids_hbm, codes_hbm, proj_hbm, teacher_hbm, student_hbm, wg_hbm, wu_hbm, wd_hbm,
    target_hbm, grad_hbm, target, grad, tg, ids, codes, proj, teacher, student_in,
    wgu, wd, weigh, packed, normed, left_x, wn, gx, rows, xk, gu, xr, act, prodf, ps, pr, vs, vr, ob, ret, tb,
    wny, wnb, pb, gxr, gs1, gr1, gs2, gr2, gs3, gr3, gt, gtt, gtf, wkt, wk, m, zs, zr,
    send_sem, recv_sem, local_sem,
):
    e = lax.axis_index("exp")
    x = lax.axis_index("pair")
    y, z, c = e // 16, (e // 2) % 8, e % 2
    sg = 1 - 2 * (z % 2)

    by_y = [lax.rem(y + d, 4) for d in range(4)]
    by_x = [lax.rem(x + d, 4) for d in range(4)]
    by_z = [lax.rem(z + d, 8) for d in range(8)]
    by_hop = {d: lax.rem(z + d * sg + 8, 8) for d in (1, -1, 2, -2, 3, -3)}
    known = {}

    def at(dy=0, dz=0, hop=0, other=False):
        key = dy % 4, dz % 8, hop, other
        if key not in known:
            zz = by_hop[hop] if hop else by_z[dz % 8]
            known[key] = (by_y[dy % 4] * 16 + zz * 2 + (1 - c if other else c), x)
        return known[key]

    def at_x(dx):
        return (e, by_x[dx % 4])

    number = [0, 0]
    started = []

    def new_recv():
        number[1] += 1
        return number[1] - 1

    def new_send():
        number[0] += 1
        return number[0] - 1

    def describe(src, dst, device, send, recv):
        return pltpu.make_async_remote_copy(
            src_ref=src, dst_ref=dst, send_sem=send_sem.at[send], recv_sem=recv_sem.at[recv],
            device_id=device, device_id_type=MESH,
        )

    def copy_to(src, dst, device, recv=None):
        copy = describe(src, dst, device, new_send(), new_recv() if recv is None else recv)
        copy.start()
        started.append(copy)
        return copy

    def group(copies, whole):
        send, recv = new_send(), new_recv()
        for src, dst, device in copies:
            describe(src, dst, device, send, recv).start()
        started.append(describe(whole, whole, at(other=True), send, recv))
        return started[-1]

    def arrival(dst, recv):
        return describe(dst, dst, at(other=True), 0, recv)

    weights = [
        pltpu.make_async_copy(wg_hbm, wgu.at[0], local_sem.at[0]),
        pltpu.make_async_copy(wu_hbm, wgu.at[1], local_sem.at[1]),
        pltpu.make_async_copy(wd_hbm, wd, local_sem.at[2]),
    ]
    operands = [
        pltpu.make_async_copy(src, dst, local_sem.at[3 + i])
        for i, (src, dst) in enumerate((
            (ids_hbm, ids), (codes_hbm, codes), (teacher_hbm, teacher), (student_hbm, student_in), (proj_hbm, proj),
        ))
    ]
    for copy in operands:
        copy.start()

    barrier = pltpu.get_barrier_semaphore()
    peers = [at(dy=dy, dz=dz) for dy in range(4) for dz in (0, 1, -1, 2, -2, 3, -3) if dy or dz]
    peers += [at(dz=4), at(other=True)] + [at_x(d) for d in (1, 2, 3)]
    for peer in peers:
        pl.semaphore_signal(barrier, inc=1, device_id=peer, device_id_type=MESH)

    operands[0].wait()
    operands[1].wait()
    place = lax.broadcasted_iota(jnp.int32, (128, 256), 0)
    hop = (place >> 3) & 3
    shift = jnp.where(hop == 0, 0, jnp.where(hop == 1, -sg, jnp.where(hop == 2, sg, 2)))
    expert = ((y + 4 - (place >> 5)) & 3) * 4 + ((z // 2 + 4 + shift) & 3)
    hit = jnp.zeros((128, 256), F32)
    code = jnp.zeros((128, 256), jnp.int32)
    for k in range(8):
        same = ids[k:k + 1, :] == expert
        hit = jnp.where(same, 1.0, hit)
        code = jnp.where(same, codes[k:k + 1, :], code)
    ahead = lax.broadcasted_iota(jnp.int32, (256, 256), 0) < lax.broadcasted_iota(jnp.int32, (256, 256), 1)
    rank = dot(hit.astype(BF), jnp.where(ahead, 1.0, 0.0).astype(BF))
    chosen = jnp.where(rank == (place & 7).astype(F32), hit, 0.0)
    weigh[...] = (chosen * code.astype(F32) * (1.0 / 256.0)).astype(BF)
    chosen = chosen.astype(BF)

    def pack(cols):
        size = cols.size
        low = dot(chosen, teacher[:, cols]).reshape(16, 8, size)
        high = dot(chosen, teacher[:, pl.ds(pl.multiple_of(896 + cols.start, 128), size)]).reshape(16, 8, size)
        packed[:, :, cols] = jnp.concatenate([low, high], axis=1).astype(BF)

    operands[2].wait()
    tiles(3, 256, pack)
    tiles(1, 128, pack, 768)
    pl.semaphore_wait(barrier, len(peers))

    out_hop = (0, -1, 2, -3)
    direct, via, over = {}, {}, {}
    first, second = new_send(), new_send()
    for j in (0, 1, 2, 3):
        direct[j] = new_recv()
        for d in (1, 3, 2, 0):
            if j or d:
                describe(
                    packed.at[d * 4 + j], rows.at[0, j, 0, d], at(dy=-d, hop=out_hop[j]), first, direct[j]
                ).start()
        if j == 0:
            via[0] = new_recv()
            for d in (0, 1, 3, 2):
                describe(packed.at[d * 4], rows.at[1, 0, 0, d], at(dy=-d, hop=1), second, via[0]).start()
    started.append(describe(packed.at[pl.ds(0, 15)], packed.at[pl.ds(0, 15)], at(other=True), first, direct[0]))
    started.append(describe(packed.at[pl.ds(0, 4)], packed.at[pl.ds(0, 4)], at(other=True), second, via[0]))
    rows[0, 0, 0, 0] = packed[0]
    for copy in weights:
        copy.start()

    operands[3].wait()
    wide = student_in[...].astype(F32)
    scale = 1.0 / jnp.sqrt(jnp.mean(wide * wide, axis=1, keepdims=True) + norm_epsilon)
    normed[...] = (wide * scale).astype(BF)
    left_x[...] = normed[:, pl.ds(pl.multiple_of(x * 512, 512), 512)].astype(F32).T.astype(BF)

    def early(cols):
        gx[:, :, :, cols] = dot(left_x[...], normed[:, cols]).reshape(8, 2, 32, 256).astype(BF)

    def early_rows(cols):
        out = dot(weigh[...], normed[:, cols]).reshape(4, 4, 8, 256)
        for j in range(4):
            wn[j, :, cols] = jnp.concatenate([out[d, j] for d in range(4)], axis=0).astype(BF)

    gram = {}

    def gram_start():
        tiles(8, 256, early)
        gram["core"] = copy_to(gx.at[:, 1 - c], gxr, at(other=True))

    def gram_0():
        gram["core"].wait_recv()
        for q in range(4):
            cols = slice(q * 512, q * 512 + 512)
            gs1[q] = (gx[:, c, :, cols].astype(F32) + gxr[:, :, cols].astype(F32)).astype(BF)
        gram["y"] = group([(gs1.at[by_y[d]], gr1.at[d], at(dy=d)) for d in (1, 3, 2)], gr1.at[pl.ds(1, 3)])

    def gram_1():
        gram["y"].wait_recv()
        total = gs1[y].astype(F32) + sum(gr1[d].astype(F32) for d in (1, 2, 3))
        gs2[...] = total.astype(BF).reshape(4, 2, 32, 512)
        gram["pair"] = copy_to(gs2.at[:, 1 - z % 2], gr2, at(hop=1))

    def gram_1b():
        gram["pair"].wait_recv()
        gs3[...] = (gs2[:, z % 2].astype(F32) + gr2[...].astype(F32)).astype(BF)
        gram["z"] = group(
            [(gs3.at[by_z[d] // 2], gr3.at[d // 2], at(dz=d)) for d in (2, 6, 4)], gr3.at[pl.ds(1, 3)]
        )

    def gram_2():
        gram["z"].wait_recv()
        total = gs3[z // 2].astype(F32) + sum(gr3[d].astype(F32) for d in range(1, 4))
        gt[x] = total.astype(BF)
        gram["x"] = group([(gt.at[x], gt.at[x], at_x(d)) for d in (1, 3, 2)], gt.at[pl.ds(0, 3)])

    early_y, swap = [], []

    def send_proj():
        operands[4].wait()
        early_y.append(group([(proj, pb.at[0, y], at(dy=d)) for d in (1, 3, 2)], pb.at[0, pl.ds(0, 3)]))
        pb[0, y] = proj[...]

    wn_y, wn_z = [], {}

    def wn_rows():
        tiles(8, 256, early_rows)

        def features(yy):
            return pl.ds(pl.multiple_of(yy * 512, 512), 512)

        wn_y.append(group(
            [(wn.at[:, :, features(by_y[4 - d])], wny.at[d], at(dy=-d)) for d in (1, 3, 2)], wny.at[pl.ds(1, 3)]
        ))
        wny[0] = wn[:, :, features(y)]

    def wn_send(j):
        while wn_y:
            wn_y.pop().wait_recv()
        if j:
            wn_z[j] = copy_to(wny.at[:, j], wnb.at[j], at(hop=out_hop[j]))

    def swap_proj():
        for copy in early_y:
            copy.wait_recv()
        swap.append(copy_to(pb.at[0], pb.at[1], at(other=True)))

    other_k = pl.ds(128, 128)

    def student_rows():
        for j in range(4):
            if j:
                wn_z[j].wait_recv()
            blocks = [(wnb[j, d] if j else wny[d, 0]).astype(F32) for d in range(4)]
            order = [blocks[(d + 4 - g) % 4][d * 8:d * 8 + 8] for g in range(4) for d in range(4)]
            wkt[j] = jnp.concatenate(order, axis=0).T.reshape(8, 2, 32, 128).astype(BF)
            wk[j, :, :, 0:128] = wkt[j, :, c]
        swap.append(copy_to(wkt.at[:, :, 1 - c], wk.at[:, :, :, other_k], at(other=True)))

    def gram_3():
        gram["x"].wait_recv()
        gtt[...] = gt[...].reshape(128, 512).astype(F32).T.reshape(8, 2, 32, 128).astype(BF)
        gtf[:, :, 0:128] = gtt[:, c]
        swap.append(copy_to(gtt.at[:, 1 - c], gtf.at[:, :, other_k], at(other=True)))

    to_x, act_x, back_core, back_pair, back_z, round_y, far_y, whole = {}, {}, {}, {}, {}, {}, {}, {}
    parts = ((0, 4), (1024, 3))

    def spans(j):
        return parts if j == 3 else ((0, 7),)

    def arrive(j):
        into = rows.at[0, 0, 0, pl.ds(1, 3)] if j == 0 else rows.at[0, j, 0]
        arrival(into, direct[j]).wait_recv()
        if j:
            via[j] = new_recv()
            copy_to(rows.at[0, j, 0], rows.at[1, j, 0], at(hop=1), via[j])

    def arrive_via(j):
        arrival(rows.at[1, j, 0], via[j]).wait_recv()
        over[j] = copy_to(rows.at[:, j, 0], rows.at[:, j, 1], at(other=True))

    def gate_up(j):
        over[j].wait_recv()

        def unfold(cols):
            block = rows[:, j, :, :, :, cols].astype(F32).reshape(16, 2, 8, 128)
            xk[:, cols] = block[:, 0].reshape(128, 128).astype(BF)
            xk[:, pl.ds(pl.multiple_of(896 + cols.start, 128), 128)] = block[:, 1].reshape(128, 128).astype(BF)

        tiles(7, 128, unfold)
        if j == 0:
            weights[0].wait()
            weights[1].wait()
        for part in range(2):
            gu[j, part] = dot(xk[...], wgu[part]).reshape(4, 32, H).astype(BF)
        to_x[j] = group([(gu.at[j, :, by_x[d]], xr.at[j, d], at_x(d)) for d in (1, 3, 2)], xr.at[j, pl.ds(1, 3)])

    def activate(j):
        to_x[j].wait_recv()
        gate, up = [
            gu[j, part, x].astype(F32) + sum(xr[j, d, part].astype(F32) for d in (1, 2, 3)) for part in range(2)
        ]
        act[j, x] = (gate / (1.0 + jnp.exp(-gate)) * up).astype(BF)
        act_x[j] = group([(act.at[j, x], act.at[j, x], at_x(d)) for d in (1, 3, 2)], act.at[j, pl.ds(0, 3)])

    def down(j):
        act_x[j].wait_recv()
        if j == 0:
            weights[2].wait()

        def step(cols):
            out = dot(act[j].reshape(128, H), wd[:, cols]).reshape(4, 32, 256)
            for i in range(2):
                prodf[j, i, :, cols] = out[2 * i]
                ps[j, i, :, cols] = out[2 * i + 1].astype(BF)

        for first, count in spans(j):
            tiles(count, 256, step, first)
            cols = pl.ds(first, count * 256)
            back_core[j, first] = copy_to(ps.at[j, :, :, cols], pr.at[j, :, :, cols], at(other=True))

    def core_sum(j):
        def step(cols):
            vs[j, :, cols] = (prodf[j, 1, :, cols] + pr[j, 1, :, cols].astype(F32)).astype(BF)

        for first, count in spans(j):
            back_core[j, first].wait_recv()
            tiles(count, 256, step, first)
            cols = pl.ds(first, count * 256)
            back_pair[j, first] = copy_to(vs.at[j, :, cols], vr.at[j, :, cols], at(hop=1))

    def pair_sum(j):
        def step(cols):
            ob[j, 0, 0, :, cols] = (
                prodf[j, 0, :, cols] + pr[j, 0, :, cols].astype(F32) + vr[j, :, cols].astype(F32)
            ).astype(BF)

        for first, count in spans(j):
            back_pair[j, first].wait_recv()
            tiles(count, 256, step, first)
            cols = pl.ds(first, count * 256)
            round_y[j, first] = [
                copy_to(ob.at[j, 0, 0, :, cols], ob.at[j, 0, g, :, cols], at(dy=g)) for g in (1, 3)
            ]
        if j:
            back_z[j] = copy_to(ob.at[j, 0, 0], ret.at[j], at(hop=-j))

    def relay(j):
        low, high = pl.ds(0, 16), pl.ds(16, 16)
        for first, count in spans(j):
            cols = pl.ds(first, count * 256)
            far_y[j, first] = []
            for side, (g, rows_g, dy) in enumerate(((1, low, 1), (3, high, -1))):
                round_y[j, first][side].wait_recv()
                far_y[j, first].append(
                    copy_to(ob.at[j, 0, g, rows_g, cols], ob.at[j, 0, 2, rows_g, cols], at(dy=dy))
                )

    def far(j):
        for first, count in spans(j):
            for copy in far_y[j, first]:
                copy.wait_recv()
            cols = pl.ds(first, count * 256)
            whole[j, first] = copy_to(ob.at[j, 0, :, :, cols], ob.at[j, 1, :, :, cols], at(other=True))

    def product(j, cols):
        return dot(wk[j].reshape(256, 256), ob[j, :, :, :, cols].reshape(256, 256))

    def student():
        for copy in swap:
            copy.wait_recv()
        for j in range(3):
            whole[j, 0].wait_recv()

        def step(cols):
            part = dot(gtf[...].reshape(256, 256), pb[:, :, :, cols].reshape(256, 256))
            part -= product(0, cols) + product(1, cols) + product(2, cols)
            m[:, :, cols] = part.reshape(8, 32, 256)

        tiles(7, 256, step)

    def finish(part):
        first, count = parts[part]
        whole[3, first].wait_recv()

        def step(cols):
            m[:, :, cols] -= product(3, cols).reshape(8, 32, 256)

        tiles(count, 256, step, first)

    def run(steps):
        for name, j in steps:
            name(j)

    def when(f):
        return (lambda _: f(), 0)

    run([
        (arrive, 0), (arrive_via, 0), (arrive, 1), when(gram_start), (arrive, 2), (gate_up, 0), (arrive_via, 1),
        when(wn_rows), (arrive, 3), (arrive_via, 2), when(gram_0), (activate, 0), (gate_up, 1), (gate_up, 2),
        (wn_send, 2), (down, 0), when(send_proj), (arrive_via, 3), (activate, 1), (core_sum, 0), (wn_send, 3),
        (gate_up, 3), (down, 1), (activate, 2), (core_sum, 1), when(gram_1), (pair_sum, 0), (wn_send, 0),
        (activate, 3), (down, 2), (wn_send, 1), when(swap_proj), (pair_sum, 1), (core_sum, 2), (down, 3), (relay, 0),
        (core_sum, 3), (relay, 1), when(gram_1b), (pair_sum, 2), (far, 0), (pair_sum, 3), when(student_rows),
        (far, 1), (relay, 2), when(gram_2), (relay, 3), (far, 2), when(gram_3), (far, 3), when(student),
    ])

    to_owner = []

    def send_target():
        for j in (1, 2, 3):
            back_z[j].wait_recv()

        def sort_rows(cols):
            blocks = [ob[0, 0, 0, :, cols].astype(F32)] + [ret[j, :, cols].astype(F32) for j in (1, 2, 3)]
            for d in range(4):
                tb[d, :, cols] = jnp.concatenate([b[d * 8:d * 8 + 8] for b in blocks], axis=0).astype(BF)

        tiles(7, 256, sort_rows)
        to_owner.append(group([(tb.at[d], tg.at[d], at(dy=d)) for d in (1, 3, 2)], tg.at[pl.ds(1, 3)]))
        tg[0] = tb[0]

    def mine(d, first, count, cols):
        return m[by_z[d % 8], first:first + count, cols]

    hops = {}
    for step in range(4):
        for half, (start, count) in enumerate(parts):
            cols = pl.ds(start, count * 256)
            if step == 0:
                finish(half)
            for way, sign in ((0, -1), (1, 1)):
                slot = step * 2 + way
                far = sign * (4 - step)
                if step == 0:
                    zs[slot, 0:16, cols] = mine(far, 16 * way, 16, cols).astype(BF)
                    src, dst = zs.at[slot, pl.ds(0, 16), cols], zr.at[slot, pl.ds(0, 16), cols]
                else:
                    hops[step - 1, half, way].wait_recv()
                    if step == 1:
                        first = 16 * way
                        total = mine(far, first, 16, cols) + zr[slot - 2, 0:16, cols].astype(F32)
                        zs[slot, first:first + 16, cols] = total.astype(BF)
                        zs[slot, 16 - first:32 - first, cols] = mine(far, 16 - first, 16, cols).astype(BF)
                    else:
                        zs[slot, :, cols] = (mine(far, 0, 32, cols) + zr[slot - 2, :, cols].astype(F32)).astype(BF)
                    src, dst = zs.at[slot, :, cols], zr.at[slot, :, cols]
                hops[step, half, way] = copy_to(src, dst, at(dz=sign))
        if step == 0:
            send_target()
        if step == 1:
            for copy in started[:-6]:
                copy.wait_send()
            del started[:-6]
        if step == 2:
            for copy in to_owner:
                copy.wait_recv()

            def write_target(cols):
                target[:, cols] = dot_t(weigh[...], tg[:, :, cols].reshape(128, 256)).astype(BF)

            tiles(7, 256, write_target)
            target_out = pltpu.make_async_copy(target, target_hbm, local_sem.at[8])
            target_out.start()
    for half, (start, count) in enumerate(parts):
        cols = pl.ds(start, count * 256)
        total = mine(0, 0, 32, cols)
        for way in range(2):
            hops[3, half, way].wait_recv()
            total += zr[6 + way, :, cols].astype(F32)
        grad[:, cols] = total * (loss_scale / 16384)
    grad_out = pltpu.make_async_copy(grad, grad_hbm, local_sem.at[9])
    grad_out.start()
    for copy in started:
        copy.wait_send()
    target_out.wait()
    grad_out.wait()


N_COPIES = 140


def body(teacher_in, expert_ids, gate_codes, w_gate, w_up, w_down, student_in, projection):
    hbm = pl.BlockSpec(memory_space=pl.ANY)
    return pl.pallas_call(
        kernel,
        out_shape=(
            jax.ShapeDtypeStruct((256, W), BF),
            jax.ShapeDtypeStruct((32, W), F32),
        ),
        in_specs=[hbm] * 8,
        out_specs=(hbm, hbm),
        scratch_shapes=[
            pltpu.VMEM((256, W), BF),
            pltpu.VMEM((32, W), F32),
            pltpu.VMEM((4, 32, W), BF),
            pltpu.VMEM((8, 256), jnp.int32),
            pltpu.VMEM((8, 256), jnp.int32),
            pltpu.VMEM((32, W), BF),
            pltpu.VMEM((256, W), BF),
            pltpu.VMEM((256, 2048), BF),
            pltpu.VMEM((2, W, H), BF),
            pltpu.VMEM((H, W), BF),
            pltpu.VMEM((128, 256), BF),
            pltpu.VMEM((16, 16, W // 2), BF),
            pltpu.VMEM((256, 2048), BF),
            pltpu.VMEM((512, 256), BF),
            pltpu.VMEM((4, 32, 2048), BF),
            pltpu.VMEM((8, 2, 32, 2048), BF),
            pltpu.VMEM((2, 4, 2, 4, 16, W // 2), BF),
            pltpu.VMEM((128, W), BF),
            pltpu.VMEM((4, 2, 4, 32, H), BF),
            pltpu.VMEM((4, 4, 2, 32, H), BF),
            pltpu.VMEM((4, 4, 32, H), BF),
            pltpu.VMEM((4, 2, 32, W), F32),
            pltpu.VMEM((4, 2, 32, W), BF),
            pltpu.VMEM((4, 2, 32, W), BF),
            pltpu.VMEM((4, 32, W), BF),
            pltpu.VMEM((4, 32, W), BF),
            pltpu.VMEM((4, 2, 4, 32, W), BF),
            pltpu.VMEM((4, 32, W), BF),
            pltpu.VMEM((4, 32, W), BF),
            pltpu.VMEM((4, 4, 32, 512), BF),
            pltpu.VMEM((4, 4, 32, 512), BF),
            pltpu.VMEM((2, 4, 32, W), BF),
            pltpu.VMEM((8, 32, 2048), BF),
            pltpu.VMEM((4, 8, 32, 512), BF),
            pltpu.VMEM((4, 8, 32, 512), BF),
            pltpu.VMEM((4, 2, 32, 512), BF),
            pltpu.VMEM((4, 32, 512), BF),
            pltpu.VMEM((4, 32, 512), BF),
            pltpu.VMEM((4, 32, 512), BF),
            pltpu.VMEM((4, 32, 512), BF),
            pltpu.VMEM((8, 2, 32, 128), BF),
            pltpu.VMEM((8, 32, 256), BF),
            pltpu.VMEM((4, 8, 2, 32, 128), BF),
            pltpu.VMEM((4, 8, 32, 256), BF),
            pltpu.VMEM((8, 32, W), F32),
            pltpu.VMEM((8, 32, W), BF),
            pltpu.VMEM((8, 32, W), BF),
            pltpu.SemaphoreType.DMA((N_COPIES,)),
            pltpu.SemaphoreType.DMA((N_COPIES,)),
            pltpu.SemaphoreType.DMA((10,)),
        ],
        compiler_params=pltpu.CompilerParams(
            collective_id=0, has_side_effects=True, vmem_limit_bytes=60 * 1024 * 1024
        ),
        cost_estimate=pl.CostEstimate(flops=8_000_000_000, bytes_accessed=12_000_000, transcendentals=0),
    )(expert_ids.T, gate_codes.T, projection, teacher_in, student_in, w_gate, w_up, w_down)


def solution(mesh):
    in_specs = (
        P("exp", "pair"),
        P("exp", None),
        P("exp", None),
        P("pair", "exp"),
        P("pair", "exp"),
        P("exp", "pair"),
        P("exp", None),
        P("exp", "pair"),
    )
    out_specs = (P("exp", "pair"), P("exp", "pair"))
    return jax.shard_map(body, mesh=mesh, in_specs=in_specs, out_specs=out_specs, check_vma=False)
```

```python
import jax
import jax.numpy as jnp
from jax import lax
from jax.experimental import pallas as pl
from jax.experimental.pallas import tpu as pltpu
from jax.sharding import PartitionSpec as P

CAP = 8
MESH = pl.DeviceIdType.MESH
BF = jnp.bfloat16
F32 = jnp.float32

loss_scale = 128.0
norm_epsilon = 1e-06

W = 1792
H = 512


def dot_t(a, b):
    return lax.dot_general(a, b, (((0,), (0,)), ((), ())), preferred_element_type=F32)


def dot(a, b):
    return jnp.dot(a, b, preferred_element_type=F32)


def tiles(count, size, f, first=0):
    for i in range(count):
        f(pl.ds(first + i * size, size))


def kernel(
    ids_hbm, codes_hbm, proj_hbm, teacher_hbm, student_hbm, wg_hbm, wu_hbm, wd_hbm,
    target_hbm, grad_hbm, target, grad, tg, ids, codes, proj, teacher, student_in,
    wgu, wd, weigh, packed, normed, left_x, wn, gx, rows, xk, gu, xr, act, prodf, ps, pr, vs, vr, ob, ret, tb,
    wny, wnb, pb, gxr, gs1, gr1, gs2, gr2, gs3, gr3, gt, gtt, gtf, wkt, wk, m, zs, zr,
    send_sem, recv_sem, local_sem,
):
    e = lax.axis_index("exp")
    x = lax.axis_index("pair")
    y, z, c = e // 16, (e // 2) % 8, e % 2
    sg = 1 - 2 * (z % 2)

    by_y = [lax.rem(y + d, 4) for d in range(4)]
    by_x = [lax.rem(x + d, 4) for d in range(4)]
    by_z = [lax.rem(z + d, 8) for d in range(8)]
    by_hop = {d: lax.rem(z + d * sg + 8, 8) for d in (1, -1, 2, -2, 3, -3)}
    known = {}

    def at(dy=0, dz=0, hop=0, other=False):
        key = dy % 4, dz % 8, hop, other
        if key not in known:
            zz = by_hop[hop] if hop else by_z[dz % 8]
            known[key] = (by_y[dy % 4] * 16 + zz * 2 + (1 - c if other else c), x)
        return known[key]

    def at_x(dx):
        return (e, by_x[dx % 4])

    number = [0, 0]
    started = []

    def new_recv():
        number[1] += 1
        return number[1] - 1

    def new_send():
        number[0] += 1
        return number[0] - 1

    def describe(src, dst, device, send, recv):
        return pltpu.make_async_remote_copy(
            src_ref=src, dst_ref=dst, send_sem=send_sem.at[send], recv_sem=recv_sem.at[recv],
            device_id=device, device_id_type=MESH,
        )

    def copy_to(src, dst, device, recv=None):
        copy = describe(src, dst, device, new_send(), new_recv() if recv is None else recv)
        copy.start()
        started.append(copy)
        return copy

    def group(copies, whole):
        send, recv = new_send(), new_recv()
        for src, dst, device in copies:
            describe(src, dst, device, send, recv).start()
        started.append(describe(whole, whole, at(other=True), send, recv))
        return started[-1]

    def arrival(dst, recv):
        return describe(dst, dst, at(other=True), 0, recv)

    weights = [
        pltpu.make_async_copy(wg_hbm, wgu.at[:, pl.ds(0, H)], local_sem.at[0]),
        pltpu.make_async_copy(wu_hbm, wgu.at[:, pl.ds(H, H)], local_sem.at[1]),
        pltpu.make_async_copy(wd_hbm, wd, local_sem.at[2]),
    ]
    operands = [
        pltpu.make_async_copy(src, dst, local_sem.at[3 + i])
        for i, (src, dst) in enumerate((
            (ids_hbm, ids), (codes_hbm, codes), (teacher_hbm, teacher), (student_hbm, student_in), (proj_hbm, proj),
        ))
    ]
    for copy in operands:
        copy.start()

    barrier = pltpu.get_barrier_semaphore()
    peers = [at(dy=dy, dz=dz) for dy in range(4) for dz in (0, 1, -1, 2, -2, 3, -3) if dy or dz]
    peers += [at(dz=4), at(other=True)] + [at_x(d) for d in (1, 2, 3)]
    for peer in peers:
        pl.semaphore_signal(barrier, inc=1, device_id=peer, device_id_type=MESH)

    operands[0].wait()
    operands[1].wait()
    place = lax.broadcasted_iota(jnp.int32, (128, 256), 0)
    hop = (place >> 3) & 3
    shift = jnp.where(hop == 0, 0, jnp.where(hop == 1, -sg, jnp.where(hop == 2, sg, 2)))
    expert = ((y + 4 - (place >> 5)) & 3) * 4 + ((z // 2 + 4 + shift) & 3)
    hit = jnp.zeros((128, 256), F32)
    code = jnp.zeros((128, 256), jnp.int32)
    for k in range(8):
        same = ids[k:k + 1, :] == expert
        hit = jnp.where(same, 1.0, hit)
        code = jnp.where(same, codes[k:k + 1, :], code)
    ahead = lax.broadcasted_iota(jnp.int32, (256, 256), 0) < lax.broadcasted_iota(jnp.int32, (256, 256), 1)
    rank = dot(hit.astype(BF), jnp.where(ahead, 1.0, 0.0).astype(BF))
    chosen = jnp.where(rank == (place & 7).astype(F32), hit, 0.0)
    weigh[...] = (chosen * code.astype(F32) * (1.0 / 256.0)).astype(BF)
    chosen = chosen.astype(BF)

    def pack(cols):
        size = cols.size
        low = dot(chosen, teacher[:, cols]).reshape(16, 8, size)
        high = dot(chosen, teacher[:, pl.ds(896 + cols.start, size)]).reshape(16, 8, size)
        packed[:, :, cols] = jnp.concatenate([low, high], axis=1).astype(BF)

    operands[2].wait()
    tiles(3, 256, pack)
    tiles(1, 128, pack, 768)
    pl.semaphore_wait(barrier, len(peers))

    out_hop = (0, -1, 2, -3)
    direct, via, over = {}, {}, {}
    first, second = new_send(), new_send()
    for j in (0, 1, 2, 3):
        direct[j] = new_recv()
        for d in (1, 3, 2, 0):
            if j or d:
                describe(
                    packed.at[d * 4 + j], rows.at[0, j, 0, d], at(dy=-d, hop=out_hop[j]), first, direct[j]
                ).start()
        if j == 0:
            via[0] = new_recv()
            for d in (0, 1, 3, 2):
                describe(packed.at[d * 4], rows.at[1, 0, 0, d], at(dy=-d, hop=1), second, via[0]).start()
    started.append(describe(packed.at[pl.ds(0, 15)], packed.at[pl.ds(0, 15)], at(other=True), first, direct[0]))
    started.append(describe(packed.at[pl.ds(0, 4)], packed.at[pl.ds(0, 4)], at(other=True), second, via[0]))
    rows[0, 0, 0, 0] = packed[0]
    for copy in weights:
        copy.start()

    operands[3].wait()
    wide = student_in[...].astype(F32)
    scale = 1.0 / jnp.sqrt(jnp.mean(wide * wide, axis=1, keepdims=True) + norm_epsilon)
    normed[...] = (wide * scale).astype(BF)
    left_x[...] = normed[:, pl.ds(pl.multiple_of(x * 512, 512), 512)].astype(F32).T.astype(BF)

    def early(cols):
        gx[:, :, :, cols] = dot(left_x[...], normed[:, cols]).reshape(8, 2, 32, 256).astype(BF)

    def early_rows(cols):
        out = dot(weigh[...], normed[:, cols]).reshape(4, 4, 8, 256)
        for j in range(4):
            wn[j, :, cols] = jnp.concatenate([out[d, j] for d in range(4)], axis=0).astype(BF)

    gram = {}

    def gram_start():
        tiles(8, 256, early)
        gram["core"] = copy_to(gx.at[:, 1 - c], gxr, at(other=True))

    def gram_0():
        gram["core"].wait_recv()
        for q in range(4):
            cols = slice(q * 512, q * 512 + 512)
            gs1[q] = (gx[:, c, :, cols].astype(F32) + gxr[:, :, cols].astype(F32)).astype(BF)
        gram["y"] = group([(gs1.at[by_y[d]], gr1.at[d], at(dy=d)) for d in (1, 3, 2)], gr1.at[pl.ds(1, 3)])

    def gram_1():
        gram["y"].wait_recv()
        total = gs1[y].astype(F32) + sum(gr1[d].astype(F32) for d in (1, 2, 3))
        gs2[...] = total.astype(BF).reshape(4, 2, 32, 512)
        gram["pair"] = copy_to(gs2.at[:, 1 - z % 2], gr2, at(hop=1))

    def gram_1b():
        gram["pair"].wait_recv()
        gs3[...] = (gs2[:, z % 2].astype(F32) + gr2[...].astype(F32)).astype(BF)
        gram["z"] = group(
            [(gs3.at[by_z[d] // 2], gr3.at[d // 2], at(dz=d)) for d in (2, 6, 4)], gr3.at[pl.ds(1, 3)]
        )

    def gram_2():
        gram["z"].wait_recv()
        total = gs3[z // 2].astype(F32) + sum(gr3[d].astype(F32) for d in range(1, 4))
        gt[x] = total.astype(BF)
        gram["x"] = group([(gt.at[x], gt.at[x], at_x(d)) for d in (1, 3, 2)], gt.at[pl.ds(0, 3)])

    early_y, swap = [], []

    def send_proj():
        operands[4].wait()
        early_y.append(group([(proj, pb.at[0, y], at(dy=d)) for d in (1, 3, 2)], pb.at[0, pl.ds(0, 3)]))
        pb[0, y] = proj[...]

    wn_y, wn_z = [], {}

    def wn_rows():
        tiles(8, 256, early_rows)

        def features(yy):
            return pl.ds(pl.multiple_of(yy * 512, 512), 512)

        wn_y.append(group(
            [(wn.at[:, :, features(by_y[4 - d])], wny.at[d], at(dy=-d)) for d in (1, 3, 2)], wny.at[pl.ds(1, 3)]
        ))
        wny[0] = wn[:, :, features(y)]

    def wn_send(j):
        while wn_y:
            wn_y.pop().wait_recv()
        if j:
            wn_z[j] = copy_to(wny.at[:, j], wnb.at[j], at(hop=out_hop[j]))

    def swap_proj():
        for copy in early_y:
            copy.wait_recv()
        swap.append(copy_to(pb.at[0], pb.at[1], at(other=True)))

    other_k = pl.ds(128, 128)

    def student_rows():
        for j in range(4):
            if j:
                wn_z[j].wait_recv()
            blocks = [(wnb[j, d] if j else wny[d, 0]).astype(F32) for d in range(4)]
            order = [blocks[(d + 4 - g) % 4][d * 8:d * 8 + 8] for g in range(4) for d in range(4)]
            wkt[j] = jnp.concatenate(order, axis=0).T.reshape(8, 2, 32, 128).astype(BF)
            wk[j, :, :, 0:128] = wkt[j, :, c]
        swap.append(copy_to(wkt.at[:, :, 1 - c], wk.at[:, :, :, other_k], at(other=True)))

    def gram_3():
        gram["x"].wait_recv()
        gtt[...] = gt[...].reshape(128, 512).astype(F32).T.reshape(8, 2, 32, 128).astype(BF)
        gtf[:, :, 0:128] = gtt[:, c]
        swap.append(copy_to(gtt.at[:, 1 - c], gtf.at[:, :, other_k], at(other=True)))

    to_x, act_x, back_core, back_pair, back_z, round_y, far_y, whole = {}, {}, {}, {}, {}, {}, {}, {}
    parts = ((0, 4), (1024, 3))

    def spans(j):
        return parts if j == 3 else ((0, 7),)

    def arrive(j):
        into = rows.at[0, 0, 0, pl.ds(1, 3)] if j == 0 else rows.at[0, j, 0]
        arrival(into, direct[j]).wait_recv()
        if j:
            via[j] = new_recv()
            copy_to(rows.at[0, j, 0], rows.at[1, j, 0], at(hop=1), via[j])

    def arrive_via(j):
        arrival(rows.at[1, j, 0], via[j]).wait_recv()
        over[j] = copy_to(rows.at[:, j, 0], rows.at[:, j, 1], at(other=True))

    def gate_up(j):
        over[j].wait_recv()

        def unfold(cols):
            block = rows[:, j, :, :, :, cols].astype(F32).reshape(16, 2, 8, 128)
            xk[:, cols] = block[:, 0].reshape(128, 128).astype(BF)
            xk[:, pl.ds(896 + cols.start, 128)] = block[:, 1].reshape(128, 128).astype(BF)

        tiles(7, 128, unfold)
        if j == 0:
            weights[0].wait()
            weights[1].wait()
        gu[j] = dot(xk[...], wgu[...]).reshape(4, 32, 2 * H).astype(BF)
        to_x[j] = group([(gu.at[j, by_x[d]], xr.at[j, d], at_x(d)) for d in (1, 3, 2)], xr.at[j, pl.ds(1, 3)])

    def activate(j):
        to_x[j].wait_recv()
        total = gu[j, x].astype(F32) + sum(xr[j, d].astype(F32) for d in (1, 2, 3))
        gate, up = total[:, :H], total[:, H:]
        act[j, x] = (gate / (1.0 + jnp.exp(-gate)) * up).astype(BF)
        act_x[j] = group([(act.at[j, x], act.at[j, x], at_x(d)) for d in (1, 3, 2)], act.at[j, pl.ds(0, 3)])

    def down(j):
        act_x[j].wait_recv()
        if j == 0:
            weights[2].wait()

        def step(cols):
            out = dot(act[j].reshape(128, H), wd[:, cols]).reshape(4, 32, 256)
            for i in range(2):
                prodf[j, i, :, cols] = out[2 * i]
                ps[j, i, :, cols] = out[2 * i + 1].astype(BF)

        for first, count in spans(j):
            tiles(count, 256, step, first)
            cols = pl.ds(first, count * 256)
            back_core[j, first] = copy_to(ps.at[j, :, :, cols], pr.at[j, :, :, cols], at(other=True))

    def core_sum(j):
        def step(cols):
            vs[j, :, cols] = (prodf[j, 1, :, cols] + pr[j, 1, :, cols].astype(F32)).astype(BF)

        for first, count in spans(j):
            back_core[j, first].wait_recv()
            tiles(count, 256, step, first)
            cols = pl.ds(first, count * 256)
            back_pair[j, first] = copy_to(vs.at[j, :, cols], vr.at[j, :, cols], at(hop=1))

    def pair_sum(j):
        def step(cols):
            ob[j, 0, 0, :, cols] = (
                prodf[j, 0, :, cols] + pr[j, 0, :, cols].astype(F32) + vr[j, :, cols].astype(F32)
            ).astype(BF)

        for first, count in spans(j):
            back_pair[j, first].wait_recv()
            tiles(count, 256, step, first)
            cols = pl.ds(first, count * 256)
            round_y[j, first] = [
                copy_to(ob.at[j, 0, 0, :, cols], ob.at[j, 0, g, :, cols], at(dy=g)) for g in (1, 3)
            ]
        if j:
            back_z[j] = copy_to(ob.at[j, 0, 0], ret.at[j], at(hop=-j))

    def relay(j):
        low, high = pl.ds(0, 16), pl.ds(16, 16)
        for first, count in spans(j):
            cols = pl.ds(first, count * 256)
            far_y[j, first] = []
            for side, (g, rows_g, dy) in enumerate(((1, low, 1), (3, high, -1))):
                round_y[j, first][side].wait_recv()
                far_y[j, first].append(
                    copy_to(ob.at[j, 0, g, rows_g, cols], ob.at[j, 0, 2, rows_g, cols], at(dy=dy))
                )

    def far(j):
        for first, count in spans(j):
            for copy in far_y[j, first]:
                copy.wait_recv()
            cols = pl.ds(first, count * 256)
            whole[j, first] = copy_to(ob.at[j, 0, :, :, cols], ob.at[j, 1, :, :, cols], at(other=True))

    def product(j, cols):
        return dot(wk[j].reshape(256, 256), ob[j, :, :, :, cols].reshape(256, 256))

    def student():
        for copy in swap:
            copy.wait_recv()
        for j in range(3):
            whole[j, 0].wait_recv()

        def step(cols):
            part = dot(gtf[...].reshape(256, 256), pb[:, :, :, cols].reshape(256, 256))
            part -= product(0, cols) + product(1, cols) + product(2, cols)
            m[:, :, cols] = part.reshape(8, 32, 256)

        tiles(7, 256, step)

    def finish(part):
        first, count = parts[part]
        whole[3, first].wait_recv()

        def step(cols):
            m[:, :, cols] -= product(3, cols).reshape(8, 32, 256)

        tiles(count, 256, step, first)

    def run(steps):
        for name, j in steps:
            name(j)

    def when(f):
        return (lambda _: f(), 0)

    run([
        (arrive, 0), (arrive_via, 0), (arrive, 1), when(gram_start), (arrive, 2), (gate_up, 0), (arrive_via, 1),
        when(wn_rows), (arrive, 3), (arrive_via, 2), when(gram_0), (activate, 0), (gate_up, 1), (gate_up, 2),
        (wn_send, 2), (down, 0), when(send_proj), (arrive_via, 3), (activate, 1), (core_sum, 0), (wn_send, 3),
        (gate_up, 3), (down, 1), (activate, 2), (core_sum, 1), when(gram_1), (pair_sum, 0), (wn_send, 0),
        (activate, 3), (down, 2), (wn_send, 1), when(swap_proj), (pair_sum, 1), (core_sum, 2), (down, 3), (relay, 0),
        (core_sum, 3), (relay, 1), when(gram_1b), (pair_sum, 2), (far, 0), (pair_sum, 3), when(student_rows),
        (far, 1), (relay, 2), when(gram_2), (relay, 3), (far, 2), when(gram_3), (far, 3), when(student),
    ])

    to_owner = []

    def send_target():
        for j in (1, 2, 3):
            back_z[j].wait_recv()

        def sort_rows(cols):
            blocks = [ob[0, 0, 0, :, cols].astype(F32)] + [ret[j, :, cols].astype(F32) for j in (1, 2, 3)]
            for d in range(4):
                tb[d, :, cols] = jnp.concatenate([b[d * 8:d * 8 + 8] for b in blocks], axis=0).astype(BF)

        tiles(7, 256, sort_rows)
        to_owner.append(group([(tb.at[d], tg.at[d], at(dy=d)) for d in (1, 3, 2)], tg.at[pl.ds(1, 3)]))
        tg[0] = tb[0]

    def mine(d, first, count, cols):
        return m[by_z[d % 8], first:first + count, cols]

    hops = {}
    for step in range(4):
        for half, (start, count) in enumerate(parts):
            cols = pl.ds(start, count * 256)
            if step == 0:
                finish(half)
            for way, sign in ((0, -1), (1, 1)):
                slot = step * 2 + way
                far = sign * (4 - step)
                if step == 0:
                    zs[slot, 0:16, cols] = mine(far, 16 * way, 16, cols).astype(BF)
                    src, dst = zs.at[slot, pl.ds(0, 16), cols], zr.at[slot, pl.ds(0, 16), cols]
                else:
                    hops[step - 1, half, way].wait_recv()
                    if step == 1:
                        first = 16 * way
                        total = mine(far, first, 16, cols) + zr[slot - 2, 0:16, cols].astype(F32)
                        zs[slot, first:first + 16, cols] = total.astype(BF)
                        zs[slot, 16 - first:32 - first, cols] = mine(far, 16 - first, 16, cols).astype(BF)
                    else:
                        zs[slot, :, cols] = (mine(far, 0, 32, cols) + zr[slot - 2, :, cols].astype(F32)).astype(BF)
                    src, dst = zs.at[slot, :, cols], zr.at[slot, :, cols]
                hops[step, half, way] = copy_to(src, dst, at(dz=sign))
        if step == 0:
            send_target()
        if step == 1:
            for copy in started[:-6]:
                copy.wait_send()
            del started[:-6]
        if step == 2:
            for copy in to_owner:
                copy.wait_recv()

            def write_target(cols):
                target[:, cols] = dot_t(weigh[...], tg[:, :, cols].reshape(128, 256)).astype(BF)

            tiles(7, 256, write_target)
            target_out = pltpu.make_async_copy(target, target_hbm, local_sem.at[8])
            target_out.start()
    for half, (start, count) in enumerate(parts):
        cols = pl.ds(start, count * 256)
        total = mine(0, 0, 32, cols)
        for way in range(2):
            hops[3, half, way].wait_recv()
            total += zr[6 + way, :, cols].astype(F32)
        grad[:, cols] = total * (loss_scale / 16384)
    grad_out = pltpu.make_async_copy(grad, grad_hbm, local_sem.at[9])
    grad_out.start()
    for copy in started:
        copy.wait_send()
    target_out.wait()
    grad_out.wait()


N_COPIES = 140


def body(teacher_in, expert_ids, gate_codes, w_gate, w_up, w_down, student_in, projection):
    hbm = pl.BlockSpec(memory_space=pl.ANY)
    return pl.pallas_call(
        kernel,
        out_shape=(
            jax.ShapeDtypeStruct((256, W), BF),
            jax.ShapeDtypeStruct((32, W), F32),
        ),
        in_specs=[hbm] * 8,
        out_specs=(hbm, hbm),
        scratch_shapes=[
            pltpu.VMEM((256, W), BF),
            pltpu.VMEM((32, W), F32),
            pltpu.VMEM((4, 32, W), BF),
            pltpu.VMEM((8, 256), jnp.int32),
            pltpu.VMEM((8, 256), jnp.int32),
            pltpu.VMEM((32, W), BF),
            pltpu.VMEM((256, W), BF),
            pltpu.VMEM((256, 2048), BF),
            pltpu.VMEM((W, 2 * H), BF),
            pltpu.VMEM((H, W), BF),
            pltpu.VMEM((128, 256), BF),
            pltpu.VMEM((16, 16, W // 2), BF),
            pltpu.VMEM((256, 2048), BF),
            pltpu.VMEM((512, 256), BF),
            pltpu.VMEM((4, 32, 2048), BF),
            pltpu.VMEM((8, 2, 32, 2048), BF),
            pltpu.VMEM((2, 4, 2, 4, 16, W // 2), BF),
            pltpu.VMEM((128, W), BF),
            pltpu.VMEM((4, 4, 32, 2 * H), BF),
            pltpu.VMEM((4, 4, 32, 2 * H), BF),
            pltpu.VMEM((4, 4, 32, H), BF),
            pltpu.VMEM((4, 2, 32, W), F32),
            pltpu.VMEM((4, 2, 32, W), BF),
            pltpu.VMEM((4, 2, 32, W), BF),
            pltpu.VMEM((4, 32, W), BF),
            pltpu.VMEM((4, 32, W), BF),
            pltpu.VMEM((4, 2, 4, 32, W), BF),
            pltpu.VMEM((4, 32, W), BF),
            pltpu.VMEM((4, 32, W), BF),
            pltpu.VMEM((4, 4, 32, 512), BF),
            pltpu.VMEM((4, 4, 32, 512), BF),
            pltpu.VMEM((2, 4, 32, W), BF),
            pltpu.VMEM((8, 32, 2048), BF),
            pltpu.VMEM((4, 8, 32, 512), BF),
            pltpu.VMEM((4, 8, 32, 512), BF),
            pltpu.VMEM((4, 2, 32, 512), BF),
            pltpu.VMEM((4, 32, 512), BF),
            pltpu.VMEM((4, 32, 512), BF),
            pltpu.VMEM((4, 32, 512), BF),
            pltpu.VMEM((4, 32, 512), BF),
            pltpu.VMEM((8, 2, 32, 128), BF),
            pltpu.VMEM((8, 32, 256), BF),
            pltpu.VMEM((4, 8, 2, 32, 128), BF),
            pltpu.VMEM((4, 8, 32, 256), BF),
            pltpu.VMEM((8, 32, W), F32),
            pltpu.VMEM((8, 32, W), BF),
            pltpu.VMEM((8, 32, W), BF),
            pltpu.SemaphoreType.DMA((N_COPIES,)),
            pltpu.SemaphoreType.DMA((N_COPIES,)),
            pltpu.SemaphoreType.DMA((10,)),
        ],
        compiler_params=pltpu.CompilerParams(
            collective_id=0, has_side_effects=True, vmem_limit_bytes=60 * 1024 * 1024
        ),
        cost_estimate=pl.CostEstimate(flops=8_000_000_000, bytes_accessed=12_000_000, transcendentals=0),
    )(expert_ids.T, gate_codes.T, projection, teacher_in, student_in, w_gate, w_up, w_down)


def solution(mesh):
    in_specs = (
        P("exp", "pair"),
        P("exp", None),
        P("exp", None),
        P("pair", "exp"),
        P("pair", "exp"),
        P("exp", "pair"),
        P("exp", None),
        P("exp", "pair"),
    )
    out_specs = (P("exp", "pair"), P("exp", "pair"))
    return jax.shard_map(body, mesh=mesh, in_specs=in_specs, out_specs=out_specs, check_vma=False)
```

```python
import jax
import jax.numpy as jnp
from jax import lax
from jax.experimental import pallas as pl
from jax.experimental.pallas import tpu as pltpu
from jax.sharding import PartitionSpec as P

CAP = 8
MESH = pl.DeviceIdType.MESH
BF = jnp.bfloat16
F32 = jnp.float32

loss_scale = 128.0
norm_epsilon = 1e-06

W = 1792
H = 512


def dot_t(a, b):
    return lax.dot_general(a, b, (((0,), (0,)), ((), ())), preferred_element_type=F32)


def dot(a, b):
    return jnp.dot(a, b, preferred_element_type=F32)


def tiles(count, size, f, first=0):
    for i in range(count):
        f(pl.ds(first + i * size, size))


def kernel(
    ids_hbm, codes_hbm, proj_hbm, teacher_hbm, student_hbm, wg_hbm, wu_hbm, wd_hbm,
    target_hbm, grad_hbm, target, grad, tg, ids, codes, proj, teacher, student_in,
    wgu, wd, weigh, packed, normed, left_x, wn, gx, rows, xk, gu, xr, act, prodf, ps, pr, vs, vr, ob, ret, tb,
    wny, wnb, pb, gxr, gs1, gr1, gs2, gr2, gs3, gr3, gt, kt, kf, m, zs, zr,
    send_sem, recv_sem, local_sem,
):
    e = lax.axis_index("exp")
    x = lax.axis_index("pair")
    y, z, c = e // 16, (e // 2) % 8, e % 2
    sg = 1 - 2 * (z % 2)

    by_y = [lax.rem(y + d, 4) for d in range(4)]
    by_x = [lax.rem(x + d, 4) for d in range(4)]
    by_z = [lax.rem(z + d, 8) for d in range(8)]
    by_hop = {d: lax.rem(z + d * sg + 8, 8) for d in (1, -1, 2, -2, 3, -3)}
    known = {}

    def at(dy=0, dz=0, hop=0, other=False):
        key = dy % 4, dz % 8, hop, other
        if key not in known:
            zz = by_hop[hop] if hop else by_z[dz % 8]
            known[key] = (by_y[dy % 4] * 16 + zz * 2 + (1 - c if other else c), x)
        return known[key]

    def at_x(dx):
        return (e, by_x[dx % 4])

    number = [0, 0]
    started = []

    def new_recv():
        number[1] += 1
        return number[1] - 1

    def copy_to(src, dst, device, recv=None):
        i = number[0]
        number[0] += 1
        copy = pltpu.make_async_remote_copy(
            src_ref=src, dst_ref=dst, send_sem=send_sem.at[i],
            recv_sem=recv_sem.at[new_recv() if recv is None else recv],
            device_id=device, device_id_type=MESH,
        )
        copy.start()
        started.append(copy)
        return copy

    def arrival(dst, recv):
        return pltpu.make_async_remote_copy(
            src_ref=dst, dst_ref=dst, send_sem=send_sem.at[0], recv_sem=recv_sem.at[recv],
            device_id=at(other=True), device_id_type=MESH,
        )

    weights = [
        pltpu.make_async_copy(wg_hbm, wgu.at[0], local_sem.at[0]),
        pltpu.make_async_copy(wu_hbm, wgu.at[1], local_sem.at[1]),
        pltpu.make_async_copy(wd_hbm, wd, local_sem.at[2]),
    ]
    operands = [
        pltpu.make_async_copy(src, dst, local_sem.at[3 + i])
        for i, (src, dst) in enumerate((
            (ids_hbm, ids), (codes_hbm, codes), (teacher_hbm, teacher), (student_hbm, student_in), (proj_hbm, proj),
        ))
    ]
    for copy in operands:
        copy.start()

    barrier = pltpu.get_barrier_semaphore()
    peers = [at(dy=d, hop=-j) for d in range(4) for j in range(4) if d or j]
    peers += [at(dy=d, hop=1) for d in range(4)] + [at(hop=2), at(dz=4), at(other=True)]
    peers += [at_x(d) for d in (1, 2, 3)]
    for peer in peers:
        pl.semaphore_signal(barrier, inc=1, device_id=peer, device_id_type=MESH)

    operands[0].wait()
    operands[1].wait()
    place = lax.broadcasted_iota(jnp.int32, (128, 256), 0)
    hop = (place >> 3) & 3
    shift = jnp.where(hop == 0, 0, jnp.where(hop == 1, -sg, jnp.where(hop == 2, sg, 2)))
    expert = ((y + 4 - (place >> 5)) & 3) * 4 + ((z // 2 + 4 + shift) & 3)
    hit = jnp.zeros((128, 256), F32)
    code = jnp.zeros((128, 256), jnp.int32)
    for k in range(8):
        same = ids[k:k + 1, :] == expert
        hit = jnp.where(same, 1.0, hit)
        code = jnp.where(same, codes[k:k + 1, :], code)
    ahead = lax.broadcasted_iota(jnp.int32, (256, 256), 0) < lax.broadcasted_iota(jnp.int32, (256, 256), 1)
    rank = dot(hit.astype(BF), jnp.where(ahead, 1.0, 0.0).astype(BF))
    chosen = jnp.where(rank == (place & 7).astype(F32), hit, 0.0)
    weigh[...] = (chosen * code.astype(F32) * (1.0 / 256.0)).astype(BF)
    chosen = chosen.astype(BF)

    def pack(cols):
        size = cols.size
        low = dot(chosen, teacher[:, cols]).reshape(16, 8, size)
        high = dot(chosen, teacher[:, pl.ds(896 + cols.start, size)]).reshape(16, 8, size)
        packed[:, :, cols] = jnp.concatenate([low, high], axis=1).astype(BF)

    operands[2].wait()
    tiles(3, 256, pack)
    tiles(1, 128, pack, 768)
    pl.semaphore_wait(barrier, len(peers))

    out_hop = (0, -1, 2, -3)
    direct, via, over = {}, {}, {}
    for j in range(4):
        direct[j] = new_recv()
        for d in (1, 3, 2, 0):
            if j or d:
                copy_to(packed.at[d * 4 + j], rows.at[0, j, 0, d], at(dy=-d, hop=out_hop[j]), direct[j])
        if j == 0:
            via[0] = new_recv()
            for d in (0, 1, 3, 2):
                copy_to(packed.at[d * 4], rows.at[1, 0, 0, d], at(dy=-d, hop=1), via[0])
    rows[0, 0, 0, 0] = packed[0]
    for copy in weights:
        copy.start()

    operands[3].wait()
    wide = student_in[...].astype(F32)
    scale = 1.0 / jnp.sqrt(jnp.mean(wide * wide, axis=1, keepdims=True) + norm_epsilon)
    normed[...] = (wide * scale).astype(BF)
    left_x[...] = normed[:, pl.ds(pl.multiple_of(x * 512, 512), 512)].astype(F32).T.astype(BF)

    def early(cols):
        gx[:, :, :, cols] = dot(left_x[...], normed[:, cols]).reshape(8, 2, 32, 256).astype(BF)

    def early_rows(cols):
        out = dot(weigh[...], normed[:, cols]).reshape(4, 4, 8, 256)
        for j in range(4):
            wn[j, :, cols] = jnp.concatenate([out[d, j] for d in range(4)], axis=0).astype(BF)

    gram = {}

    def gram_start():
        tiles(8, 256, early)
        gram["core"] = copy_to(gx.at[:, 1 - c], gxr, at(other=True))

    def gram_0():
        gram["core"].wait_recv()
        for q in range(4):
            cols = slice(q * 512, q * 512 + 512)
            gs1[q] = (gx[:, c, :, cols].astype(F32) + gxr[:, :, cols].astype(F32)).astype(BF)
        gram["y"] = [copy_to(gs1.at[by_y[d]], gr1.at[d], at(dy=d)) for d in (1, 3, 2)]

    def gram_1():
        for copy in gram["y"]:
            copy.wait_recv()
        total = gs1[y].astype(F32) + sum(gr1[d].astype(F32) for d in (1, 2, 3))
        gs2[...] = total.astype(BF).reshape(4, 2, 32, 512)
        gram["pair"] = copy_to(gs2.at[:, 1 - z % 2], gr2, at(hop=1))

    def gram_1b():
        gram["pair"].wait_recv()
        gs3[...] = (gs2[:, z % 2].astype(F32) + gr2[...].astype(F32)).astype(BF)
        gram["z"] = [copy_to(gs3.at[by_z[d] // 2], gr3.at[d // 2], at(dz=d)) for d in (2, 6, 4)]

    def gram_2():
        for copy in gram["z"]:
            copy.wait_recv()
        total = gs3[z // 2].astype(F32) + sum(gr3[d].astype(F32) for d in range(1, 4))
        gt[x] = total.astype(BF)
        gram["x"] = [copy_to(gt.at[x], gt.at[x], at_x(d)) for d in (1, 3, 2)]

    early_y, swap = [], []

    def send_proj():
        operands[4].wait()
        early_y.extend([copy_to(proj, pb.at[0, y], at(dy=d)) for d in (1, 3, 2)])
        pb[0, y] = proj[...]

    wn_y, wn_z = [], {}

    def wn_rows():
        tiles(8, 256, early_rows)

        def features(yy):
            return pl.ds(pl.multiple_of(yy * 512, 512), 512)

        wn_y.extend([copy_to(wn.at[:, :, features(by_y[4 - d])], wny.at[d], at(dy=-d)) for d in (1, 3, 2)])
        wny[0] = wn[:, :, features(y)]

    def wn_send(j):
        while wn_y:
            wn_y.pop().wait_recv()
        if j:
            wn_z[j] = copy_to(wny.at[:, j], wnb.at[j], at(hop=out_hop[j]))

    def swap_proj():
        for copy in early_y:
            copy.wait_recv()
        swap.append(copy_to(pb.at[0], pb.at[1], at(other=True)))

    other_k = pl.ds(128, 128)

    def student_rows():
        for j in range(4):
            if j:
                wn_z[j].wait_recv()
            blocks = [(wnb[j, d] if j else wny[d, 0]).astype(F32) for d in range(4)]
            order = [blocks[(d + 4 - g) % 4][d * 8:d * 8 + 8] for g in range(4) for d in range(4)]
            kt[j] = jnp.concatenate(order, axis=0).T.reshape(8, 2, 32, 128).astype(BF)
            kf[j, :, :, 0:128] = kt[j, :, c]

    def gram_3():
        for copy in gram["x"]:
            copy.wait_recv()
        kt[4] = gt[...].reshape(128, 512).astype(F32).T.reshape(8, 2, 32, 128).astype(BF)
        kf[4, :, :, 0:128] = kt[4, :, c]
        swap.append(copy_to(kt.at[:, :, 1 - c], kf.at[:, :, :, other_k], at(other=True)))

    to_x, act_x, back_core, back_pair, back_z, round_y, far_y, whole = {}, {}, {}, {}, {}, {}, {}, {}
    parts = ((0, 4), (1024, 3))

    joint = {1: pl.ds(0, 2), 2: pl.ds(2, 1), 3: pl.ds(3, 1)}

    def spans(j):
        return parts if j == 3 else ((0, 7),)

    def arrive(j):
        into = rows.at[0, 0, 0, pl.ds(1, 3)] if j == 0 else rows.at[0, j, 0]
        arrival(into, direct[j]).wait_recv()
        if j:
            via[j] = new_recv()
            copy_to(rows.at[0, j, 0], rows.at[1, j, 0], at(hop=1), via[j])

    def arrive_via(j):
        arrival(rows.at[1, j, 0], via[j]).wait_recv()
        over[j] = copy_to(rows.at[:, j, 0], rows.at[:, j, 1], at(other=True))

    def gate_up(j):
        over[j].wait_recv()

        def unfold(cols):
            block = rows[:, j, :, :, :, cols].astype(F32).reshape(16, 2, 8, 128)
            xk[:, cols] = block[:, 0].reshape(128, 128).astype(BF)
            xk[:, pl.ds(896 + cols.start, 128)] = block[:, 1].reshape(128, 128).astype(BF)

        tiles(7, 128, unfold)
        if j == 0:
            weights[0].wait()
            weights[1].wait()
        for part in range(2):
            gu[j, part] = dot(xk[...], wgu[part]).reshape(4, 32, H).astype(BF)
        to_x[j] = [copy_to(gu.at[j, :, by_x[d]], xr.at[j, d], at_x(d)) for d in (1, 3, 2)]

    def activate(j):
        for copy in to_x[j]:
            copy.wait_recv()
        gate, up = [
            gu[j, part, x].astype(F32) + sum(xr[j, d, part].astype(F32) for d in (1, 2, 3)) for part in range(2)
        ]
        act[j, x] = (gate / (1.0 + jnp.exp(-gate)) * up).astype(BF)
        act_x[j] = [copy_to(act.at[j, x], act.at[j, x], at_x(d)) for d in (1, 3, 2)]

    def down(j):
        for copy in act_x[j]:
            copy.wait_recv()
        if j == 0:
            weights[2].wait()

        def step(cols):
            out = dot(act[j].reshape(128, H), wd[:, cols]).reshape(4, 32, 256)
            for i in range(2):
                prodf[j, i, :, cols] = out[2 * i]
                ps[j, i, :, cols] = out[2 * i + 1].astype(BF)

        for first, count in spans(j):
            tiles(count, 256, step, first)
            cols = pl.ds(first, count * 256)
            back_core[j, first] = copy_to(ps.at[j, :, :, cols], pr.at[j, :, :, cols], at(other=True))

    def core_sum(j):
        def step(cols):
            vs[j, :, cols] = (prodf[j, 1, :, cols] + pr[j, 1, :, cols].astype(F32)).astype(BF)

        for first, count in spans(j):
            back_core[j, first].wait_recv()
            tiles(count, 256, step, first)
            cols = pl.ds(first, count * 256)
            back_pair[j, first] = copy_to(vs.at[j, :, cols], vr.at[j, :, cols], at(hop=1))

    def pair_sum(j):
        def step(cols):
            ob[j, 0, 0, :, cols] = (
                prodf[j, 0, :, cols] + pr[j, 0, :, cols].astype(F32) + vr[j, :, cols].astype(F32)
            ).astype(BF)

        for first, count in spans(j):
            back_pair[j, first].wait_recv()
            tiles(count, 256, step, first)
            cols = pl.ds(first, count * 256)
            if j:
                round_y[j, first] = [
                    copy_to(ob.at[joint[j], 0, 0, :, cols], ob.at[joint[j], 0, g, :, cols], at(dy=g)) for g in (1, 3)
                ]
        if j:
            back_z[j] = copy_to(ob.at[j, 0, 0], ret.at[j], at(hop=-j))

    def relay(j):
        low, high = pl.ds(0, 16), pl.ds(16, 16)
        for first, count in spans(j):
            cols = pl.ds(first, count * 256)
            far_y[j, first] = []
            for side, (g, rows_g, dy) in enumerate(((1, low, 1), (3, high, -1))):
                round_y[j, first][side].wait_recv()
                far_y[j, first].append(
                    copy_to(ob.at[joint[j], 0, g, rows_g, cols], ob.at[joint[j], 0, 2, rows_g, cols], at(dy=dy))
                )

    def far(j):
        for first, count in spans(j):
            for copy in far_y[j, first]:
                copy.wait_recv()
            cols = pl.ds(first, count * 256)
            whole[j, first] = copy_to(
                ob.at[joint[j], 0, :, :, cols], ob.at[joint[j], 1, :, :, cols], at(other=True)
            )

    def product(j, cols):
        return dot(kf[j].reshape(256, 256), ob[j, :, :, :, cols].reshape(256, 256))

    def student():
        for copy in swap:
            copy.wait_recv()
        for j in (1, 2):
            whole[j, 0].wait_recv()

        def step(cols):
            part = dot(kf[4].reshape(256, 256), pb[:, :, :, cols].reshape(256, 256))
            part -= product(0, cols) + product(1, cols) + product(2, cols)
            m[:, :, cols] = part.reshape(8, 32, 256)

        tiles(7, 256, step)

    def finish(part):
        first, count = parts[part]
        whole[3, first].wait_recv()

        def step(cols):
            m[:, :, cols] -= product(3, cols).reshape(8, 32, 256)

        tiles(count, 256, step, first)

    def run(steps):
        for name, j in steps:
            name(j)

    def when(f):
        return (lambda _: f(), 0)

    run([
        (arrive, 0), (arrive_via, 0), (arrive, 1), when(gram_start), (arrive, 2), (gate_up, 0), (arrive_via, 1),
        when(wn_rows), (arrive, 3), (arrive_via, 2), when(gram_0), (activate, 0), (gate_up, 1), (gate_up, 2),
        (wn_send, 2), (down, 0), when(send_proj), (arrive_via, 3), (activate, 1), (core_sum, 0), (wn_send, 3),
        (gate_up, 3), (down, 1), (activate, 2), (core_sum, 1), when(gram_1), (pair_sum, 0), (wn_send, 0),
        (activate, 3), (down, 2), (wn_send, 1), when(swap_proj), (pair_sum, 1), (core_sum, 2), (down, 3),
        (core_sum, 3), when(gram_1b), (pair_sum, 2), (relay, 1), (pair_sum, 3), when(student_rows), (relay, 2),
        (far, 1), when(gram_2), (relay, 3), (far, 2), when(gram_3), (far, 3), when(student),
    ])

    to_owner = []

    def send_target():
        for j in (1, 2, 3):
            back_z[j].wait_recv()

        def sort_rows(cols):
            blocks = [ob[0, 0, 0, :, cols].astype(F32)] + [ret[j, :, cols].astype(F32) for j in (1, 2, 3)]
            for d in range(4):
                tb[d, :, cols] = jnp.concatenate([b[d * 8:d * 8 + 8] for b in blocks], axis=0).astype(BF)

        tiles(7, 256, sort_rows)
        to_owner.extend([copy_to(tb.at[d], tg.at[d], at(dy=d)) for d in (1, 3, 2)])
        tg[0] = tb[0]

    def mine(d, first, count, cols):
        return m[by_z[d % 8], first:first + count, cols]

    hops = {}
    for step in range(4):
        for half, (start, count) in enumerate(parts):
            cols = pl.ds(start, count * 256)
            if step == 0:
                finish(half)
            for way, sign in ((0, -1), (1, 1)):
                slot = step * 2 + way
                far = sign * (4 - step)
                if step == 0:
                    zs[slot, 0:16, cols] = mine(far, 16 * way, 16, cols).astype(BF)
                    src, dst = zs.at[slot, pl.ds(0, 16), cols], zr.at[slot, pl.ds(0, 16), cols]
                else:
                    hops[step - 1, half, way].wait_recv()
                    if step == 1:
                        first = 16 * way
                        total = mine(far, first, 16, cols) + zr[slot - 2, 0:16, cols].astype(F32)
                        zs[slot, first:first + 16, cols] = total.astype(BF)
                        zs[slot, 16 - first:32 - first, cols] = mine(far, 16 - first, 16, cols).astype(BF)
                    else:
                        zs[slot, :, cols] = (mine(far, 0, 32, cols) + zr[slot - 2, :, cols].astype(F32)).astype(BF)
                    src, dst = zs.at[slot, :, cols], zr.at[slot, :, cols]
                hops[step, half, way] = copy_to(src, dst, at(dz=sign))
        if step == 0:
            send_target()
        if step == 1:
            for copy in started[:-8]:
                copy.wait_send()
            del started[:-8]
        if step == 2:
            for copy in to_owner:
                copy.wait_recv()

            def write_target(cols):
                target[:, cols] = dot_t(weigh[...], tg[:, :, cols].reshape(128, 256)).astype(BF)

            tiles(7, 256, write_target)
            target_out = pltpu.make_async_copy(target, target_hbm, local_sem.at[8])
            target_out.start()
    for half, (start, count) in enumerate(parts):
        cols = pl.ds(start, count * 256)
        total = mine(0, 0, 32, cols)
        for way in range(2):
            hops[3, half, way].wait_recv()
            total += zr[6 + way, :, cols].astype(F32)
        grad[:, cols] = total * (loss_scale / 16384)
    grad_out = pltpu.make_async_copy(grad, grad_hbm, local_sem.at[9])
    grad_out.start()
    for copy in started:
        copy.wait_send()
    target_out.wait()
    grad_out.wait()


N_COPIES = 140


def body(teacher_in, expert_ids, gate_codes, w_gate, w_up, w_down, student_in, projection):
    hbm = pl.BlockSpec(memory_space=pl.ANY)
    return pl.pallas_call(
        kernel,
        out_shape=(
            jax.ShapeDtypeStruct((256, W), BF),
            jax.ShapeDtypeStruct((32, W), F32),
        ),
        in_specs=[hbm] * 8,
        out_specs=(hbm, hbm),
        scratch_shapes=[
            pltpu.VMEM((256, W), BF),
            pltpu.VMEM((32, W), F32),
            pltpu.VMEM((4, 32, W), BF),
            pltpu.VMEM((8, 256), jnp.int32),
            pltpu.VMEM((8, 256), jnp.int32),
            pltpu.VMEM((32, W), BF),
            pltpu.VMEM((256, W), BF),
            pltpu.VMEM((256, 2048), BF),
            pltpu.VMEM((2, W, H), BF),
            pltpu.VMEM((H, W), BF),
            pltpu.VMEM((128, 256), BF),
            pltpu.VMEM((16, 16, W // 2), BF),
            pltpu.VMEM((256, 2048), BF),
            pltpu.VMEM((512, 256), BF),
            pltpu.VMEM((4, 32, 2048), BF),
            pltpu.VMEM((8, 2, 32, 2048), BF),
            pltpu.VMEM((2, 4, 2, 4, 16, W // 2), BF),
            pltpu.VMEM((128, W), BF),
            pltpu.VMEM((4, 2, 4, 32, H), BF),
            pltpu.VMEM((4, 4, 2, 32, H), BF),
            pltpu.VMEM((4, 4, 32, H), BF),
            pltpu.VMEM((4, 2, 32, W), F32),
            pltpu.VMEM((4, 2, 32, W), BF),
            pltpu.VMEM((4, 2, 32, W), BF),
            pltpu.VMEM((4, 32, W), BF),
            pltpu.VMEM((4, 32, W), BF),
            pltpu.VMEM((4, 2, 4, 32, W), BF),
            pltpu.VMEM((4, 32, W), BF),
            pltpu.VMEM((4, 32, W), BF),
            pltpu.VMEM((4, 4, 32, 512), BF),
            pltpu.VMEM((4, 4, 32, 512), BF),
            pltpu.VMEM((2, 4, 32, W), BF),
            pltpu.VMEM((8, 32, 2048), BF),
            pltpu.VMEM((4, 8, 32, 512), BF),
            pltpu.VMEM((4, 8, 32, 512), BF),
            pltpu.VMEM((4, 2, 32, 512), BF),
            pltpu.VMEM((4, 32, 512), BF),
            pltpu.VMEM((4, 32, 512), BF),
            pltpu.VMEM((4, 32, 512), BF),
            pltpu.VMEM((4, 32, 512), BF),
            pltpu.VMEM((5, 8, 2, 32, 128), BF),
            pltpu.VMEM((5, 8, 32, 256), BF),
            pltpu.VMEM((8, 32, W), F32),
            pltpu.VMEM((8, 32, W), BF),
            pltpu.VMEM((8, 32, W), BF),
            pltpu.SemaphoreType.DMA((N_COPIES,)),
            pltpu.SemaphoreType.DMA((N_COPIES,)),
            pltpu.SemaphoreType.DMA((10,)),
        ],
        compiler_params=pltpu.CompilerParams(
            collective_id=0, has_side_effects=True, vmem_limit_bytes=60 * 1024 * 1024
        ),
        cost_estimate=pl.CostEstimate(flops=8_000_000_000, bytes_accessed=12_000_000, transcendentals=0),
    )(expert_ids.T, gate_codes.T, projection, teacher_in, student_in, w_gate, w_up, w_down)


def solution(mesh):
    in_specs = (
        P("exp", "pair"),
        P("exp", None),
        P("exp", None),
        P("pair", "exp"),
        P("pair", "exp"),
        P("exp", "pair"),
        P("exp", None),
        P("exp", "pair"),
    )
    out_specs = (P("exp", "pair"), P("exp", "pair"))
    return jax.shard_map(body, mesh=mesh, in_specs=in_specs, out_specs=out_specs, check_vma=False)
```

```python
import jax
import jax.numpy as jnp
from jax import lax
from jax.experimental import pallas as pl
from jax.experimental.pallas import tpu as pltpu
from jax.sharding import PartitionSpec as P

CAP = 8
MESH = pl.DeviceIdType.MESH
BF = jnp.bfloat16
F32 = jnp.float32

loss_scale = 128.0
norm_epsilon = 1e-06

W = 1792
H = 512


def dot_t(a, b):
    return lax.dot_general(a, b, (((0,), (0,)), ((), ())), preferred_element_type=F32)


def dot(a, b):
    return jnp.dot(a, b, preferred_element_type=F32)


def tiles(count, size, f, first=0):
    for i in range(count):
        f(pl.ds(first + i * size, size))


def kernel(
    ids_hbm, codes_hbm, proj_hbm, teacher_hbm, student_hbm, wg_hbm, wu_hbm, wd_hbm,
    target_hbm, grad_hbm, target, grad, tg, ids, codes, proj, teacher, student_in,
    wgu, wd, weigh, packed, normed, left_x, wn, gx, rows, xk, gu, xr, act, prodf, ps, pr, vs, vr, ob, ret, tb,
    wny, wnb, pb, gxr, gs1, gr1, gs2, gr2, gs3, gr3, gt, gtt, gtf, wkt, wk, m, zs, zr,
    send_sem, recv_sem, local_sem,
):
    e = lax.axis_index("exp")
    x = lax.axis_index("pair")
    y, z, c = e // 16, (e // 2) % 8, e % 2
    sg = 1 - 2 * (z % 2)

    by_y = [lax.rem(y + d, 4) for d in range(4)]
    by_x = [lax.rem(x + d, 4) for d in range(4)]
    by_z = [lax.rem(z + d, 8) for d in range(8)]
    by_hop = {d: lax.rem(z + d * sg + 8, 8) for d in (1, -1, 2, -2, 3, -3)}
    known = {}

    def at(dy=0, dz=0, hop=0, other=False):
        key = dy % 4, dz % 8, hop, other
        if key not in known:
            zz = by_hop[hop] if hop else by_z[dz % 8]
            known[key] = (by_y[dy % 4] * 16 + zz * 2 + (1 - c if other else c), x)
        return known[key]

    def at_x(dx):
        return (e, by_x[dx % 4])

    number = [0, 0]
    started = []

    def new_recv():
        number[1] += 1
        return number[1] - 1

    def copy_to(src, dst, device, recv=None):
        i = number[0]
        number[0] += 1
        copy = pltpu.make_async_remote_copy(
            src_ref=src, dst_ref=dst, send_sem=send_sem.at[i],
            recv_sem=recv_sem.at[new_recv() if recv is None else recv],
            device_id=device, device_id_type=MESH,
        )
        copy.start()
        started.append(copy)
        return copy

    def arrival(dst, recv):
        return pltpu.make_async_remote_copy(
            src_ref=dst, dst_ref=dst, send_sem=send_sem.at[0], recv_sem=recv_sem.at[recv],
            device_id=at(other=True), device_id_type=MESH,
        )

    weights = [
        pltpu.make_async_copy(wg_hbm, wgu.at[0], local_sem.at[0]),
        pltpu.make_async_copy(wu_hbm, wgu.at[1], local_sem.at[1]),
        pltpu.make_async_copy(wd_hbm, wd, local_sem.at[2]),
    ]
    operands = [
        pltpu.make_async_copy(src, dst, local_sem.at[3 + i])
        for i, (src, dst) in enumerate((
            (ids_hbm, ids), (codes_hbm, codes), (teacher_hbm, teacher), (student_hbm, student_in), (proj_hbm, proj),
        ))
    ]
    for copy in operands:
        copy.start()

    barrier = pltpu.get_barrier_semaphore()
    peers = [at(dy=dy, dz=dz) for dy in range(4) for dz in (0, 1, -1, 2, -2, 3, -3) if dy or dz]
    peers += [at(dz=4), at(other=True)] + [at_x(d) for d in (1, 2, 3)]
    for peer in peers:
        pl.semaphore_signal(barrier, inc=1, device_id=peer, device_id_type=MESH)

    operands[0].wait()
    operands[1].wait()
    place = lax.broadcasted_iota(jnp.int32, (128, 256), 0)
    hop = (place >> 3) & 3
    shift = jnp.where(hop == 0, 0, jnp.where(hop == 1, -sg, jnp.where(hop == 2, sg, 2)))
    expert = ((y + 4 - (place >> 5)) & 3) * 4 + ((z // 2 + 4 + shift) & 3)
    hit = jnp.zeros((128, 256), F32)
    code = jnp.zeros((128, 256), jnp.int32)
    for k in range(8):
        same = ids[k:k + 1, :] == expert
        hit = jnp.where(same, 1.0, hit)
        code = jnp.where(same, codes[k:k + 1, :], code)
    ahead = lax.broadcasted_iota(jnp.int32, (256, 256), 0) < lax.broadcasted_iota(jnp.int32, (256, 256), 1)
    rank = dot(hit.astype(BF), jnp.where(ahead, 1.0, 0.0).astype(BF))
    chosen = jnp.where(rank == (place & 7).astype(F32), hit, 0.0)
    weigh[...] = (chosen * code.astype(F32) * (1.0 / 256.0)).astype(BF)
    chosen = chosen.astype(BF)

    def pack(cols):
        size = cols.size
        low = dot(chosen, teacher[:, cols]).reshape(16, 8, size)
        high = dot(chosen, teacher[:, pl.ds(896 + cols.start, size)]).reshape(16, 8, size)
        packed[:, :, cols] = jnp.concatenate([low, high], axis=1).astype(BF)

    operands[2].wait()
    tiles(3, 256, pack)
    tiles(1, 128, pack, 768)
    pl.semaphore_wait(barrier, len(peers))

    out_hop = (0, -1, 2, -3)
    direct, via, over = {}, {}, {}
    for j in range(4):
        direct[j] = new_recv()
        for d in (1, 3, 2, 0):
            if j or d:
                copy_to(packed.at[d * 4 + j], rows.at[0, j, 0, d], at(dy=-d, hop=out_hop[j]), direct[j])
        if j == 0:
            via[0] = new_recv()
            for d in (0, 1, 3, 2):
                copy_to(packed.at[d * 4], rows.at[1, 0, 0, d], at(dy=-d, hop=1), via[0])
    rows[0, 0, 0, 0] = packed[0]
    for copy in weights:
        copy.start()

    operands[3].wait()
    wide = student_in[...].astype(F32)
    scale = 1.0 / jnp.sqrt(jnp.mean(wide * wide, axis=1, keepdims=True) + norm_epsilon)
    normed[...] = (wide * scale).astype(BF)
    left_x[...] = normed[:, pl.ds(pl.multiple_of(x * 512, 512), 512)].astype(F32).T.astype(BF)

    def early(cols):
        gx[:, :, :, cols] = dot(left_x[...], normed[:, cols]).reshape(8, 2, 32, 256).astype(BF)

    def early_rows(cols):
        out = dot(weigh[...], normed[:, cols]).reshape(4, 4, 8, 256)
        for j in range(4):
            wn[j, :, cols] = jnp.concatenate([out[d, j] for d in range(4)], axis=0).astype(BF)

    gram = {}

    def gram_start():
        tiles(8, 256, early)
        gram["core"] = copy_to(gx.at[:, 1 - c], gxr, at(other=True))

    def gram_0():
        gram["core"].wait_recv()
        for q in range(4):
            cols = slice(q * 512, q * 512 + 512)
            gs1[q] = (gx[:, c, :, cols].astype(F32) + gxr[:, :, cols].astype(F32)).astype(BF)
        gram["y"] = [copy_to(gs1.at[by_y[d]], gr1.at[d], at(dy=d)) for d in (1, 3, 2)]

    def gram_1():
        for copy in gram["y"]:
            copy.wait_recv()
        total = gs1[y].astype(F32) + sum(gr1[d].astype(F32) for d in (1, 2, 3))
        gs2[...] = total.astype(BF).reshape(4, 2, 32, 512)
        gram["pair"] = copy_to(gs2.at[:, 1 - z % 2], gr2, at(hop=1))

    def gram_1b():
        gram["pair"].wait_recv()
        gs3[...] = (gs2[:, z % 2].astype(F32) + gr2[...].astype(F32)).astype(BF)
        gram["z"] = [copy_to(gs3.at[by_z[d] // 2], gr3.at[d // 2], at(dz=d)) for d in (2, 6, 4)]

    def gram_2():
        for copy in gram["z"]:
            copy.wait_recv()
        total = gs3[z // 2].astype(F32) + sum(gr3[d].astype(F32) for d in range(1, 4))
        gt[x] = total.astype(BF)
        gram["x"] = [copy_to(gt.at[x], gt.at[x], at_x(d)) for d in (1, 3, 2)]

    early_y, swap = [], []

    def send_proj():
        operands[4].wait()
        early_y.extend([copy_to(proj, pb.at[0, y], at(dy=d)) for d in (1, 3, 2)])
        pb[0, y] = proj[...]

    wn_y, wn_z = [], {}

    def wn_rows():
        tiles(8, 256, early_rows)

        def features(yy):
            return pl.ds(pl.multiple_of(yy * 512, 512), 512)

        wn_y.extend([copy_to(wn.at[:, :, features(by_y[4 - d])], wny.at[d], at(dy=-d)) for d in (1, 3, 2)])
        wny[0] = wn[:, :, features(y)]

    def wn_send(j):
        while wn_y:
            wn_y.pop().wait_recv()
        if j:
            wn_z[j] = copy_to(wny.at[:, j], wnb.at[j], at(hop=out_hop[j]))

    def swap_proj():
        for copy in early_y:
            copy.wait_recv()
        swap.append(copy_to(pb.at[0], pb.at[1], at(other=True)))

    other_k = pl.ds(128, 128)

    def student_rows():
        for j in range(4):
            if j:
                wn_z[j].wait_recv()
            blocks = [(wnb[j, d] if j else wny[d, 0]).astype(F32) for d in range(4)]
            order = [blocks[(d + 4 - g) % 4][d * 8:d * 8 + 8] for g in range(4) for d in range(4)]
            wkt[j] = (-jnp.concatenate(order, axis=0)).T.reshape(8, 2, 32, 128).astype(BF)
            wk[j, :, :, 0:128] = wkt[j, :, c]
        swap.append(copy_to(wkt.at[:, :, 1 - c], wk.at[:, :, :, other_k], at(other=True)))

    def gram_3():
        for copy in gram["x"]:
            copy.wait_recv()
        gtt[...] = gt[...].reshape(128, 512).astype(F32).T.reshape(8, 2, 32, 128).astype(BF)
        gtf[:, :, 0:128] = gtt[:, c]
        swap.append(copy_to(gtt.at[:, 1 - c], gtf.at[:, :, other_k], at(other=True)))

    to_x, act_x, back_core, back_pair, back_z, round_y, far_y, whole = {}, {}, {}, {}, {}, {}, {}, {}
    parts = ((0, 4), (1024, 3))

    def spans(j):
        return parts if j == 3 else ((0, 7),)

    def arrive(j):
        into = rows.at[0, 0, 0, pl.ds(1, 3)] if j == 0 else rows.at[0, j, 0]
        arrival(into, direct[j]).wait_recv()
        if j:
            via[j] = new_recv()
            copy_to(rows.at[0, j, 0], rows.at[1, j, 0], at(hop=1), via[j])

    def arrive_via(j):
        arrival(rows.at[1, j, 0], via[j]).wait_recv()
        over[j] = copy_to(rows.at[:, j, 0], rows.at[:, j, 1], at(other=True))

    def gate_up(j):
        over[j].wait_recv()

        def unfold(cols):
            block = rows[:, j, :, :, :, cols].astype(F32).reshape(16, 2, 8, 128)
            xk[:, cols] = block[:, 0].reshape(128, 128).astype(BF)
            xk[:, pl.ds(896 + cols.start, 128)] = block[:, 1].reshape(128, 128).astype(BF)

        tiles(7, 128, unfold)
        if j == 0:
            weights[0].wait()
            weights[1].wait()
        for part in range(2):
            gu[j, part] = dot(xk[...], wgu[part]).reshape(4, 32, H).astype(BF)
        to_x[j] = [copy_to(gu.at[j, :, by_x[d]], xr.at[j, d], at_x(d)) for d in (1, 3, 2)]

    def activate(j):
        for copy in to_x[j]:
            copy.wait_recv()
        gate, up = [
            gu[j, part, x].astype(F32) + sum(xr[j, d, part].astype(F32) for d in (1, 2, 3)) for part in range(2)
        ]
        act[j, x] = (gate / (1.0 + jnp.exp(-gate)) * up).astype(BF)
        act_x[j] = [copy_to(act.at[j, x], act.at[j, x], at_x(d)) for d in (1, 3, 2)]

    def down(j):
        for copy in act_x[j]:
            copy.wait_recv()
        if j == 0:
            weights[2].wait()

        def step(cols):
            out = dot(act[j].reshape(128, H), wd[:, cols]).reshape(4, 32, 256)
            for i in range(2):
                prodf[j, i, :, cols] = out[2 * i]
                ps[j, i, :, cols] = out[2 * i + 1].astype(BF)

        for first, count in spans(j):
            tiles(count, 256, step, first)
            cols = pl.ds(first, count * 256)
            back_core[j, first] = copy_to(ps.at[j, :, :, cols], pr.at[j, :, :, cols], at(other=True))

    def core_sum(j):
        def step(cols):
            vs[j, :, cols] = (prodf[j, 1, :, cols] + pr[j, 1, :, cols].astype(F32)).astype(BF)

        for first, count in spans(j):
            back_core[j, first].wait_recv()
            tiles(count, 256, step, first)
            cols = pl.ds(first, count * 256)
            back_pair[j, first] = copy_to(vs.at[j, :, cols], vr.at[j, :, cols], at(hop=1))

    def pair_sum(j):
        def step(cols):
            ob[j, 0, 0, :, cols] = (
                prodf[j, 0, :, cols] + pr[j, 0, :, cols].astype(F32) + vr[j, :, cols].astype(F32)
            ).astype(BF)

        for first, count in spans(j):
            back_pair[j, first].wait_recv()
            tiles(count, 256, step, first)
            cols = pl.ds(first, count * 256)
            round_y[j, first] = [
                copy_to(ob.at[j, 0, 0, :, cols], ob.at[j, 0, g, :, cols], at(dy=g)) for g in (1, 3)
            ]
        if j:
            back_z[j] = copy_to(ob.at[j, 0, 0], ret.at[j], at(hop=-j))

    def relay(j):
        low, high = pl.ds(0, 16), pl.ds(16, 16)
        for first, count in spans(j):
            cols = pl.ds(first, count * 256)
            far_y[j, first] = []
            for side, (g, rows_g, dy) in enumerate(((1, low, 1), (3, high, -1))):
                round_y[j, first][side].wait_recv()
                far_y[j, first].append(
                    copy_to(ob.at[j, 0, g, rows_g, cols], ob.at[j, 0, 2, rows_g, cols], at(dy=dy))
                )

    def far(j):
        for first, count in spans(j):
            for copy in far_y[j, first]:
                copy.wait_recv()
            cols = pl.ds(first, count * 256)
            whole[j, first] = copy_to(ob.at[j, 0, :, :, cols], ob.at[j, 1, :, :, cols], at(other=True))

    def finish(part):
        if part == 0:
            for copy in swap:
                copy.wait_recv()
            for j in range(3):
                whole[j, 0].wait_recv()
        first, count = parts[part]
        whole[3, first].wait_recv()

        def step(cols):
            left = [wk[j].reshape(256, 256) for j in range(4)] + [gtf[...].reshape(256, 256)]
            right = [ob[j, :, :, :, cols].reshape(256, 256) for j in range(4)]
            right.append(pb[:, :, :, cols].reshape(256, 256))
            out = dot(jnp.concatenate(left, axis=1), jnp.concatenate(right, axis=0))
            m[:, :, cols] = out.reshape(8, 32, 256)

        tiles(count, 256, step, first)

    def run(steps):
        for name, j in steps:
            name(j)

    def when(f):
        return (lambda _: f(), 0)

    run([
        (arrive, 0), (arrive_via, 0), (arrive, 1), when(gram_start), (arrive, 2), (gate_up, 0), (arrive_via, 1),
        when(wn_rows), (arrive, 3), (arrive_via, 2), when(gram_0), (activate, 0), (gate_up, 1), (gate_up, 2),
        (wn_send, 2), (down, 0), when(send_proj), (arrive_via, 3), (activate, 1), (core_sum, 0), (wn_send, 3),
        (gate_up, 3), (down, 1), (activate, 2), (core_sum, 1), when(gram_1), (pair_sum, 0), (wn_send, 0),
        (activate, 3), (down, 2), (wn_send, 1), when(swap_proj), (pair_sum, 1), (core_sum, 2), (down, 3), (relay, 0),
        (core_sum, 3), (relay, 1), when(gram_1b), (pair_sum, 2), (far, 0), (pair_sum, 3), when(student_rows),
        (far, 1), (relay, 2), when(gram_2), (relay, 3), (far, 2), when(gram_3), (far, 3),
    ])

    to_owner = []

    def send_target():
        for j in (1, 2, 3):
            back_z[j].wait_recv()

        def sort_rows(cols):
            blocks = [ob[0, 0, 0, :, cols].astype(F32)] + [ret[j, :, cols].astype(F32) for j in (1, 2, 3)]
            for d in range(4):
                tb[d, :, cols] = jnp.concatenate([b[d * 8:d * 8 + 8] for b in blocks], axis=0).astype(BF)

        tiles(7, 256, sort_rows)
        to_owner.extend([copy_to(tb.at[d], tg.at[d], at(dy=d)) for d in (1, 3, 2)])
        tg[0] = tb[0]

    def mine(d, first, count, cols):
        return m[by_z[d % 8], first:first + count, cols]

    hops = {}
    for step in range(4):
        for half, (start, count) in enumerate(parts):
            cols = pl.ds(start, count * 256)
            if step == 0:
                finish(half)
            for way, sign in ((0, -1), (1, 1)):
                slot = step * 2 + way
                far = sign * (4 - step)
                if step == 0:
                    zs[slot, 0:16, cols] = mine(far, 16 * way, 16, cols).astype(BF)
                    src, dst = zs.at[slot, pl.ds(0, 16), cols], zr.at[slot, pl.ds(0, 16), cols]
                else:
                    hops[step - 1, half, way].wait_recv()
                    if step == 1:
                        first = 16 * way
                        total = mine(far, first, 16, cols) + zr[slot - 2, 0:16, cols].astype(F32)
                        zs[slot, first:first + 16, cols] = total.astype(BF)
                        zs[slot, 16 - first:32 - first, cols] = mine(far, 16 - first, 16, cols).astype(BF)
                    else:
                        zs[slot, :, cols] = (mine(far, 0, 32, cols) + zr[slot - 2, :, cols].astype(F32)).astype(BF)
                    src, dst = zs.at[slot, :, cols], zr.at[slot, :, cols]
                hops[step, half, way] = copy_to(src, dst, at(dz=sign))
        if step == 0:
            send_target()
        if step == 1:
            for copy in started[:-8]:
                copy.wait_send()
            del started[:-8]
        if step == 2:
            for copy in to_owner:
                copy.wait_recv()

            def write_target(cols):
                target[:, cols] = dot_t(weigh[...], tg[:, :, cols].reshape(128, 256)).astype(BF)

            tiles(7, 256, write_target)
            target_out = pltpu.make_async_copy(target, target_hbm, local_sem.at[8])
            target_out.start()
    for half, (start, count) in enumerate(parts):
        cols = pl.ds(start, count * 256)
        total = mine(0, 0, 32, cols)
        for way in range(2):
            hops[3, half, way].wait_recv()
            total += zr[6 + way, :, cols].astype(F32)
        grad[:, cols] = total * (loss_scale / 16384)
    grad_out = pltpu.make_async_copy(grad, grad_hbm, local_sem.at[9])
    grad_out.start()
    for copy in started:
        copy.wait_send()
    target_out.wait()
    grad_out.wait()


N_COPIES = 140


def body(teacher_in, expert_ids, gate_codes, w_gate, w_up, w_down, student_in, projection):
    hbm = pl.BlockSpec(memory_space=pl.ANY)
    return pl.pallas_call(
        kernel,
        out_shape=(
            jax.ShapeDtypeStruct((256, W), BF),
            jax.ShapeDtypeStruct((32, W), F32),
        ),
        in_specs=[hbm] * 8,
        out_specs=(hbm, hbm),
        scratch_shapes=[
            pltpu.VMEM((256, W), BF),
            pltpu.VMEM((32, W), F32),
            pltpu.VMEM((4, 32, W), BF),
            pltpu.VMEM((8, 256), jnp.int32),
            pltpu.VMEM((8, 256), jnp.int32),
            pltpu.VMEM((32, W), BF),
            pltpu.VMEM((256, W), BF),
            pltpu.VMEM((256, 2048), BF),
            pltpu.VMEM((2, W, H), BF),
            pltpu.VMEM((H, W), BF),
            pltpu.VMEM((128, 256), BF),
            pltpu.VMEM((16, 16, W // 2), BF),
            pltpu.VMEM((256, 2048), BF),
            pltpu.VMEM((512, 256), BF),
            pltpu.VMEM((4, 32, 2048), BF),
            pltpu.VMEM((8, 2, 32, 2048), BF),
            pltpu.VMEM((2, 4, 2, 4, 16, W // 2), BF),
            pltpu.VMEM((128, W), BF),
            pltpu.VMEM((4, 2, 4, 32, H), BF),
            pltpu.VMEM((4, 4, 2, 32, H), BF),
            pltpu.VMEM((4, 4, 32, H), BF),
            pltpu.VMEM((4, 2, 32, W), F32),
            pltpu.VMEM((4, 2, 32, W), BF),
            pltpu.VMEM((4, 2, 32, W), BF),
            pltpu.VMEM((4, 32, W), BF),
            pltpu.VMEM((4, 32, W), BF),
            pltpu.VMEM((4, 2, 4, 32, W), BF),
            pltpu.VMEM((4, 32, W), BF),
            pltpu.VMEM((4, 32, W), BF),
            pltpu.VMEM((4, 4, 32, 512), BF),
            pltpu.VMEM((4, 4, 32, 512), BF),
            pltpu.VMEM((2, 4, 32, W), BF),
            pltpu.VMEM((8, 32, 2048), BF),
            pltpu.VMEM((4, 8, 32, 512), BF),
            pltpu.VMEM((4, 8, 32, 512), BF),
            pltpu.VMEM((4, 2, 32, 512), BF),
            pltpu.VMEM((4, 32, 512), BF),
            pltpu.VMEM((4, 32, 512), BF),
            pltpu.VMEM((4, 32, 512), BF),
            pltpu.VMEM((4, 32, 512), BF),
            pltpu.VMEM((8, 2, 32, 128), BF),
            pltpu.VMEM((8, 32, 256), BF),
            pltpu.VMEM((4, 8, 2, 32, 128), BF),
            pltpu.VMEM((4, 8, 32, 256), BF),
            pltpu.VMEM((8, 32, W), F32),
            pltpu.VMEM((8, 32, W), BF),
            pltpu.VMEM((8, 32, W), BF),
            pltpu.SemaphoreType.DMA((N_COPIES,)),
            pltpu.SemaphoreType.DMA((N_COPIES,)),
            pltpu.SemaphoreType.DMA((10,)),
        ],
        compiler_params=pltpu.CompilerParams(
            collective_id=0, has_side_effects=True, vmem_limit_bytes=60 * 1024 * 1024
        ),
        cost_estimate=pl.CostEstimate(flops=8_000_000_000, bytes_accessed=12_000_000, transcendentals=0),
    )(expert_ids.T, gate_codes.T, projection, teacher_in, student_in, w_gate, w_up, w_down)


def solution(mesh):
    in_specs = (
        P("exp", "pair"),
        P("exp", None),
        P("exp", None),
        P("pair", "exp"),
        P("pair", "exp"),
        P("exp", "pair"),
        P("exp", None),
        P("exp", "pair"),
    )
    out_specs = (P("exp", "pair"), P("exp", "pair"))
    return jax.shard_map(body, mesh=mesh, in_specs=in_specs, out_specs=out_specs, check_vma=False)
```

```python
import jax
import jax.numpy as jnp
from jax import lax
from jax.experimental import pallas as pl
from jax.experimental.pallas import tpu as pltpu
from jax.sharding import PartitionSpec as P

CAP = 8
MESH = pl.DeviceIdType.MESH
BF = jnp.bfloat16
F32 = jnp.float32

loss_scale = 128.0
norm_epsilon = 1e-06

W = 1792
H = 512


def dot_t(a, b):
    return lax.dot_general(a, b, (((0,), (0,)), ((), ())), preferred_element_type=F32)


def dot(a, b):
    return jnp.dot(a, b, preferred_element_type=F32)


def tiles(count, size, f, first=0):
    for i in range(count):
        f(pl.ds(first + i * size, size))


def kernel(
    ids_hbm, codes_hbm, proj_hbm, teacher_hbm, student_hbm, wg_hbm, wu_hbm, wd_hbm,
    target_hbm, grad_hbm, target, grad, tg, ids, codes, proj, teacher, student_in,
    wgu, wd, weigh, packed, normed, left_x, wn, gx, rows, xk, gu, xr, act, prodf, ps, pr, vs, vr, ob, ret, tb,
    wny, wnb, pb, gxr, gs1, gr1, gs2, gr2, gs3, gr3, gt, gtt, gtf, wkt, wk, m, zs, zr,
    send_sem, recv_sem, local_sem,
):
    e = lax.axis_index("exp")
    x = lax.axis_index("pair")
    y, z, c = e // 16, (e // 2) % 8, e % 2
    sg = 1 - 2 * (z % 2)

    by_y = [lax.rem(y + d, 4) for d in range(4)]
    by_x = [lax.rem(x + d, 4) for d in range(4)]
    by_z = [lax.rem(z + d, 8) for d in range(8)]
    by_hop = {d: lax.rem(z + d * sg + 8, 8) for d in (1, -1, 2, -2, 3, -3)}
    known = {}

    def at(dy=0, dz=0, hop=0, other=False):
        key = dy % 4, dz % 8, hop, other
        if key not in known:
            zz = by_hop[hop] if hop else by_z[dz % 8]
            known[key] = (by_y[dy % 4] * 16 + zz * 2 + (1 - c if other else c), x)
        return known[key]

    def at_x(dx):
        return (e, by_x[dx % 4])

    number = [0, 0]
    started = []

    def new_recv():
        number[1] += 1
        return number[1] - 1

    def copy_to(src, dst, device, recv=None):
        i = number[0]
        number[0] += 1
        copy = pltpu.make_async_remote_copy(
            src_ref=src, dst_ref=dst, send_sem=send_sem.at[i],
            recv_sem=recv_sem.at[new_recv() if recv is None else recv],
            device_id=device, device_id_type=MESH,
        )
        copy.start()
        started.append(copy)
        return copy

    def arrival(dst, recv):
        return pltpu.make_async_remote_copy(
            src_ref=dst, dst_ref=dst, send_sem=send_sem.at[0], recv_sem=recv_sem.at[recv],
            device_id=at(other=True), device_id_type=MESH,
        )

    weights = [
        pltpu.make_async_copy(wg_hbm, wgu.at[0], local_sem.at[0]),
        pltpu.make_async_copy(wu_hbm, wgu.at[1], local_sem.at[1]),
        pltpu.make_async_copy(wd_hbm, wd, local_sem.at[2]),
    ]
    operands = [
        pltpu.make_async_copy(src, dst, local_sem.at[3 + i])
        for i, (src, dst) in enumerate((
            (ids_hbm, ids), (codes_hbm, codes), (teacher_hbm, teacher), (student_hbm, student_in), (proj_hbm, proj),
        ))
    ]
    for copy in operands:
        copy.start()

    barrier = pltpu.get_barrier_semaphore()
    peers = [at(dy=dy, dz=dz) for dy in range(4) for dz in (0, 1, -1, 2, -2, 3, -3) if dy or dz]
    peers += [at(dz=4), at(other=True)] + [at_x(d) for d in (1, 2, 3)]
    for peer in peers:
        pl.semaphore_signal(barrier, inc=1, device_id=peer, device_id_type=MESH)

    operands[0].wait()
    operands[1].wait()
    place = lax.broadcasted_iota(jnp.int32, (128, 256), 0)
    hop = (place >> 3) & 3
    shift = jnp.where(hop == 0, 0, jnp.where(hop == 1, -sg, jnp.where(hop == 2, sg, 2)))
    expert = ((y + 4 - (place >> 5)) & 3) * 4 + ((z // 2 + 4 + shift) & 3)
    hit = jnp.zeros((128, 256), F32)
    code = jnp.zeros((128, 256), jnp.int32)
    for k in range(8):
        same = ids[k:k + 1, :] == expert
        hit = jnp.where(same, 1.0, hit)
        code = jnp.where(same, codes[k:k + 1, :], code)
    ahead = lax.broadcasted_iota(jnp.int32, (256, 256), 0) < lax.broadcasted_iota(jnp.int32, (256, 256), 1)
    rank = dot(hit.astype(BF), jnp.where(ahead, 1.0, 0.0).astype(BF))
    chosen = jnp.where(rank == (place & 7).astype(F32), hit, 0.0)
    weigh[...] = (chosen * code.astype(F32) * (1.0 / 256.0)).astype(BF)
    chosen = chosen.astype(BF)

    def pack(cols):
        size = cols.size
        low = dot(chosen, teacher[:, cols]).reshape(16, 8, size)
        high = dot(chosen, teacher[:, pl.ds(896 + cols.start, size)]).reshape(16, 8, size)
        packed[:, :, cols] = jnp.concatenate([low, high], axis=1).astype(BF)

    operands[2].wait()
    tiles(3, 256, pack)
    tiles(1, 128, pack, 768)
    pl.semaphore_wait(barrier, len(peers))

    out_hop = (0, -1, 2, -3)
    direct, via, over = {}, {}, {}
    for j in range(4):
        direct[j] = new_recv()
        for d in (1, 3, 2, 0):
            if j or d:
                copy_to(packed.at[d * 4 + j], rows.at[0, j, 0, d], at(dy=-d, hop=out_hop[j]), direct[j])
        if j == 0:
            via[0] = new_recv()
            for d in (0, 1, 3, 2):
                copy_to(packed.at[d * 4], rows.at[1, 0, 0, d], at(dy=-d, hop=1), via[0])
    rows[0, 0, 0, 0] = packed[0]
    for copy in weights:
        copy.start()

    operands[3].wait()
    wide = student_in[...].astype(F32)
    scale = 1.0 / jnp.sqrt(jnp.mean(wide * wide, axis=1, keepdims=True) + norm_epsilon)
    normed[...] = (wide * scale).astype(BF)
    left_x[...] = normed[:, pl.ds(pl.multiple_of(x * 512, 512), 512)].astype(F32).T.astype(BF)

    def early(cols):
        gx[:, :, :, cols] = dot(left_x[...], normed[:, cols]).reshape(8, 2, 32, 256).astype(BF)

    def early_rows(cols):
        out = dot(weigh[...], normed[:, cols]).reshape(4, 4, 8, 256)
        for j in range(4):
            wn[j, :, cols] = jnp.concatenate([out[d, j] for d in range(4)], axis=0).astype(BF)

    gram = {}

    def gram_start():
        tiles(8, 256, early)
        gram["core"] = copy_to(gx.at[:, 1 - c], gxr, at(other=True))

    def gram_0():
        gram["core"].wait_recv()
        for q in range(4):
            cols = slice(q * 512, q * 512 + 512)
            gs1[q] = (gx[:, c, :, cols].astype(F32) + gxr[:, :, cols].astype(F32)).astype(BF)
        gram["y"] = [copy_to(gs1.at[by_y[d]], gr1.at[d], at(dy=d)) for d in (1, 3, 2)]

    def gram_1():
        for copy in gram["y"]:
            copy.wait_recv()
        total = gs1[y].astype(F32) + sum(gr1[d].astype(F32) for d in (1, 2, 3))
        gs2[...] = total.astype(BF).reshape(4, 2, 32, 512)
        gram["pair"] = copy_to(gs2.at[:, 1 - z % 2], gr2, at(hop=1))

    def gram_1b():
        gram["pair"].wait_recv()
        gs3[...] = (gs2[:, z % 2].astype(F32) + gr2[...].astype(F32)).astype(BF)
        gram["z"] = [copy_to(gs3.at[by_z[d] // 2], gr3.at[d // 2], at(dz=d)) for d in (2, 6, 4)]

    def gram_2():
        for copy in gram["z"]:
            copy.wait_recv()
        total = gs3[z // 2].astype(F32) + sum(gr3[d].astype(F32) for d in range(1, 4))
        gt[x] = total.astype(BF)
        gram["x"] = [copy_to(gt.at[x], gt.at[x], at_x(d)) for d in (1, 3, 2)]

    early_y, swap = [], []

    def send_proj():
        operands[4].wait()
        early_y.extend([copy_to(proj, pb.at[0, y], at(dy=d)) for d in (1, 3, 2)])
        pb[0, y] = proj[...]

    wn_y, wn_z = [], {}

    def wn_rows():
        tiles(8, 256, early_rows)

        def features(yy):
            return pl.ds(pl.multiple_of(yy * 512, 512), 512)

        wn_y.extend([copy_to(wn.at[:, :, features(by_y[4 - d])], wny.at[d], at(dy=-d)) for d in (1, 3, 2)])
        wny[0] = wn[:, :, features(y)]

    def wn_send(j):
        while wn_y:
            wn_y.pop().wait_recv()
        if j:
            wn_z[j] = copy_to(wny.at[:, j], wnb.at[j], at(hop=out_hop[j]))

    def swap_proj():
        for copy in early_y:
            copy.wait_recv()
        swap.append(copy_to(pb.at[0], pb.at[1], at(other=True)))

    other_k = pl.ds(128, 128)

    def student_rows():
        for j in range(4):
            if j:
                wn_z[j].wait_recv()
            blocks = [(wnb[j, d] if j else wny[d, 0]).astype(F32) for d in range(4)]
            order = [blocks[(d + 4 - g) % 4][d * 8:d * 8 + 8] for g in range(4) for d in range(4)]
            wkt[j] = (-jnp.concatenate(order, axis=0)).T.reshape(8, 2, 32, 128).astype(BF)
            wk[j, :, :, 0:128] = wkt[j, :, c]
        swap.append(copy_to(wkt.at[:, :, 1 - c], wk.at[:, :, :, other_k], at(other=True)))

    def gram_3():
        for copy in gram["x"]:
            copy.wait_recv()
        gtt[...] = gt[...].reshape(128, 512).astype(F32).T.reshape(8, 2, 32, 128).astype(BF)
        gtf[:, :, 0:128] = gtt[:, c]
        swap.append(copy_to(gtt.at[:, 1 - c], gtf.at[:, :, other_k], at(other=True)))

    to_x, act_x, back_core, back_pair, back_z, round_y, far_y, whole = {}, {}, {}, {}, {}, {}, {}, {}
    parts = ((0, 3), (768, 2), (1280, 2))

    def spans(j):
        return parts if j == 3 else ((0, 7),)

    def arrive(j):
        into = rows.at[0, 0, 0, pl.ds(1, 3)] if j == 0 else rows.at[0, j, 0]
        arrival(into, direct[j]).wait_recv()
        if j:
            via[j] = new_recv()
            copy_to(rows.at[0, j, 0], rows.at[1, j, 0], at(hop=1), via[j])

    def arrive_via(j):
        arrival(rows.at[1, j, 0], via[j]).wait_recv()
        over[j] = copy_to(rows.at[:, j, 0], rows.at[:, j, 1], at(other=True))

    def gate_up(j):
        over[j].wait_recv()

        def unfold(cols):
            block = rows[:, j, :, :, :, cols].astype(F32).reshape(16, 2, 8, 128)
            xk[:, cols] = block[:, 0].reshape(128, 128).astype(BF)
            xk[:, pl.ds(896 + cols.start, 128)] = block[:, 1].reshape(128, 128).astype(BF)

        tiles(7, 128, unfold)
        if j == 0:
            weights[0].wait()
            weights[1].wait()
        for part in range(2):
            gu[j, part] = dot(xk[...], wgu[part]).reshape(4, 32, H).astype(BF)
        to_x[j] = [copy_to(gu.at[j, :, by_x[d]], xr.at[j, d], at_x(d)) for d in (1, 3, 2)]

    def activate(j):
        for copy in to_x[j]:
            copy.wait_recv()
        gate, up = [
            gu[j, part, x].astype(F32) + sum(xr[j, d, part].astype(F32) for d in (1, 2, 3)) for part in range(2)
        ]
        act[j, x] = (gate / (1.0 + jnp.exp(-gate)) * up).astype(BF)
        act_x[j] = [copy_to(act.at[j, x], act.at[j, x], at_x(d)) for d in (1, 3, 2)]

    def down(j):
        for copy in act_x[j]:
            copy.wait_recv()
        if j == 0:
            weights[2].wait()

        def step(cols):
            out = dot(act[j].reshape(128, H), wd[:, cols]).reshape(4, 32, 256)
            for i in range(2):
                prodf[j, i, :, cols] = out[2 * i]
                ps[j, i, :, cols] = out[2 * i + 1].astype(BF)

        for first, count in spans(j):
            tiles(count, 256, step, first)
            cols = pl.ds(first, count * 256)
            back_core[j, first] = copy_to(ps.at[j, :, :, cols], pr.at[j, :, :, cols], at(other=True))

    def core_sum(j):
        def step(cols):
            vs[j, :, cols] = (prodf[j, 1, :, cols] + pr[j, 1, :, cols].astype(F32)).astype(BF)

        for first, count in spans(j):
            back_core[j, first].wait_recv()
            tiles(count, 256, step, first)
            cols = pl.ds(first, count * 256)
            back_pair[j, first] = copy_to(vs.at[j, :, cols], vr.at[j, :, cols], at(hop=1))

    def pair_sum(j):
        def step(cols):
            ob[j, 0, 0, :, cols] = (
                prodf[j, 0, :, cols] + pr[j, 0, :, cols].astype(F32) + vr[j, :, cols].astype(F32)
            ).astype(BF)

        for first, count in spans(j):
            back_pair[j, first].wait_recv()
            tiles(count, 256, step, first)
            cols = pl.ds(first, count * 256)
            round_y[j, first] = [
                copy_to(ob.at[j, 0, 0, :, cols], ob.at[j, 0, g, :, cols], at(dy=g)) for g in (1, 3)
            ]
        if j:
            back_z[j] = copy_to(ob.at[j, 0, 0], ret.at[j], at(hop=-j))

    def relay(j):
        low, high = pl.ds(0, 16), pl.ds(16, 16)
        for first, count in spans(j):
            cols = pl.ds(first, count * 256)
            far_y[j, first] = []
            for side, (g, rows_g, dy) in enumerate(((1, low, 1), (3, high, -1))):
                round_y[j, first][side].wait_recv()
                far_y[j, first].append(
                    copy_to(ob.at[j, 0, g, rows_g, cols], ob.at[j, 0, 2, rows_g, cols], at(dy=dy))
                )

    def far(j):
        for first, count in spans(j):
            for copy in far_y[j, first]:
                copy.wait_recv()
            cols = pl.ds(first, count * 256)
            whole[j, first] = copy_to(ob.at[j, 0, :, :, cols], ob.at[j, 1, :, :, cols], at(other=True))

    def finish(part):
        if part == 0:
            for copy in swap:
                copy.wait_recv()
            for j in range(3):
                whole[j, 0].wait_recv()
        first, count = parts[part]
        whole[3, first].wait_recv()

        def step(cols):
            left = [wk[j].reshape(256, 256) for j in range(4)] + [gtf[...].reshape(256, 256)]
            right = [ob[j, :, :, :, cols].reshape(256, 256) for j in range(4)]
            right.append(pb[:, :, :, cols].reshape(256, 256))
            out = dot(jnp.concatenate(left, axis=1), jnp.concatenate(right, axis=0))
            m[:, :, cols] = out.reshape(8, 32, 256)

        tiles(count, 256, step, first)

    def run(steps):
        for name, j in steps:
            name(j)

    def when(f):
        return (lambda _: f(), 0)

    run([
        (arrive, 0), (arrive_via, 0), (arrive, 1), when(gram_start), (arrive, 2), (gate_up, 0), (arrive_via, 1),
        when(wn_rows), (arrive, 3), (arrive_via, 2), when(gram_0), (activate, 0), (gate_up, 1), (gate_up, 2),
        (wn_send, 2), (down, 0), when(send_proj), (arrive_via, 3), (activate, 1), (core_sum, 0), (wn_send, 3),
        (gate_up, 3), (down, 1), (activate, 2), (core_sum, 1), when(gram_1), (pair_sum, 0), (wn_send, 0),
        (activate, 3), (down, 2), (wn_send, 1), when(swap_proj), (pair_sum, 1), (core_sum, 2), (down, 3), (relay, 0),
        (core_sum, 3), (relay, 1), when(gram_1b), (pair_sum, 2), (far, 0), (pair_sum, 3), when(student_rows),
        (far, 1), (relay, 2), when(gram_2), (relay, 3), (far, 2), when(gram_3), (far, 3),
    ])

    to_owner = []

    def send_target():
        for j in (1, 2, 3):
            back_z[j].wait_recv()

        def sort_rows(cols):
            blocks = [ob[0, 0, 0, :, cols].astype(F32)] + [ret[j, :, cols].astype(F32) for j in (1, 2, 3)]
            for d in range(4):
                tb[d, :, cols] = jnp.concatenate([b[d * 8:d * 8 + 8] for b in blocks], axis=0).astype(BF)

        tiles(7, 256, sort_rows)
        to_owner.extend([copy_to(tb.at[d], tg.at[d], at(dy=d)) for d in (1, 3, 2)])
        tg[0] = tb[0]

    def mine(d, first, count, cols):
        return m[by_z[d % 8], first:first + count, cols]

    hops = {}
    for step in range(4):
        for half, (start, count) in enumerate(parts):
            cols = pl.ds(start, count * 256)
            if step == 0:
                finish(half)
            for way, sign in ((0, -1), (1, 1)):
                slot = step * 2 + way
                far = sign * (4 - step)
                if step == 0:
                    zs[slot, 0:16, cols] = mine(far, 16 * way, 16, cols).astype(BF)
                    src, dst = zs.at[slot, pl.ds(0, 16), cols], zr.at[slot, pl.ds(0, 16), cols]
                else:
                    hops[step - 1, half, way].wait_recv()
                    if step == 1:
                        first = 16 * way
                        total = mine(far, first, 16, cols) + zr[slot - 2, 0:16, cols].astype(F32)
                        zs[slot, first:first + 16, cols] = total.astype(BF)
                        zs[slot, 16 - first:32 - first, cols] = mine(far, 16 - first, 16, cols).astype(BF)
                    else:
                        zs[slot, :, cols] = (mine(far, 0, 32, cols) + zr[slot - 2, :, cols].astype(F32)).astype(BF)
                    src, dst = zs.at[slot, :, cols], zr.at[slot, :, cols]
                hops[step, half, way] = copy_to(src, dst, at(dz=sign))
        if step == 0:
            send_target()
        if step == 1:
            for copy in started[:-10]:
                copy.wait_send()
            del started[:-10]
        if step == 2:
            for copy in to_owner:
                copy.wait_recv()

            def write_target(cols):
                target[:, cols] = dot_t(weigh[...], tg[:, :, cols].reshape(128, 256)).astype(BF)

            tiles(7, 256, write_target)
            target_out = pltpu.make_async_copy(target, target_hbm, local_sem.at[8])
            target_out.start()
    for half, (start, count) in enumerate(parts):
        cols = pl.ds(start, count * 256)
        total = mine(0, 0, 32, cols)
        for way in range(2):
            hops[3, half, way].wait_recv()
            total += zr[6 + way, :, cols].astype(F32)
        grad[:, cols] = total * (loss_scale / 16384)
    grad_out = pltpu.make_async_copy(grad, grad_hbm, local_sem.at[9])
    grad_out.start()
    for copy in started:
        copy.wait_send()
    target_out.wait()
    grad_out.wait()


N_COPIES = 180


def body(teacher_in, expert_ids, gate_codes, w_gate, w_up, w_down, student_in, projection):
    hbm = pl.BlockSpec(memory_space=pl.ANY)
    return pl.pallas_call(
        kernel,
        out_shape=(
            jax.ShapeDtypeStruct((256, W), BF),
            jax.ShapeDtypeStruct((32, W), F32),
        ),
        in_specs=[hbm] * 8,
        out_specs=(hbm, hbm),
        scratch_shapes=[
            pltpu.VMEM((256, W), BF),
            pltpu.VMEM((32, W), F32),
            pltpu.VMEM((4, 32, W), BF),
            pltpu.VMEM((8, 256), jnp.int32),
            pltpu.VMEM((8, 256), jnp.int32),
            pltpu.VMEM((32, W), BF),
            pltpu.VMEM((256, W), BF),
            pltpu.VMEM((256, 2048), BF),
            pltpu.VMEM((2, W, H), BF),
            pltpu.VMEM((H, W), BF),
            pltpu.VMEM((128, 256), BF),
            pltpu.VMEM((16, 16, W // 2), BF),
            pltpu.VMEM((256, 2048), BF),
            pltpu.VMEM((512, 256), BF),
            pltpu.VMEM((4, 32, 2048), BF),
            pltpu.VMEM((8, 2, 32, 2048), BF),
            pltpu.VMEM((2, 4, 2, 4, 16, W // 2), BF),
            pltpu.VMEM((128, W), BF),
            pltpu.VMEM((4, 2, 4, 32, H), BF),
            pltpu.VMEM((4, 4, 2, 32, H), BF),
            pltpu.VMEM((4, 4, 32, H), BF),
            pltpu.VMEM((4, 2, 32, W), F32),
            pltpu.VMEM((4, 2, 32, W), BF),
            pltpu.VMEM((4, 2, 32, W), BF),
            pltpu.VMEM((4, 32, W), BF),
            pltpu.VMEM((4, 32, W), BF),
            pltpu.VMEM((4, 2, 4, 32, W), BF),
            pltpu.VMEM((4, 32, W), BF),
            pltpu.VMEM((4, 32, W), BF),
            pltpu.VMEM((4, 4, 32, 512), BF),
            pltpu.VMEM((4, 4, 32, 512), BF),
            pltpu.VMEM((2, 4, 32, W), BF),
            pltpu.VMEM((8, 32, 2048), BF),
            pltpu.VMEM((4, 8, 32, 512), BF),
            pltpu.VMEM((4, 8, 32, 512), BF),
            pltpu.VMEM((4, 2, 32, 512), BF),
            pltpu.VMEM((4, 32, 512), BF),
            pltpu.VMEM((4, 32, 512), BF),
            pltpu.VMEM((4, 32, 512), BF),
            pltpu.VMEM((4, 32, 512), BF),
            pltpu.VMEM((8, 2, 32, 128), BF),
            pltpu.VMEM((8, 32, 256), BF),
            pltpu.VMEM((4, 8, 2, 32, 128), BF),
            pltpu.VMEM((4, 8, 32, 256), BF),
            pltpu.VMEM((8, 32, W), F32),
            pltpu.VMEM((8, 32, W), BF),
            pltpu.VMEM((8, 32, W), BF),
            pltpu.SemaphoreType.DMA((N_COPIES,)),
            pltpu.SemaphoreType.DMA((N_COPIES,)),
            pltpu.SemaphoreType.DMA((10,)),
        ],
        compiler_params=pltpu.CompilerParams(
            collective_id=0, has_side_effects=True, vmem_limit_bytes=60 * 1024 * 1024
        ),
        cost_estimate=pl.CostEstimate(flops=8_000_000_000, bytes_accessed=12_000_000, transcendentals=0),
    )(expert_ids.T, gate_codes.T, projection, teacher_in, student_in, w_gate, w_up, w_down)


def solution(mesh):
    in_specs = (
        P("exp", "pair"),
        P("exp", None),
        P("exp", None),
        P("pair", "exp"),
        P("pair", "exp"),
        P("exp", "pair"),
        P("exp", None),
        P("exp", "pair"),
    )
    out_specs = (P("exp", "pair"), P("exp", "pair"))
    return jax.shard_map(body, mesh=mesh, in_specs=in_specs, out_specs=out_specs, check_vma=False)
```

```python
import jax
import jax.numpy as jnp
from jax import lax
from jax.experimental import pallas as pl
from jax.experimental.pallas import tpu as pltpu
from jax.sharding import PartitionSpec as P

CAP = 8
MESH = pl.DeviceIdType.MESH
BF = jnp.bfloat16
F32 = jnp.float32

loss_scale = 128.0
norm_epsilon = 1e-06

W = 1792
H = 512


def dot_t(a, b):
    return lax.dot_general(a, b, (((0,), (0,)), ((), ())), preferred_element_type=F32)


def dot(a, b):
    return jnp.dot(a, b, preferred_element_type=F32)


def tiles(count, size, f, first=0):
    for i in range(count):
        f(pl.ds(first + i * size, size))


def kernel(
    ids_hbm, codes_hbm, proj_hbm, teacher_hbm, student_hbm, wg_hbm, wu_hbm, wd_hbm,
    target_hbm, grad_hbm, target, grad, tg, ids, codes, proj, teacher, student_in,
    wgu, wd, weigh, packed, normed, left_x, wn, gx, rows, xk, gu, xr, act, prodf, ps, pr, vs, vr, ob, ret, tb,
    wny, wnb, pb, gxr, gs1, gr1, gs2, gr2, gs3, gr3, gt, gtt, gtf, wkt, wk, m, zs, zr,
    send_sem, recv_sem, local_sem,
):
    e = lax.axis_index("exp")
    x = lax.axis_index("pair")
    y, z, c = e // 16, (e // 2) % 8, e % 2
    sg = 1 - 2 * (z % 2)

    by_y = [lax.rem(y + d, 4) for d in range(4)]
    by_x = [lax.rem(x + d, 4) for d in range(4)]
    by_z = [lax.rem(z + d, 8) for d in range(8)]
    by_hop = {d: lax.rem(z + d * sg + 8, 8) for d in (1, -1, 2, -2, 3, -3)}
    known = {}

    def at(dy=0, dz=0, hop=0, other=False):
        key = dy % 4, dz % 8, hop, other
        if key not in known:
            zz = by_hop[hop] if hop else by_z[dz % 8]
            known[key] = (by_y[dy % 4] * 16 + zz * 2 + (1 - c if other else c), x)
        return known[key]

    def at_x(dx):
        return (e, by_x[dx % 4])

    number = [0, 0]
    started = []

    def new_recv():
        number[1] += 1
        return number[1] - 1

    def copy_to(src, dst, device, recv=None):
        i = number[0]
        number[0] += 1
        copy = pltpu.make_async_remote_copy(
            src_ref=src, dst_ref=dst, send_sem=send_sem.at[i],
            recv_sem=recv_sem.at[new_recv() if recv is None else recv],
            device_id=device, device_id_type=MESH,
        )
        copy.start()
        started.append(copy)
        return copy

    def arrival(dst, recv):
        return pltpu.make_async_remote_copy(
            src_ref=dst, dst_ref=dst, send_sem=send_sem.at[0], recv_sem=recv_sem.at[recv],
            device_id=at(other=True), device_id_type=MESH,
        )

    weights = [
        pltpu.make_async_copy(wg_hbm, wgu.at[0], local_sem.at[0]),
        pltpu.make_async_copy(wu_hbm, wgu.at[1], local_sem.at[1]),
        pltpu.make_async_copy(wd_hbm, wd, local_sem.at[2]),
    ]
    operands = [
        pltpu.make_async_copy(src, dst, local_sem.at[3 + i])
        for i, (src, dst) in enumerate((
            (ids_hbm, ids), (codes_hbm, codes), (teacher_hbm, teacher), (student_hbm, student_in), (proj_hbm, proj),
        ))
    ]
    for copy in operands:
        copy.start()

    barrier = pltpu.get_barrier_semaphore()
    peers = [at(dy=d, hop=-j) for d in range(4) for j in range(4) if d or j]
    peers += [at(dy=d, hop=1) for d in range(4)] + [at(hop=2), at(dz=4), at(other=True)]
    peers += [at_x(d) for d in (1, 2, 3)]
    for peer in peers:
        pl.semaphore_signal(barrier, inc=1, device_id=peer, device_id_type=MESH)

    operands[0].wait()
    operands[1].wait()
    place = lax.broadcasted_iota(jnp.int32, (128, 256), 0)
    hop = (place >> 3) & 3
    shift = jnp.where(hop == 0, 0, jnp.where(hop == 1, -sg, jnp.where(hop == 2, sg, 2)))
    expert = ((y + 4 - (place >> 5)) & 3) * 4 + ((z // 2 + 4 + shift) & 3)
    hit = jnp.zeros((128, 256), F32)
    code = jnp.zeros((128, 256), jnp.int32)
    for k in range(8):
        same = ids[k:k + 1, :] == expert
        hit = jnp.where(same, 1.0, hit)
        code = jnp.where(same, codes[k:k + 1, :], code)
    ahead = lax.broadcasted_iota(jnp.int32, (256, 256), 0) < lax.broadcasted_iota(jnp.int32, (256, 256), 1)
    rank = dot(hit.astype(BF), jnp.where(ahead, 1.0, 0.0).astype(BF))
    chosen = jnp.where(rank == (place & 7).astype(F32), hit, 0.0)
    weigh[...] = (chosen * code.astype(F32) * (1.0 / 256.0)).astype(BF)
    chosen = chosen.astype(BF)

    def pack(cols):
        size = cols.size
        low = dot(chosen, teacher[:, cols]).reshape(16, 8, size)
        high = dot(chosen, teacher[:, pl.ds(896 + cols.start, size)]).reshape(16, 8, size)
        packed[:, :, cols] = jnp.concatenate([low, high], axis=1).astype(BF)

    operands[2].wait()
    tiles(3, 256, pack)
    tiles(1, 128, pack, 768)
    pl.semaphore_wait(barrier, len(peers))

    out_hop = (0, -1, 2, -3)
    direct, via, over = {}, {}, {}
    for j in range(4):
        direct[j] = new_recv()
        for d in (1, 3, 2, 0):
            if j or d:
                copy_to(packed.at[d * 4 + j], rows.at[0, j, 0, d], at(dy=-d, hop=out_hop[j]), direct[j])
        if j == 0:
            via[0] = new_recv()
            for d in (0, 1, 3, 2):
                copy_to(packed.at[d * 4], rows.at[1, 0, 0, d], at(dy=-d, hop=1), via[0])
    rows[0, 0, 0, 0] = packed[0]
    for copy in weights:
        copy.start()

    operands[3].wait()
    wide = student_in[...].astype(F32)
    scale = 1.0 / jnp.sqrt(jnp.mean(wide * wide, axis=1, keepdims=True) + norm_epsilon)
    normed[...] = (wide * scale).astype(BF)
    left_x[...] = normed[:, pl.ds(pl.multiple_of(x * 512, 512), 512)].astype(F32).T.astype(BF)

    def early(cols):
        gx[:, :, :, cols] = dot(left_x[...], normed[:, cols]).reshape(8, 2, 32, 256).astype(BF)

    def early_rows(cols):
        out = dot(weigh[...], normed[:, cols]).reshape(4, 4, 8, 256)
        for j in range(4):
            wn[j, :, cols] = jnp.concatenate([out[d, j] for d in range(4)], axis=0).astype(BF)

    gram = {}

    def gram_start():
        tiles(8, 256, early)
        gram["core"] = copy_to(gx.at[:, 1 - c], gxr, at(other=True))

    def gram_0():
        gram["core"].wait_recv()
        for q in range(4):
            cols = slice(q * 512, q * 512 + 512)
            gs1[q] = (gx[:, c, :, cols].astype(F32) + gxr[:, :, cols].astype(F32)).astype(BF)
        gram["y"] = [copy_to(gs1.at[by_y[d]], gr1.at[d], at(dy=d)) for d in (1, 3, 2)]

    def gram_1():
        for copy in gram["y"]:
            copy.wait_recv()
        total = gs1[y].astype(F32) + sum(gr1[d].astype(F32) for d in (1, 2, 3))
        gs2[...] = total.astype(BF).reshape(4, 2, 32, 512)
        gram["pair"] = copy_to(gs2.at[:, 1 - z % 2], gr2, at(hop=1))

    def gram_1b():
        gram["pair"].wait_recv()
        gs3[...] = (gs2[:, z % 2].astype(F32) + gr2[...].astype(F32)).astype(BF)
        gram["z"] = [copy_to(gs3.at[by_z[d] // 2], gr3.at[d // 2], at(dz=d)) for d in (2, 6, 4)]

    def gram_2():
        for copy in gram["z"]:
            copy.wait_recv()
        total = gs3[z // 2].astype(F32) + sum(gr3[d].astype(F32) for d in range(1, 4))
        gt[x] = total.astype(BF)
        gram["x"] = [copy_to(gt.at[x], gt.at[x], at_x(d)) for d in (1, 3, 2)]

    early_y, swap = [], []

    def send_proj():
        operands[4].wait()
        early_y.extend([copy_to(proj, pb.at[0, y], at(dy=d)) for d in (1, 3, 2)])
        pb[0, y] = proj[...]

    wn_y, wn_z = [], {}

    def wn_rows():
        tiles(8, 256, early_rows)

        def features(yy):
            return pl.ds(pl.multiple_of(yy * 512, 512), 512)

        wn_y.extend([copy_to(wn.at[:, :, features(by_y[4 - d])], wny.at[d], at(dy=-d)) for d in (1, 3, 2)])
        wny[0] = wn[:, :, features(y)]

    def wn_send(j):
        while wn_y:
            wn_y.pop().wait_recv()
        if j:
            wn_z[j] = copy_to(wny.at[:, j], wnb.at[j], at(hop=out_hop[j]))

    def swap_proj():
        for copy in early_y:
            copy.wait_recv()
        swap.append(copy_to(pb.at[0], pb.at[1], at(other=True)))

    other_k = pl.ds(128, 128)

    def student_rows():
        for j in range(4):
            if j:
                wn_z[j].wait_recv()
            blocks = [(wnb[j, d] if j else wny[d, 0]).astype(F32) for d in range(4)]
            order = [blocks[(d + 4 - g) % 4][d * 8:d * 8 + 8] for g in range(4) for d in range(4)]
            wkt[j] = (-jnp.concatenate(order, axis=0)).T.reshape(8, 2, 32, 128).astype(BF)
            wk[j, :, :, 0:128] = wkt[j, :, c]
        swap.append(copy_to(wkt.at[:, :, 1 - c], wk.at[:, :, :, other_k], at(other=True)))

    def gram_3():
        for copy in gram["x"]:
            copy.wait_recv()
        gtt[...] = gt[...].reshape(128, 512).astype(F32).T.reshape(8, 2, 32, 128).astype(BF)
        gtf[:, :, 0:128] = gtt[:, c]
        swap.append(copy_to(gtt.at[:, 1 - c], gtf.at[:, :, other_k], at(other=True)))

    to_x, act_x, back_core, back_pair, back_z, round_y, far_y, whole = {}, {}, {}, {}, {}, {}, {}, {}
    parts = ((0, 4), (1024, 3))

    def spans(j):
        return parts if j == 3 else ((0, 7),)

    def arrive(j):
        into = rows.at[0, 0, 0, pl.ds(1, 3)] if j == 0 else rows.at[0, j, 0]
        arrival(into, direct[j]).wait_recv()
        if j:
            via[j] = new_recv()
            copy_to(rows.at[0, j, 0], rows.at[1, j, 0], at(hop=1), via[j])

    def arrive_via(j):
        arrival(rows.at[1, j, 0], via[j]).wait_recv()
        over[j] = copy_to(rows.at[:, j, 0], rows.at[:, j, 1], at(other=True))

    def gate_up(j):
        over[j].wait_recv()

        def unfold(cols):
            block = rows[:, j, :, :, :, cols].astype(F32).reshape(16, 2, 8, 128)
            xk[:, cols] = block[:, 0].reshape(128, 128).astype(BF)
            xk[:, pl.ds(896 + cols.start, 128)] = block[:, 1].reshape(128, 128).astype(BF)

        tiles(7, 128, unfold)
        if j == 0:
            weights[0].wait()
            weights[1].wait()
        for part in range(2):
            gu[j, part] = dot(xk[...], wgu[part]).reshape(4, 32, H).astype(BF)
        to_x[j] = [copy_to(gu.at[j, :, by_x[d]], xr.at[j, d], at_x(d)) for d in (1, 3, 2)]

    def activate(j):
        for copy in to_x[j]:
            copy.wait_recv()
        gate, up = [
            gu[j, part, x].astype(F32) + sum(xr[j, d, part].astype(F32) for d in (1, 2, 3)) for part in range(2)
        ]
        act[j, x] = (gate / (1.0 + jnp.exp(-gate)) * up).astype(BF)
        act_x[j] = [copy_to(act.at[j, x], act.at[j, x], at_x(d)) for d in (1, 3, 2)]

    def down(j):
        for copy in act_x[j]:
            copy.wait_recv()
        if j == 0:
            weights[2].wait()

        def step(cols):
            out = dot(act[j].reshape(128, H), wd[:, cols]).reshape(4, 32, 256)
            for i in range(2):
                prodf[j, i, :, cols] = out[2 * i]
                ps[j, i, :, cols] = out[2 * i + 1].astype(BF)

        for first, count in spans(j):
            tiles(count, 256, step, first)
            cols = pl.ds(first, count * 256)
            back_core[j, first] = copy_to(ps.at[j, :, :, cols], pr.at[j, :, :, cols], at(other=True))

    def core_sum(j):
        def step(cols):
            vs[j, :, cols] = (prodf[j, 1, :, cols] + pr[j, 1, :, cols].astype(F32)).astype(BF)

        for first, count in spans(j):
            back_core[j, first].wait_recv()
            tiles(count, 256, step, first)
            cols = pl.ds(first, count * 256)
            back_pair[j, first] = copy_to(vs.at[j, :, cols], vr.at[j, :, cols], at(hop=1))

    def pair_sum(j):
        def step(cols):
            ob[j, 0, 0, :, cols] = (
                prodf[j, 0, :, cols] + pr[j, 0, :, cols].astype(F32) + vr[j, :, cols].astype(F32)
            ).astype(BF)

        for first, count in spans(j):
            back_pair[j, first].wait_recv()
            tiles(count, 256, step, first)
            cols = pl.ds(first, count * 256)
            round_y[j, first] = [
                copy_to(ob.at[j, 0, 0, :, cols], ob.at[j, 0, g, :, cols], at(dy=g)) for g in (1, 3)
            ]
        if j:
            back_z[j] = copy_to(ob.at[j, 0, 0], ret.at[j], at(hop=-j))

    def relay(j):
        low, high = pl.ds(0, 16), pl.ds(16, 16)
        for first, count in spans(j):
            cols = pl.ds(first, count * 256)
            far_y[j, first] = []
            for side, (g, rows_g, dy) in enumerate(((1, low, 1), (3, high, -1))):
                round_y[j, first][side].wait_recv()
                far_y[j, first].append(
                    copy_to(ob.at[j, 0, g, rows_g, cols], ob.at[j, 0, 2, rows_g, cols], at(dy=dy))
                )

    def far(j):
        for first, count in spans(j):
            for copy in far_y[j, first]:
                copy.wait_recv()
            cols = pl.ds(first, count * 256)
            whole[j, first] = copy_to(ob.at[j, 0, :, :, cols], ob.at[j, 1, :, :, cols], at(other=True))

    def finish(part):
        if part == 0:
            for copy in swap:
                copy.wait_recv()
            for j in range(3):
                whole[j, 0].wait_recv()
        first, count = parts[part]
        whole[3, first].wait_recv()

        def step(cols):
            left = [wk[j].reshape(256, 256) for j in range(4)] + [gtf[...].reshape(256, 256)]
            right = [ob[j, :, :, :, cols].reshape(256, 256) for j in range(4)]
            right.append(pb[:, :, :, cols].reshape(256, 256))
            out = dot(jnp.concatenate(left, axis=1), jnp.concatenate(right, axis=0))
            m[:, :, cols] = out.reshape(8, 32, 256)

        tiles(count, 256, step, first)

    def run(steps):
        for name, j in steps:
            name(j)

    def when(f):
        return (lambda _: f(), 0)

    run([
        (arrive, 0), (arrive_via, 0), (arrive, 1), when(gram_start), (arrive, 2), (gate_up, 0), (arrive_via, 1),
        when(wn_rows), (arrive, 3), (arrive_via, 2), when(gram_0), (activate, 0), (gate_up, 1), (gate_up, 2),
        (wn_send, 2), (down, 0), when(send_proj), (arrive_via, 3), (activate, 1), (core_sum, 0), (wn_send, 3),
        (gate_up, 3), (down, 1), (activate, 2), (core_sum, 1), when(gram_1), (pair_sum, 0), (wn_send, 0),
        (activate, 3), (down, 2), (wn_send, 1), when(swap_proj), (pair_sum, 1), (core_sum, 2), (down, 3), (relay, 0),
        (core_sum, 3), (relay, 1), when(gram_1b), (pair_sum, 2), (far, 0), (pair_sum, 3), when(student_rows),
        (far, 1), (relay, 2), when(gram_2), (relay, 3), (far, 2), when(gram_3), (far, 3),
    ])

    to_owner = []

    def send_target():
        for j in (1, 2, 3):
            back_z[j].wait_recv()

        def sort_rows(cols):
            blocks = [ob[0, 0, 0, :, cols].astype(F32)] + [ret[j, :, cols].astype(F32) for j in (1, 2, 3)]
            for d in range(4):
                tb[d, :, cols] = jnp.concatenate([b[d * 8:d * 8 + 8] for b in blocks], axis=0).astype(BF)

        tiles(7, 256, sort_rows)
        to_owner.extend([copy_to(tb.at[d], tg.at[d], at(dy=d)) for d in (1, 3, 2)])
        tg[0] = tb[0]

    def mine(d, first, count, cols):
        return m[by_z[d % 8], first:first + count, cols]

    hops = {}
    for step in range(4):
        for half, (start, count) in enumerate(parts):
            cols = pl.ds(start, count * 256)
            if step == 0:
                finish(half)
            for way, sign in ((0, -1), (1, 1)):
                slot = step * 2 + way
                far = sign * (4 - step)
                if step == 0:
                    zs[slot, 0:16, cols] = mine(far, 16 * way, 16, cols).astype(BF)
                    src, dst = zs.at[slot, pl.ds(0, 16), cols], zr.at[slot, pl.ds(0, 16), cols]
                else:
                    hops[step - 1, half, way].wait_recv()
                    if step == 1:
                        first = 16 * way
                        total = mine(far, first, 16, cols) + zr[slot - 2, 0:16, cols].astype(F32)
                        zs[slot, first:first + 16, cols] = total.astype(BF)
                        zs[slot, 16 - first:32 - first, cols] = mine(far, 16 - first, 16, cols).astype(BF)
                    else:
                        zs[slot, :, cols] = (mine(far, 0, 32, cols) + zr[slot - 2, :, cols].astype(F32)).astype(BF)
                    src, dst = zs.at[slot, :, cols], zr.at[slot, :, cols]
                hops[step, half, way] = copy_to(src, dst, at(dz=sign))
        if step == 1:
            send_target()
        if step == 2:
            for copy in started[:-12]:
                copy.wait_send()
            del started[:-12]
        if step == 3:
            for copy in to_owner:
                copy.wait_recv()

            def write_target(cols):
                target[:, cols] = dot_t(weigh[...], tg[:, :, cols].reshape(128, 256)).astype(BF)

            tiles(7, 256, write_target)
            target_out = pltpu.make_async_copy(target, target_hbm, local_sem.at[8])
            target_out.start()
    for half, (start, count) in enumerate(parts):
        cols = pl.ds(start, count * 256)
        total = mine(0, 0, 32, cols)
        for way in range(2):
            hops[3, half, way].wait_recv()
            total += zr[6 + way, :, cols].astype(F32)
        grad[:, cols] = total * (loss_scale / 16384)
    grad_out = pltpu.make_async_copy(grad, grad_hbm, local_sem.at[9])
    grad_out.start()
    for copy in started:
        copy.wait_send()
    target_out.wait()
    grad_out.wait()


N_COPIES = 140


def body(teacher_in, expert_ids, gate_codes, w_gate, w_up, w_down, student_in, projection):
    hbm = pl.BlockSpec(memory_space=pl.ANY)
    return pl.pallas_call(
        kernel,
        out_shape=(
            jax.ShapeDtypeStruct((256, W), BF),
            jax.ShapeDtypeStruct((32, W), F32),
        ),
        in_specs=[hbm] * 8,
        out_specs=(hbm, hbm),
        scratch_shapes=[
            pltpu.VMEM((256, W), BF),
            pltpu.VMEM((32, W), F32),
            pltpu.VMEM((4, 32, W), BF),
            pltpu.VMEM((8, 256), jnp.int32),
            pltpu.VMEM((8, 256), jnp.int32),
            pltpu.VMEM((32, W), BF),
            pltpu.VMEM((256, W), BF),
            pltpu.VMEM((256, 2048), BF),
            pltpu.VMEM((2, W, H), BF),
            pltpu.VMEM((H, W), BF),
            pltpu.VMEM((128, 256), BF),
            pltpu.VMEM((16, 16, W // 2), BF),
            pltpu.VMEM((256, 2048), BF),
            pltpu.VMEM((512, 256), BF),
            pltpu.VMEM((4, 32, 2048), BF),
            pltpu.VMEM((8, 2, 32, 2048), BF),
            pltpu.VMEM((2, 4, 2, 4, 16, W // 2), BF),
            pltpu.VMEM((128, W), BF),
            pltpu.VMEM((4, 2, 4, 32, H), BF),
            pltpu.VMEM((4, 4, 2, 32, H), BF),
            pltpu.VMEM((4, 4, 32, H), BF),
            pltpu.VMEM((4, 2, 32, W), F32),
            pltpu.VMEM((4, 2, 32, W), BF),
            pltpu.VMEM((4, 2, 32, W), BF),
            pltpu.VMEM((4, 32, W), BF),
            pltpu.VMEM((4, 32, W), BF),
            pltpu.VMEM((4, 2, 4, 32, W), BF),
            pltpu.VMEM((4, 32, W), BF),
            pltpu.VMEM((4, 32, W), BF),
            pltpu.VMEM((4, 4, 32, 512), BF),
            pltpu.VMEM((4, 4, 32, 512), BF),
            pltpu.VMEM((2, 4, 32, W), BF),
            pltpu.VMEM((8, 32, 2048), BF),
            pltpu.VMEM((4, 8, 32, 512), BF),
            pltpu.VMEM((4, 8, 32, 512), BF),
            pltpu.VMEM((4, 2, 32, 512), BF),
            pltpu.VMEM((4, 32, 512), BF),
            pltpu.VMEM((4, 32, 512), BF),
            pltpu.VMEM((4, 32, 512), BF),
            pltpu.VMEM((4, 32, 512), BF),
            pltpu.VMEM((8, 2, 32, 128), BF),
            pltpu.VMEM((8, 32, 256), BF),
            pltpu.VMEM((4, 8, 2, 32, 128), BF),
            pltpu.VMEM((4, 8, 32, 256), BF),
            pltpu.VMEM((8, 32, W), F32),
            pltpu.VMEM((8, 32, W), BF),
            pltpu.VMEM((8, 32, W), BF),
            pltpu.SemaphoreType.DMA((N_COPIES,)),
            pltpu.SemaphoreType.DMA((N_COPIES,)),
            pltpu.SemaphoreType.DMA((10,)),
        ],
        compiler_params=pltpu.CompilerParams(
            collective_id=0, has_side_effects=True, vmem_limit_bytes=60 * 1024 * 1024
        ),
        cost_estimate=pl.CostEstimate(flops=8_000_000_000, bytes_accessed=12_000_000, transcendentals=0),
    )(expert_ids.T, gate_codes.T, projection, teacher_in, student_in, w_gate, w_up, w_down)


def solution(mesh):
    in_specs = (
        P("exp", "pair"),
        P("exp", None),
        P("exp", None),
        P("pair", "exp"),
        P("pair", "exp"),
        P("exp", "pair"),
        P("exp", None),
        P("exp", "pair"),
    )
    out_specs = (P("exp", "pair"), P("exp", "pair"))
    return jax.shard_map(body, mesh=mesh, in_specs=in_specs, out_specs=out_specs, check_vma=False)
```
